32 devices in a mesh: dp: 4 (over x, core), gx: 4 (over z), gy: 2 (over y).
Axes of the slice: x: 2, y: 2, z: 4, core: 2. Of those that a mesh axis runs over, the one named last changes fastest.
Arguments:
- features: bfloat16 [4, 4, 2, 4, 512, 128], P('dp', 'gx', 'gy'), may hold values from -6 to 6
- weight: bfloat16 [3456, 128], replicated, may hold values from -0.109375 to 0.109375
- cotangent: bfloat16 [4, 4, 2, 4, 512, 128], P('dp', 'gx', 'gy'), may hold values from -6 to 6
- neighbours: int32 [4, 4, 2, 4, 27], P('dp', 'gx', 'gy'), may hold values from -1 to 19, as said below
- send_slots: int32 [4, 4, 2, 8, 2], P('dp', 'gx', 'gy'), may hold values from -1 to 3, as said below
Outputs:
- activations: bfloat16 [4, 4, 2, 4, 512, 128], P('dp', 'gx', 'gy')
- input_grad: bfloat16 [4, 4, 2, 4, 512, 128], P('dp', 'gx', 'gy')
- weight_grad: float32 [3456, 128], replicated
The draws below stay inside these ranges and needn't reach their ends.
Inputs may be any that keep to these rules, and one draw needn't show every extreme that they name: `neighbours`: occupied slots come first in every tile and hold 1 to 4 bricks; the row of an occupied slot k has k at entry 13, other entries are a slot of the same tile, or 4 + r * 2 + q for the brick in entry q of send list 7 - r of the tile at relative position r, or -1 for an empty brick or one outside the grid; rows of empty slots are all -1. Some tile has all 4 slots occupied. Entries never point outside the grid. `send_slots`: row d lists, in a fixed order of brick positions, the slots of the tile's bricks on its face or corner column toward the tile at relative position d; -1 marks empty positions and unused entries.
All inputs are finite; a program needn't handle non-finite values.
Results may differ from the reference program's by a relative error of at most 0.0051.
Values may be sent and summed in bfloat16 or wider, within the bound.
No kernel may reach another device: no remote copies, remote signals or barrier semaphores. Data moves between devices by JAX's collectives and lax.ppermute only.
A program may use at most 64 MiB of HBM per device.

```python
import math
import jax
import jax.numpy as jnp
import numpy as np
from jax import lax

C = 128
EDGE = 8
TILE = 2
BZ = 1
SLOTS = 4
SEND = 2
VOXELS = 512
TAP_ROWS = 3456
SCENES = 4
TILES_X = 4
TILES_Y = 2


DIRECTIONS = ((-1, -1), (-1, 0), (-1, 1), (0, -1), (0, 1), (1, -1), (1, 0), (1, 1))


def face_member(direction_step, coordinate):
    if direction_step > 0:
        return coordinate == TILE - 1
    if direction_step < 0:
        return coordinate == 0
    return True


def face_tables():
    positions = TILE * TILE * BZ
    face_rows = np.full((8, SEND), -1, dtype=np.int32)
    lookup = np.full((8, positions), -1, dtype=np.int32)
    for number in range(8):
        step_x, step_y = DIRECTIONS[number]
        filled = 0
        for position in range(positions):
            brick_x = position // (TILE * BZ)
            brick_y = position // BZ % TILE
            if face_member(step_x, brick_x) and face_member(step_y, brick_y):
                face_rows[number, filled] = position
                lookup[number, position] = filled
                filled += 1
    return (face_rows, lookup)


def tap_tables():
    positions = TILE * TILE * BZ
    face_rows, lookup = face_tables()
    valid_tab = np.zeros((positions, 27), dtype=np.int32)
    region_tab = np.full((positions, 27), -1, dtype=np.int32)
    target_tab = np.zeros((positions, 27), dtype=np.int32)
    slot_tab = np.zeros((positions, 27), dtype=np.int32)
    shift_x_tab = np.zeros((positions, 27), dtype=np.int32)
    shift_y_tab = np.zeros((positions, 27), dtype=np.int32)
    for position in range(positions):
        brick_x = position // (TILE * BZ)
        brick_y = position // BZ % TILE
        brick_z = position % BZ
        for tap_number in range(27):
            off_x = tap_number // 9 - 1
            off_y = tap_number // 3 % 3 - 1
            off_z = tap_number % 3 - 1
            reach_x = brick_x + off_x
            reach_y = brick_y + off_y
            reach_z = brick_z + off_z
            if reach_z < 0 or reach_z >= BZ:
                continue
            valid_tab[position, tap_number] = 1
            region_x = -1 if reach_x < 0 else 1 if reach_x >= TILE else 0
            region_y = -1 if reach_y < 0 else 1 if reach_y >= TILE else 0
            target = (reach_x % TILE * TILE + reach_y % TILE) * BZ + reach_z
            target_tab[position, tap_number] = target
            shift_x_tab[position, tap_number] = region_x
            shift_y_tab[position, tap_number] = region_y
            if region_x != 0 or region_y != 0:
                region = DIRECTIONS.index((region_x, region_y))
                region_tab[position, tap_number] = region
                slot_tab[position, tap_number] = lookup[7 - region, target]
    return (valid_tab, region_tab, target_tab, slot_tab, shift_x_tab, shift_y_tab)


def geometry(key):
    positions = TILE * TILE * BZ
    inner = jax.random.fold_in(key, 7)
    key_first, key_second, key_full, key_order = jax.random.split(inner, 4)
    shape = (SCENES, TILES_X, TILES_Y)
    first = jax.random.randint(key_first, shape, 0, SLOTS)
    second = jax.random.randint(key_second, shape, 0, SLOTS)
    counts = SLOTS - jnp.minimum(first, second)
    full_tile = jax.random.randint(key_full, (), 0, SCENES * TILES_X * TILES_Y)
    counts = counts.reshape(-1).at[full_tile].set(SLOTS).reshape(shape)
    scores = jax.random.randint(key_order, shape + (positions,), 0, 1 << 20) * positions + jnp.arange(positions, dtype=jnp.int32)
    order = jnp.argsort(scores, axis=-1).astype(jnp.int32)
    ranks = jnp.argsort(order, axis=-1).astype(jnp.int32)
    slot_of = jnp.where(ranks < counts[..., None], ranks, -1).astype(jnp.int32)
    return (counts, order, slot_of)


def draw_neighbours(key, part):
    counts, order, slot_of = geometry(key)
    valid_tab, region_tab, target_tab, slot_tab, shift_x_tab, shift_y_tab = tap_tables()
    holder = order[..., :SLOTS]
    valid_now = jnp.asarray(valid_tab)[holder]
    region_now = jnp.asarray(region_tab)[holder]
    target_now = jnp.asarray(target_tab)[holder]
    slot_now = jnp.asarray(slot_tab)[holder]
    shift_x_now = jnp.asarray(shift_x_tab)[holder]
    shift_y_now = jnp.asarray(shift_y_tab)[holder]
    padded = jnp.pad(slot_of, ((0, 0), (1, 1), (1, 1), (0, 0)), constant_values=-1)
    scene_ids = jnp.arange(SCENES, dtype=jnp.int32)[:, None, None, None, None]
    tile_x = jnp.arange(TILES_X, dtype=jnp.int32)[None, :, None, None, None]
    tile_y = jnp.arange(TILES_Y, dtype=jnp.int32)[None, None, :, None, None]
    found = padded[scene_ids, tile_x + 1 + shift_x_now, tile_y + 1 + shift_y_now, target_now]
    remote_entry = SLOTS + SEND * region_now + slot_now
    entry = jnp.where(region_now < 0, found, jnp.where(found >= 0, remote_entry, -1))
    entry = jnp.where(valid_now > 0, entry, -1)
    live = jnp.arange(SLOTS, dtype=jnp.int32)[None, None, None, :, None] < counts[..., None, None]
    return jnp.where(live, entry, -1).astype(jnp.int32)


def draw_send_slots(key, part):
    counts, order, slot_of = geometry(key)
    face_rows, lookup = face_tables()
    face_now = jnp.asarray(face_rows)
    gotten = jnp.take(slot_of, jnp.maximum(face_now, 0), axis=-1)
    return jnp.where(face_now >= 0, gotten, -1).astype(jnp.int32)


def levels(stream_key, shape, cuts, least, high):
    def one(dim, blocks):
        heights = jax.random.uniform(jax.random.fold_in(jax.random.fold_in(stream_key, 6), dim), (blocks,), jnp.float32, least / len(cuts), high / len(cuts))
        return jnp.repeat(jnp.exp(heights), shape[dim] // blocks).reshape((-1,) + (1,) * (len(shape) - dim - 1))

    gain = one(*cuts[0])
    for cut in cuts[1:]:
        gain = gain * one(*cut)
    return gain


def normal_values(key, dims, spread, reach, shards=(), held_as=jnp.bfloat16):
    values = spread * jax.random.normal(key, dims, jnp.float32)
    if shards:
        values = values * levels(key, dims, shards, -0.22, 0.18)
    return jnp.clip(values, -reach, reach).astype(held_as)


def setup_inputs(seed: int = 0) -> dict:
    key_list = jax.random.split(jax.random.key(seed), 6)
    features = normal_values(key_list[0], (SCENES, TILES_X, TILES_Y, SLOTS, VOXELS, C), 1.0, 6.0, ((0, 4), (1, 4), (2, 2)))
    weight = normal_values(key_list[1], (TAP_ROWS, C), TAP_ROWS ** -0.5, 0.109375)
    cotangent = normal_values(key_list[2], (SCENES, TILES_X, TILES_Y, SLOTS, VOXELS, C), 1.0, 6.0, ((0, 4), (1, 4), (2, 2)))
    neighbours = draw_neighbours(jax.random.fold_in(key_list[5], 71), 0)
    send_slots = draw_send_slots(jax.random.fold_in(key_list[5], 71), 0)
    return dict(features=features, weight=weight, cotangent=cotangent, neighbours=neighbours, send_slots=send_slots)


DIRECTIONS = ((-1, -1), (-1, 0), (-1, 1), (0, -1), (0, 1), (1, -1), (1, 0), (1, 1))

def silu_slope(preact):
    sigmoid_of = jax.nn.sigmoid(preact)
    return sigmoid_of * (1.0 + preact * (1.0 - sigmoid_of))

def brick_columns(store, brick_row):
    channels = store.shape[-1]
    chosen = jnp.where(brick_row < 0, store.shape[0] - 1, brick_row).astype(jnp.int32)
    picked = jnp.take(store, chosen, axis=0)
    big_cube = picked.reshape(3, 3, 3, EDGE, EDGE, EDGE, channels)
    big_cube = big_cube.transpose(0, 3, 1, 4, 2, 5, 6).reshape(3 * EDGE, 3 * EDGE, 3 * EDGE, channels)
    padded = big_cube[EDGE - 1:2 * EDGE + 1, EDGE - 1:2 * EDGE + 1, EDGE - 1:2 * EDGE + 1]
    pieces = []
    for offset_x in range(3):
        for offset_y in range(3):
            for offset_z in range(3):
                window = padded[offset_x:offset_x + EDGE, offset_y:offset_y + EDGE, offset_z:offset_z + EDGE]
                pieces.append(window.reshape(EDGE * EDGE * EDGE, channels))
    return jnp.concatenate(pieces, axis=1)

def tile_store(bricks, send_slots, scene_at, tile_x, tile_y):
    count_x = bricks.shape[1]
    count_y = bricks.shape[2]
    voxel_count = bricks.shape[4]
    channels = bricks.shape[5]
    own_bricks = bricks[scene_at, tile_x, tile_y]
    arrived = []
    for number in range(8):
        step_x, step_y = DIRECTIONS[number]
        source_x = tile_x + step_x
        source_y = tile_y + step_y
        inside = (source_x >= 0) & (source_x < count_x) & (source_y >= 0) & (source_y < count_y)
        clamp_x = jnp.clip(source_x, 0, count_x - 1).astype(jnp.int32)
        clamp_y = jnp.clip(source_y, 0, count_y - 1).astype(jnp.int32)
        listing = send_slots[scene_at, clamp_x, clamp_y, 7 - number]
        owned_bricks = bricks[scene_at, clamp_x, clamp_y]
        taken_bricks = jnp.take(owned_bricks, jnp.maximum(listing, 0).astype(jnp.int32), axis=0)
        kept_mask = inside & (listing >= 0)
        arrived.append(jnp.where(kept_mask[:, None, None], taken_bricks, jnp.zeros_like(taken_bricks)))
    zero_brick = jnp.zeros((1, voxel_count, channels), bricks.dtype)
    return jnp.concatenate([own_bricks] + arrived + [zero_brick], axis=0)

def reference(features, weight, cotangent, neighbours, send_slots):
    scenes = features.shape[0]
    count_x = features.shape[1]
    count_y = features.shape[2]
    slot_count = features.shape[3]
    voxel_count = features.shape[4]
    channels = features.shape[5]
    total_tiles = scenes * count_x * count_y
    flipped = weight.reshape(27, channels, channels)[::-1].transpose(0, 2, 1).reshape(27 * channels, channels)

    def locate(flat_index):
        return (flat_index // (count_x * count_y), flat_index // count_y % count_x, flat_index % count_y)

    def forward_tile(state_now, flat_index):
        scene_at, tile_x, tile_y = locate(flat_index)
        store = tile_store(features, send_slots, scene_at, tile_x, tile_y)
        brick_rows = neighbours[scene_at, tile_x, tile_y]

        def slot_forward(brick_row, grad_out):
            columns = brick_columns(store, brick_row)
            preact = jnp.dot(columns, weight, preferred_element_type=jnp.float32)
            activated = jax.nn.silu(preact).astype(jnp.bfloat16)
            occupied = brick_row[13] >= 0
            grad_pre = jnp.where(occupied, grad_out.astype(jnp.float32) * silu_slope(preact), 0.0).astype(jnp.bfloat16)
            term = lax.dot_general(columns, grad_pre, (((0,), (0,)), ((), ())), preferred_element_type=jnp.float32)
            return (activated, grad_pre, term)
        activated, grad_pre, terms = jax.vmap(slot_forward)(brick_rows, cotangent[scene_at, tile_x, tile_y])
        return (state_now + lax.optimization_barrier(jnp.sum(terms, axis=0)), (activated, grad_pre))
    initial = jnp.zeros((27 * channels, channels), jnp.float32)
    tile_ids = jnp.arange(total_tiles, dtype=jnp.int32)
    summed, stacked = lax.scan(forward_tile, initial, tile_ids)
    activations = stacked[0].reshape(features.shape)
    grads_all = stacked[1].reshape(features.shape)

    def backward_tile(flat_index):
        scene_at, tile_x, tile_y = locate(flat_index)
        store = tile_store(grads_all, send_slots, scene_at, tile_x, tile_y)
        brick_rows = neighbours[scene_at, tile_x, tile_y]

        def slot_backward(brick_row):
            return jnp.dot(brick_columns(store, brick_row), flipped, preferred_element_type=jnp.float32).astype(jnp.bfloat16)
        return jax.vmap(slot_backward)(brick_rows)
    input_grad = lax.map(backward_tile, tile_ids).reshape(features.shape)
    factor = 1.0 / math.sqrt(float(total_tiles * slot_count * voxel_count))
    weight_grad = summed * factor
    return (activations, input_grad, weight_grad)
```

```python
import functools
import math

import jax
import jax.numpy as jnp
from jax import lax
from jax.experimental import pallas as pl
from jax.experimental.pallas import tpu as pltpu
from jax.sharding import PartitionSpec as P

EDGE = 8
PLANE = EDGE * EDGE
DIRECTIONS = ((-1, -1), (-1, 0), (-1, 1), (0, -1), (0, 1), (1, -1), (1, 0), (1, 1))
VMEM_BYTES = 28 * 2**20
CORES = 2

F32 = jnp.float32
BF16 = jnp.bfloat16


def swap_phases(size):
    return [None] + ([0] if size > 1 else []) + ([1] if size > 2 else [])


def swap_partner(at, size, phase):
    if phase is None:
        return at
    other = at + 1 if at % 2 == phase else at - 1
    return other if 0 <= other < size else None


def routes_of(count_x, count_y):
    both = [(px, py) for px in swap_phases(count_x) for py in swap_phases(count_y)]
    return [route for route in both if route != (None, None)]


def route_pairs(route, count_x, count_y):
    pairs = []
    for x in range(count_x):
        for y in range(count_y):
            to_x = swap_partner(x, count_x, route[0])
            to_y = swap_partner(y, count_y, route[1])
            if to_x is not None and to_y is not None:
                pairs.append((x * count_y + y, to_x * count_y + to_y))
    return pairs


def step_of(at, phase):
    return 0 if phase is None else jnp.where(at % 2 == phase, 1, -1)


def direction_of(route, at_x, at_y):
    step_x, step_y = step_of(at_x, route[0]), step_of(at_y, route[1])
    flat = 3 * (step_x + 1) + step_y + 1
    return flat - jnp.where(flat > 4, 1, 0), step_x, step_y


def box_shape(route, send):
    if route[0] is None or route[1] is None:
        return (send, PLANE, 128)
    return (send * EDGE, 128)


def low_or_high(group, upper):
    wide = group.astype(F32)
    return wide[..., EDGE:, :] if upper else wide[..., :EDGE, :]


def pack_boxes(bricks, lists, boxes, routes, at_x, at_y, send):
    for route, box in zip(routes, boxes):
        number, step_x, step_y = direction_of(route, at_x, at_y)
        pieces = []
        for entry in range(send):
            listed = lists[number, entry]
            slot = jnp.maximum(listed, 0)
            kept = listed >= 0
            if route[1] is None:
                face = bricks[slot, jnp.where(step_x > 0, EDGE - 1, 0)]
                box[entry] = jnp.where(kept, face, jnp.zeros_like(face))
            elif route[0] is None:
                low = low_or_high(bricks[slot, :, 0:16, :], False)
                high = low_or_high(bricks[slot, :, PLANE - 16 : PLANE, :], True)
                face = jnp.where(kept, jnp.where(step_y > 0, high, low), 0.0)
                box[entry] = face.reshape(PLANE, 128).astype(BF16)
            else:
                plane = jnp.where(step_x > 0, EDGE - 1, 0)
                low = low_or_high(bricks[slot, plane, 0:16, :], False)
                high = low_or_high(bricks[slot, plane, PLANE - 16 : PLANE, :], True)
                pieces.append(jnp.where(kept, jnp.where(step_y > 0, high, low), 0.0))
        if pieces:
            box[...] = jnp.concatenate(pieces, axis=0).astype(BF16)


def fill_store(store, bricks, boxes, routes, at_x, at_y, send):
    slots = bricks.shape[0]
    store[0:slots] = bricks[...]
    store[store.shape[0] - 1] = jnp.zeros(store.shape[1:], BF16)
    for route, box in zip(routes, boxes):
        number, _, _ = direction_of(route, at_x, at_y)
        if not (route[0] is None or route[1] is None):
            edges = box[...].astype(F32)
        for entry in range(send):
            at = slots + number * send + entry
            if route[1] is None:
                store[at, 0] = box[entry]
                store[at, EDGE - 1] = box[entry]
            elif route[0] is None:
                rows = box[entry].astype(F32).reshape(EDGE, EDGE, 128)
                twice = jnp.concatenate([rows, rows], axis=1).astype(BF16)
                store[at, :, 0:16, :] = twice
                store[at, :, PLANE - 16 : PLANE, :] = twice
            else:
                rows = edges[entry * EDGE : (entry + 1) * EDGE]
                twice = jnp.concatenate([rows, rows], axis=0).astype(BF16)
                for plane in (0, EDGE - 1):
                    store[at, plane, 0:16, :] = twice
                    store[at, plane, PLANE - 16 : PLANE, :] = twice


def fill_views(views, store, table, slot):
    zero_at = store.shape[0] - 1

    def entry(off_x, off_y):
        listed = table[slot, 9 * (off_x + 1) + 3 * (off_y + 1) + 1]
        return jnp.where(listed < 0, zero_at, listed)

    for off_x, source, target in ((-1, EDGE - 1, 0), (0, slice(0, EDGE), slice(1, EDGE + 1)), (1, 0, EDGE + 1)):
        middle = store[entry(off_x, 0), source]
        before = low_or_high(store[entry(off_x, -1), source, PLANE - 16 : PLANE, :], True)
        after = low_or_high(store[entry(off_x, 1), source, 0:16, :], False)
        wide = middle.astype(F32)
        axis = wide.ndim - 2
        views[target, :, 128:256] = middle
        views[target, :, 0:128] = jnp.concatenate(
            [before, wide[..., : PLANE - EDGE, :]], axis=axis
        ).astype(BF16)
        views[target, :, 256:384] = jnp.concatenate(
            [wide[..., EDGE:, :], after], axis=axis
        ).astype(BF16)


def lhs_of(views):
    return jnp.concatenate(
        [views[dx : dx + EDGE].reshape(EDGE * PLANE, 384) for dx in range(3)], axis=1
    )


def shift_rows(wide, step):
    row = lax.broadcasted_iota(jnp.int32, wide.shape, 1)
    moved = pltpu.roll(wide, (-step) % EDGE, 1)
    return jnp.where(row == (EDGE - 1 if step > 0 else 0), 0.0, moved)


def join_taps(parts):
    blocks = [parts[:, 128 * dz : 128 * dz + 128].reshape(PLANE, EDGE, 128) for dz in range(3)]
    return blocks[1] + shift_rows(blocks[0], -1) + shift_rows(blocks[2], 1)


def pack_kernel(routes, send, lists, bricks, *boxes):
    at_x, at_y = lax.axis_index("gx"), lax.axis_index("gy")
    pack_boxes(bricks, lists, boxes, routes, at_x, at_y, send)


def forward_kernel(routes, send, factor, table, lists, bricks, cotangent, weight, *rest):
    count = len(routes)
    boxes_in, rest = rest[:count], rest[count:]
    activated, grads, kept_term, sent_term = rest[:4]
    boxes_out, rest = rest[4 : 4 + count], rest[4 + count :]
    store, views, taps = rest
    at_x, at_y = lax.axis_index("gx"), lax.axis_index("gy")
    core = lax.axis_index("dp") % CORES
    slots = bricks.shape[0]
    for tap in range(27):
        taps[tap // 3 * 128 : tap // 3 * 128 + 128, tap % 3 * 128 : tap % 3 * 128 + 128] = weight[tap]
    fill_store(store, bricks, boxes_in, routes, at_x, at_y, send)
    for slot in range(slots):
        fill_views(views.at[slot], store, table, slot)
        parts = jnp.dot(lhs_of(views.at[slot]), taps[...], preferred_element_type=F32)
        preact = join_taps(parts)
        sigmoid = jax.nn.sigmoid(preact)
        activated[slot] = (preact * sigmoid).reshape(EDGE, PLANE, 128).astype(BF16)
        slope = sigmoid * (1.0 + preact * (1.0 - sigmoid))
        wide = cotangent[slot].astype(F32).reshape(PLANE, EDGE, 128) * slope
        wide = jnp.where(table[slot, 13] >= 0, wide, 0.0)
        grads[slot] = wide.reshape(EDGE, PLANE, 128).astype(BF16)
    pack_boxes(grads, lists, boxes_out, routes, at_x, at_y, send)
    total = None
    for slot in range(slots):
        grad = grads[slot].astype(F32).reshape(PLANE, EDGE, 128)
        shifted = [shift_rows(grad, 1), grad, shift_rows(grad, -1)]
        rhs = jnp.concatenate([s.reshape(EDGE * PLANE, 128) for s in shifted], axis=1).astype(BF16)
        term = lax.dot_general(
            lhs_of(views.at[slot]), rhs, (((0,), (0,)), ((), ())), preferred_element_type=F32
        )
        total = term if total is None else total + term
    half = 128 // CORES
    for tap in range(27):
        block = total[tap // 3 * 128 : tap // 3 * 128 + 128, tap % 3 * 128 : tap % 3 * 128 + 128]
        block = block * factor
        first, second = block[:half], block[half:]
        kept_term[tap] = jnp.where(core == 0, first, second)
        sent_term[tap] = jnp.where(core == 0, second, first).astype(BF16)


def backward_kernel(routes, send, table, bricks, weight, *rest):
    count = len(routes)
    boxes_in, (result, store, views, taps) = rest[:count], rest[count:]
    at_x, at_y = lax.axis_index("gx"), lax.axis_index("gy")
    for tap in range(27):
        taps[tap % 3 * 128 : tap % 3 * 128 + 128, tap // 3 * 128 : tap // 3 * 128 + 128] = weight[26 - tap]
    fill_store(store, bricks, boxes_in, routes, at_x, at_y, send)
    for slot in range(bricks.shape[0]):
        fill_views(views.at[slot], store, table, slot)
        parts = lax.dot_general(
            lhs_of(views.at[slot]), taps[...], (((1,), (1,)), ((), ())), preferred_element_type=F32
        )
        result[slot] = join_taps(parts).reshape(EDGE, PLANE, 128).astype(BF16)


VMEM = pl.BlockSpec(memory_space=pltpu.VMEM)
SMEM = pl.BlockSpec(memory_space=pltpu.SMEM)
PARAMS = pltpu.CompilerParams(vmem_limit_bytes=VMEM_BYTES)


def xor_swap(x, axes, sizes, masks):
    pairs = []
    total = math.prod(sizes)
    for flat in range(total):
        left, where = flat, []
        for size in reversed(sizes):
            where.append(left % size)
            left //= size
        where.reverse()
        to = 0
        for size, at, mask in zip(sizes, where, masks):
            to = to * size + (at ^ mask)
        pairs.append((flat, to))
    return lax.ppermute(x, axes, pairs)


def tree_sum(terms):
    while len(terms) > 1:
        terms = [a + b for a, b in zip(terms[::2], terms[1::2])]
    return terms[0]


def own_piece(pieces, at):
    return lax.dynamic_index_in_dim(pieces, at, 1, keepdims=False)


def summed_everywhere(kept, sent):
    dp, gx, gy = (lax.axis_size(name) for name in ("dp", "gx", "gy"))
    me = lax.axis_index("dp")
    core = me % CORES
    half = kept + xor_swap(sent, ("dp",), (dp,), (1,)).astype(F32)
    chips = dp // CORES
    group = chips * gy
    mine = (me // CORES) * gy + lax.axis_index("gy")
    shares = half.reshape(half.shape[0], group, half.shape[1] // group, 128)
    masks = [(m // gy * CORES, m % gy) for m in range(group)]
    total = own_piece(shares, mine)
    for m in range(1, group):
        piece = own_piece(shares, mine ^ m).astype(BF16)
        total = total + xor_swap(piece, ("dp", "gy"), (dp, gy), masks[m]).astype(F32)
    rounded = total.astype(BF16)
    terms = [rounded] + [xor_swap(rounded, ("gx",), (gx,), (m,)) for m in range(1, gx)]
    rounded = tree_sum([term.astype(F32) for term in terms]).astype(BF16)
    parts = [rounded] + [xor_swap(rounded, ("dp", "gy"), (dp, gy), masks[m]) for m in range(1, group)]
    stacked = jnp.stack(parts, axis=1)
    order = jnp.arange(group) ^ mine
    half = jnp.take(stacked, order, axis=1).reshape(half.shape)
    other = xor_swap(half, ("dp",), (dp,), (1,))
    first = jnp.where(core == 0, half, other)
    second = jnp.where(core == 0, other, half)
    return jnp.concatenate([first, second], axis=1).astype(F32)


def body(features, weight, cotangent, neighbours, send_slots):
    slots, _, channels = features.shape[3:]
    send = send_slots.shape[-1]
    gx, gy = lax.axis_size("gx"), lax.axis_size("gy")
    devices = lax.axis_size("dp") * gx * gy
    routes = routes_of(gx, gy)
    bricks = features.reshape(slots, EDGE, PLANE, channels)
    cot = cotangent.reshape(slots, EDGE, PLANE, channels)
    table = neighbours.reshape(slots, 27)
    lists = send_slots.reshape(8, send)
    taps = weight.reshape(27, channels, channels)
    factor = 1.0 / math.sqrt(float(devices * slots * EDGE * PLANE))
    box_types = [jax.ShapeDtypeStruct(box_shape(route, send), BF16) for route in routes]
    bricks_type = jax.ShapeDtypeStruct(bricks.shape, BF16)
    entries = slots + 8 * send + 1
    scratch = [
        pltpu.VMEM((entries, EDGE, PLANE, 128), BF16),
        pltpu.VMEM((slots, EDGE + 2, PLANE, 384), BF16),
    ]

    def moved(boxes):
        return [
            lax.ppermute(box, ("gx", "gy"), route_pairs(route, gx, gy))
            for route, box in zip(routes, boxes)
        ]

    boxes = pl.pallas_call(
        functools.partial(pack_kernel, routes, send),
        out_shape=box_types,
        in_specs=[SMEM, VMEM],
        out_specs=[VMEM] * len(routes),
        compiler_params=PARAMS,
        name="pack",
    )(lists, bricks)
    arrived = moved(boxes)
    half_shape = (27, channels // CORES, channels)
    activated, grads, kept, sent, *boxes = pl.pallas_call(
        functools.partial(forward_kernel, routes, send, factor),
        out_shape=[
            bricks_type,
            bricks_type,
            jax.ShapeDtypeStruct(half_shape, F32),
            jax.ShapeDtypeStruct(half_shape, BF16),
            *box_types,
        ],
        in_specs=[SMEM, SMEM, VMEM, VMEM, VMEM] + [VMEM] * len(routes),
        out_specs=[VMEM] * (4 + len(routes)),
        scratch_shapes=scratch + [pltpu.VMEM((1152, 384), BF16)],
        compiler_params=PARAMS,
        name="forward",
    )(table, lists, bricks, cot, taps, *arrived)
    arrived = moved(boxes)
    weight_grad = summed_everywhere(kept, sent)
    input_grad = pl.pallas_call(
        functools.partial(backward_kernel, routes, send),
        out_shape=bricks_type,
        in_specs=[SMEM, VMEM, VMEM] + [VMEM] * len(routes),
        out_specs=VMEM,
        scratch_shapes=scratch + [pltpu.VMEM((384, 1152), BF16)],
        compiler_params=PARAMS,
        name="backward",
    )(table, grads, taps, *arrived)
    return (
        activated.reshape(features.shape),
        input_grad.reshape(features.shape),
        weight_grad.reshape(weight.shape),
    )


def solution(mesh):
    split = P("dp", "gx", "gy", None, None, None)
    table = P("dp", "gx", "gy", None, None)
    return jax.shard_map(
        body,
        mesh=mesh,
        in_specs=(split, P(), split, table, table),
        out_specs=(split, split, P()),
        check_vma=False,
    )
```

```python
import functools
import math

import jax
import jax.numpy as jnp
from jax import lax
from jax.experimental import pallas as pl
from jax.experimental.pallas import tpu as pltpu
from jax.sharding import PartitionSpec as P

EDGE = 8
PLANE = EDGE * EDGE
VMEM_BYTES = 28 * 2**20
CORES = 2

F32 = jnp.float32
BF16 = jnp.bfloat16


def swap_phases(size):
    return ([0] if size > 1 else []) + ([1] if size > 2 else [])


def swap_pairs(size, phase):
    pairs = []
    for low in range(phase, size - 1, 2):
        pairs += [(low, low + 1), (low + 1, low)]
    return pairs


def step_of(at, phase):
    return jnp.where(at % 2 == phase, 1, -1)


def direction(step_x, step_y):
    flat = 3 * (step_x + 1) + step_y + 1
    return flat - jnp.where(flat > 4, 1, 0)


def low_or_high(group, upper):
    wide = group.astype(F32)
    return wide[..., EDGE:, :] if upper else wide[..., :EDGE, :]


def y_edge(bricks, slot, plane, step_y):
    low = low_or_high(bricks[slot, plane, 0:16, :], False)
    high = low_or_high(bricks[slot, plane, PLANE - 16 : PLANE, :], True)
    return jnp.where(step_y > 0, high, low)


def pack_along_y(bricks, lists, box, step_y, send):
    number = direction(0, step_y)
    for entry in range(send):
        listed = lists[number, entry]
        face = y_edge(bricks, jnp.maximum(listed, 0), slice(0, EDGE), step_y)
        face = jnp.where(listed >= 0, face, 0.0).reshape(PLANE, 128)
        box[entry * PLANE : (entry + 1) * PLANE] = face.astype(BF16)
    at = send * PLANE
    for step_x in (-1, 1):
        number = direction(step_x, step_y)
        pieces = []
        for entry in range(send):
            listed = lists[number, entry]
            plane = EDGE - 1 if step_x > 0 else 0
            edge = y_edge(bricks, jnp.maximum(listed, 0), plane, step_y)
            pieces.append(jnp.where(listed >= 0, edge, 0.0))
        box[at : at + send * EDGE] = jnp.concatenate(pieces, axis=0).astype(BF16)
        at += send * EDGE


def pack_along_x(bricks, lists, box, y_boxes, step_x, send):
    number = direction(step_x, 0)
    for entry in range(send):
        listed = lists[number, entry]
        face = bricks[jnp.maximum(listed, 0), jnp.where(step_x > 0, EDGE - 1, 0)]
        box[entry * PLANE : (entry + 1) * PLANE] = jnp.where(listed >= 0, face, jnp.zeros_like(face))
    at = send * PLANE
    for y_box in y_boxes:
        first = y_box[send * PLANE : send * PLANE + send * EDGE]
        second = y_box[send * PLANE + send * EDGE : send * PLANE + 2 * send * EDGE]
        box[at : at + send * EDGE] = jnp.where(step_x > 0, second, first)
        at += send * EDGE


def fill_remote(store, base, x_boxes, y_boxes, steps_x, steps_y, send):
    store[store.shape[0] - 1] = jnp.zeros(store.shape[1:], BF16)
    for step_y, box in zip(steps_y, y_boxes):
        number = direction(0, step_y)
        for entry in range(send):
            rows = box[entry * PLANE : (entry + 1) * PLANE].astype(F32).reshape(EDGE, EDGE, 128)
            twice = jnp.concatenate([rows, rows], axis=1).astype(BF16)
            store[base + number * send + entry, :, 0:16, :] = twice
            store[base + number * send + entry, :, PLANE - 16 : PLANE, :] = twice
    for step_x, box in zip(steps_x, x_boxes):
        number = direction(step_x, 0)
        for entry in range(send):
            face = box[entry * PLANE : (entry + 1) * PLANE]
            store[base + number * send + entry, 0] = face
            store[base + number * send + entry, EDGE - 1] = face
        at = send * PLANE
        for step_y in steps_y:
            number = direction(step_x, step_y)
            edges = box[at : at + send * EDGE].astype(F32)
            at += send * EDGE
            for entry in range(send):
                rows = edges[entry * EDGE : (entry + 1) * EDGE]
                twice = jnp.concatenate([rows, rows], axis=0).astype(BF16)
                for plane in (0, EDGE - 1):
                    store[base + number * send + entry, plane, 0:16, :] = twice
                    store[base + number * send + entry, plane, PLANE - 16 : PLANE, :] = twice


def view_of(store, entry, off_x, source):
    middle = store[entry(off_x, 0), source]
    before = low_or_high(store[entry(off_x, -1), source, PLANE - 16 : PLANE, :], True)
    after = low_or_high(store[entry(off_x, 1), source, 0:16, :], False)
    wide = middle.astype(F32)
    axis = wide.ndim - 2
    left = jnp.concatenate([before, wide[..., : PLANE - EDGE, :]], axis=axis).astype(BF16)
    right = jnp.concatenate([wide[..., EDGE:, :], after], axis=axis).astype(BF16)
    return jnp.concatenate([left, middle, right], axis=axis + 1)


def fill_views(views, store, entry):
    views[0] = view_of(store, entry, -1, EDGE - 1)
    views[1 : EDGE + 1] = view_of(store, entry, 0, slice(0, EDGE))
    views[EDGE + 1] = view_of(store, entry, 1, 0)


def lookup(table, slot, first, last, zero_at):
    def entry(off_x, off_y):
        listed = table[slot, 9 * (off_x + 1) + 3 * (off_y + 1) + 1]
        return jnp.where((listed >= first) & (listed < last), listed - first, zero_at)

    return entry


def lhs_of(views):
    return jnp.concatenate(
        [views[dx : dx + EDGE].reshape(EDGE * PLANE, 384) for dx in range(3)], axis=1
    )


def shift_rows(wide, step):
    row = lax.broadcasted_iota(jnp.int32, wide.shape, 1)
    moved = pltpu.roll(wide, (-step) % EDGE, 1)
    return jnp.where(row == (EDGE - 1 if step > 0 else 0), 0.0, moved)


def join_taps(parts):
    shape = (parts.shape[0] // EDGE, EDGE, 128)
    blocks = [parts[:, 128 * dz : 128 * dz + 128].reshape(shape) for dz in range(3)]
    return blocks[1] + shift_rows(blocks[0], -1) + shift_rows(blocks[2], 1)


def steps_here(counts):
    steps_x = [step_of(lax.axis_index("gx"), phase) for phase in swap_phases(counts[0])]
    steps_y = [step_of(lax.axis_index("gy"), phase) for phase in swap_phases(counts[1])]
    return steps_x, steps_y


def pack_y_kernel(counts, send, lists, bricks, *boxes):
    for step_y, box in zip(steps_here(counts)[1], boxes):
        pack_along_y(bricks, lists, box, step_y, send)


def pack_x_kernel(counts, send, lists, bricks, *rest):
    steps_x, steps_y = steps_here(counts)
    y_boxes, x_boxes = rest[: len(steps_y)], rest[len(steps_y) :]
    for step_x, box in zip(steps_x, x_boxes):
        pack_along_x(bricks, lists, box, y_boxes, step_x, send)


def taps_kernel(weight, forward, backward):
    for tap in range(27):
        far, near = tap // 3 * 128, tap % 3 * 128
        forward[far : far + 128, near : near + 128] = weight[tap]
        backward[near : near + 128, far : far + 128] = weight[26 - tap]


def own_kernel(table, bricks, taps, views, preact, store):
    slots = bricks.shape[0]
    store[0:slots] = bricks[...]
    store[slots] = jnp.zeros(store.shape[1:], BF16)
    for slot in range(slots):
        fill_views(views.at[slot], store, lookup(table, slot, 0, slots, slots))
        parts = jnp.dot(lhs_of(views.at[slot]), taps[...], preferred_element_type=F32)
        preact[slot] = join_taps(parts).reshape(EDGE, EDGE, EDGE, 128)


def forward_kernel(counts, send, factor, table, lists, own_views, own_preact, cotangent, taps, *rest):
    steps_x, steps_y = steps_here(counts)
    number_x, number_y = len(steps_x), len(steps_y)
    x_boxes, y_boxes, rest = rest[:number_x], rest[number_x : number_x + number_y], rest[number_x + number_y :]
    views, preacts, activated, grads, kept_term, sent_term = rest[:6]
    boxes_out, (store, sides) = rest[6 : 6 + number_y], rest[6 + number_y :]
    core = lax.axis_index("dp") % CORES
    slots = cotangent.shape[0]
    fill_remote(store, 0, x_boxes, y_boxes, steps_x, steps_y, send)
    nothing = jnp.zeros((EDGE, EDGE, 128), F32)
    for slot in range(slots):
        rows = slice(slot * PLANE, (slot + 1) * PLANE)
        entry = lookup(table, slot, slots, slots + 8 * send, store.shape[0] - 1)
        for side, off_x, source, target in ((0, -1, EDGE - 1, 0), (1, 1, 0, EDGE + 1)):
            plane = view_of(store, entry, off_x, source)
            sides[side, rows] = plane
            views[slot, target] = views[slot, target] + plane
        for side, off_y, base, lanes in ((2, -1, 0, 0), (3, 1, PLANE - 16, 256)):
            group = slice(PLANE - 16, PLANE) if off_y < 0 else slice(0, 16)
            edge = low_or_high(store[entry(0, off_y), :, group, :], off_y < 0)
            padded = jnp.concatenate([nothing[:1], edge, nothing[:1]], axis=0)
            for dx in range(3):
                sides[side, rows, 128 * dx : 128 * dx + 128] = (
                    padded[dx : dx + EDGE].reshape(PLANE, 128).astype(BF16)
                )
            both = [edge, nothing] if off_y < 0 else [nothing, edge]
            wide = jnp.concatenate(both, axis=1).astype(BF16)
            at = (slot, slice(1, EDGE + 1), slice(base, base + 16), slice(lanes, lanes + 128))
            views[at] = views[at] + wide
    added = []
    for side in range(4):
        if side < 2:
            part = taps[768 * side : 768 * side + 384]
        else:
            dy = 0 if side == 2 else 2
            part = jnp.concatenate(
                [taps[(3 * dx + dy) * 128 : (3 * dx + dy) * 128 + 128] for dx in range(3)], axis=0
            )
        product = join_taps(jnp.dot(sides[side], part, preferred_element_type=F32))
        added.append(product.reshape(slots, EDGE, EDGE, 128))
    for slot in range(slots):
        preacts[slot, 0] = preacts[slot, 0] + added[0][slot]
        preacts[slot, EDGE - 1] = preacts[slot, EDGE - 1] + added[1][slot]
        preacts[slot, :, 0] = preacts[slot, :, 0] + added[2][slot]
        preacts[slot, :, EDGE - 1] = preacts[slot, :, EDGE - 1] + added[3][slot]
        preact = preacts[slot].reshape(PLANE, EDGE, 128)
        sigmoid = jax.nn.sigmoid(preact)
        activated[slot] = (preact * sigmoid).reshape(EDGE, PLANE, 128).astype(BF16)
        slope = sigmoid * (1.0 + preact * (1.0 - sigmoid))
        wide = cotangent[slot].astype(F32).reshape(PLANE, EDGE, 128) * slope
        wide = jnp.where(table[slot, 13] >= 0, wide, 0.0)
        grads[slot] = wide.reshape(EDGE, PLANE, 128).astype(BF16)
    for step_y, box in zip(steps_y, boxes_out):
        pack_along_y(grads, lists, box, step_y, send)
    total = None
    for slot in range(slots):
        grad = grads[slot].astype(F32).reshape(PLANE, EDGE, 128)
        shifted = [shift_rows(grad, 1), grad, shift_rows(grad, -1)]
        rhs = jnp.concatenate([s.reshape(EDGE * PLANE, 128) for s in shifted], axis=1).astype(BF16)
        term = lax.dot_general(
            lhs_of(views.at[slot]), rhs, (((0,), (0,)), ((), ())), preferred_element_type=F32
        )
        total = term if total is None else total + term
    half = 128 // CORES
    for tap in range(27):
        far, near = tap // 3 * 128, tap % 3 * 128
        block = total[far : far + 128, near : near + 128] * factor
        first, second = block[:half], block[half:]
        kept_term[tap] = jnp.where(core == 0, first, second)
        sent_term[tap] = jnp.where(core == 0, second, first).astype(BF16)


def backward_kernel(counts, send, table, bricks, taps, *rest):
    steps_x, steps_y = steps_here(counts)
    x_boxes, y_boxes = rest[: len(steps_x)], rest[len(steps_x) : len(steps_x) + len(steps_y)]
    result, store, views = rest[-3:]
    slots = bricks.shape[0]
    store[0:slots] = bricks[...]
    fill_remote(store, slots, x_boxes, y_boxes, steps_x, steps_y, send)
    zero_at = store.shape[0] - 1
    for slot in range(slots):
        fill_views(views.at[slot], store, lookup(table, slot, 0, zero_at, zero_at))
        parts = lax.dot_general(
            lhs_of(views.at[slot]), taps[...], (((1,), (1,)), ((), ())), preferred_element_type=F32
        )
        result[slot] = join_taps(parts).reshape(EDGE, PLANE, 128).astype(BF16)


VMEM = pl.BlockSpec(memory_space=pltpu.VMEM)
SMEM = pl.BlockSpec(memory_space=pltpu.SMEM)
PARAMS = pltpu.CompilerParams(vmem_limit_bytes=VMEM_BYTES)


def xor_swap(x, axes, sizes, masks):
    pairs = []
    total = math.prod(sizes)
    for flat in range(total):
        left, where = flat, []
        for size in reversed(sizes):
            where.append(left % size)
            left //= size
        where.reverse()
        to = 0
        for size, at, mask in zip(sizes, where, masks):
            to = to * size + (at ^ mask)
        pairs.append((flat, to))
    return lax.ppermute(x, axes, pairs)


def tree_sum(terms):
    while len(terms) > 1:
        terms = [a + b for a, b in zip(terms[::2], terms[1::2])]
    return terms[0]


def own_piece(pieces, at):
    return lax.dynamic_index_in_dim(pieces, at, 1, keepdims=False)


def summed_everywhere(kept, sent):
    dp, gx, gy = (lax.axis_size(name) for name in ("dp", "gx", "gy"))
    me = lax.axis_index("dp")
    core = me % CORES
    half = kept + xor_swap(sent, ("dp",), (dp,), (1,)).astype(F32)
    chips = dp // CORES
    group = chips * gy
    mine = (me // CORES) * gy + lax.axis_index("gy")
    shares = half.reshape(half.shape[0], group, half.shape[1] // group, 128)
    masks = [(m // gy * CORES, m % gy) for m in range(group)]
    total = own_piece(shares, mine)
    for m in range(1, group):
        piece = own_piece(shares, mine ^ m).astype(BF16)
        total = total + xor_swap(piece, ("dp", "gy"), (dp, gy), masks[m]).astype(F32)
    rounded = total.astype(BF16)
    terms = [rounded] + [xor_swap(rounded, ("gx",), (gx,), (m,)) for m in range(1, gx)]
    rounded = tree_sum([term.astype(F32) for term in terms]).astype(BF16)
    parts = [rounded] + [xor_swap(rounded, ("dp", "gy"), (dp, gy), masks[m]) for m in range(1, group)]
    stacked = jnp.stack(parts, axis=1)
    order = jnp.arange(group) ^ mine
    half = jnp.take(stacked, order, axis=1).reshape(half.shape)
    other = xor_swap(half, ("dp",), (dp,), (1,))
    first = jnp.where(core == 0, half, other)
    second = jnp.where(core == 0, other, half)
    return jnp.concatenate([first, second], axis=1).astype(F32)


def run(kernel, out_shape, ins, outs, scratch=(), aliases=None, micros=1.0):
    cost = pl.CostEstimate(flops=int(micros * 1e9), bytes_accessed=2**16, transcendentals=0)
    return pl.pallas_call(
        kernel,
        out_shape=out_shape,
        in_specs=ins,
        out_specs=outs,
        scratch_shapes=list(scratch),
        input_output_aliases=aliases or {},
        compiler_params=PARAMS,
        cost_estimate=cost,
    )


def body(features, weight, cotangent, neighbours, send_slots):
    slots, _, channels = features.shape[3:]
    send = send_slots.shape[-1]
    counts = (lax.axis_size("gx"), lax.axis_size("gy"))
    devices = lax.axis_size("dp") * counts[0] * counts[1]
    bricks = features.reshape(slots, EDGE, PLANE, channels)
    cot = cotangent.reshape(slots, EDGE, PLANE, channels)
    table = neighbours.reshape(slots, 27)
    lists = send_slots.reshape(8, send)
    factor = 1.0 / math.sqrt(float(devices * slots * EDGE * PLANE))
    phases_x, phases_y = swap_phases(counts[0]), swap_phases(counts[1])
    number_x, number_y = len(phases_x), len(phases_y)
    y_type = jax.ShapeDtypeStruct((send * (PLANE + 2 * EDGE), 128), BF16)
    x_type = jax.ShapeDtypeStruct((send * (PLANE + number_y * EDGE), 128), BF16)
    bricks_type = jax.ShapeDtypeStruct(bricks.shape, BF16)
    views_type = jax.ShapeDtypeStruct((slots, EDGE + 2, PLANE, 384), BF16)
    preact_type = jax.ShapeDtypeStruct((slots, EDGE, EDGE, EDGE, 128), F32)
    half_shape = (27, channels // CORES, channels)

    def swapped(boxes, axis, phases):
        size = lax.axis_size(axis)
        return [
            lax.ppermute(box, axis, swap_pairs(size, phase)) for box, phase in zip(boxes, phases)
        ]

    def store_of(entries):
        return pltpu.VMEM((entries, EDGE, PLANE, 128), BF16)

    pack_x = run(
        functools.partial(pack_x_kernel, counts, send),
        [x_type] * number_x,
        [SMEM, VMEM] + [VMEM] * number_y,
        [VMEM] * number_x,
    )

    y_boxes = run(
        functools.partial(pack_y_kernel, counts, send), [y_type] * number_y, [SMEM, VMEM], [VMEM] * number_y
    )(lists, bricks)
    y_boxes = swapped(y_boxes, "gy", phases_y)
    taps, back_taps = run(
        taps_kernel,
        [jax.ShapeDtypeStruct((1152, 384), BF16), jax.ShapeDtypeStruct((384, 1152), BF16)],
        [VMEM],
        [VMEM, VMEM],
    )(weight.reshape(27, channels, channels))
    x_boxes = swapped(pack_x(lists, bricks, *y_boxes), "gx", phases_x)
    views, preacts = run(
        own_kernel, [views_type, preact_type], [SMEM, VMEM, VMEM], [VMEM, VMEM], [store_of(slots + 1)], micros=4.0
    )(table, bricks, taps)
    _, _, activated, grads, kept, sent, *y_boxes = run(
        functools.partial(forward_kernel, counts, send, factor),
        [
            views_type,
            preact_type,
            bricks_type,
            bricks_type,
            jax.ShapeDtypeStruct(half_shape, F32),
            jax.ShapeDtypeStruct(half_shape, BF16),
        ]
        + [y_type] * number_y,
        [SMEM, SMEM] + [VMEM] * (4 + number_x + number_y),
        [VMEM] * (6 + number_y),
        [store_of(8 * send + 1), pltpu.VMEM((4, slots * PLANE, 384), BF16)],
        aliases={2: 0, 3: 1},
        micros=5.0,
    )(table, lists, views, preacts, cot, taps, *x_boxes, *y_boxes)
    y_boxes = swapped(y_boxes, "gy", phases_y)
    x_boxes = swapped(pack_x(lists, grads, *y_boxes), "gx", phases_x)
    input_grad = run(
        functools.partial(backward_kernel, counts, send),
        bricks_type,
        [SMEM, VMEM, VMEM] + [VMEM] * (number_x + number_y),
        VMEM,
        [store_of(slots + 8 * send + 1), pltpu.VMEM(views_type.shape, BF16)],
        micros=5.0,
    )(table, grads, back_taps, *x_boxes, *y_boxes)
    weight_grad = summed_everywhere(kept, sent)
    return (
        activated.reshape(features.shape),
        input_grad.reshape(features.shape),
        weight_grad.reshape(weight.shape),
    )


def solution(mesh):
    split = P("dp", "gx", "gy", None, None, None)
    table = P("dp", "gx", "gy", None, None)
    return jax.shard_map(
        body,
        mesh=mesh,
        in_specs=(split, P(), split, table, table),
        out_specs=(split, split, P()),
        check_vma=False,
    )
```

```python
import functools
import math

import jax
import jax.numpy as jnp
from jax import lax
from jax.experimental import pallas as pl
from jax.experimental.pallas import tpu as pltpu
from jax.sharding import PartitionSpec as P

EDGE = 8
PLANE = EDGE * EDGE
VMEM_BYTES = 28 * 2**20
CORES = 2

F32 = jnp.float32
BF16 = jnp.bfloat16


def swap_phases(size):
    return ([0] if size > 1 else []) + ([1] if size > 2 else [])


def swap_pairs(size, phase):
    pairs = []
    for low in range(phase, size - 1, 2):
        pairs += [(low, low + 1), (low + 1, low)]
    return pairs


def step_of(at, phase):
    return jnp.where(at % 2 == phase, 1, -1)


def direction(step_x, step_y):
    flat = 3 * (step_x + 1) + step_y + 1
    return flat - jnp.where(flat > 4, 1, 0)


def low_or_high(group, upper):
    wide = group.astype(F32)
    return wide[..., EDGE:, :] if upper else wide[..., :EDGE, :]


def y_edge(bricks, slot, plane, step_y):
    low = low_or_high(bricks[slot, plane, 0:16, :], False)
    high = low_or_high(bricks[slot, plane, PLANE - 16 : PLANE, :], True)
    return jnp.where(step_y > 0, high, low)


def pack_along_y(bricks, lists, box, step_y, send):
    number = direction(0, step_y)
    for entry in range(send):
        listed = lists[entry, number]
        face = y_edge(bricks, jnp.maximum(listed, 0), slice(0, EDGE), step_y)
        face = jnp.where(listed >= 0, face, 0.0).reshape(PLANE, 128)
        box[entry * PLANE : (entry + 1) * PLANE] = face.astype(BF16)
    at = send * PLANE
    for step_x in (-1, 1):
        number = direction(step_x, step_y)
        pieces = []
        for entry in range(send):
            listed = lists[entry, number]
            plane = EDGE - 1 if step_x > 0 else 0
            edge = y_edge(bricks, jnp.maximum(listed, 0), plane, step_y)
            pieces.append(jnp.where(listed >= 0, edge, 0.0))
        box[at : at + send * EDGE] = jnp.concatenate(pieces, axis=0).astype(BF16)
        at += send * EDGE


def pack_along_x(bricks, lists, box, y_boxes, step_x, send):
    number = direction(step_x, 0)
    for entry in range(send):
        listed = lists[entry, number]
        face = bricks[jnp.maximum(listed, 0), jnp.where(step_x > 0, EDGE - 1, 0)]
        box[entry * PLANE : (entry + 1) * PLANE] = jnp.where(listed >= 0, face, jnp.zeros_like(face))
    at = send * PLANE
    for y_box in y_boxes:
        first = y_box[send * PLANE : send * PLANE + send * EDGE]
        second = y_box[send * PLANE + send * EDGE : send * PLANE + 2 * send * EDGE]
        box[at : at + send * EDGE] = jnp.where(step_x > 0, second, first)
        at += send * EDGE


def fill_remote(store, base, x_boxes, y_boxes, steps_x, steps_y, send):
    store[store.shape[0] - 1] = jnp.zeros(store.shape[1:], BF16)
    for step_y, box in zip(steps_y, y_boxes):
        number = direction(0, step_y)
        for entry in range(send):
            rows = box[entry * PLANE : (entry + 1) * PLANE].astype(F32).reshape(EDGE, EDGE, 128)
            twice = jnp.concatenate([rows, rows], axis=1).astype(BF16)
            store[base + number * send + entry, :, 0:16, :] = twice
            store[base + number * send + entry, :, PLANE - 16 : PLANE, :] = twice
    for step_x, box in zip(steps_x, x_boxes):
        number = direction(step_x, 0)
        for entry in range(send):
            face = box[entry * PLANE : (entry + 1) * PLANE]
            store[base + number * send + entry, 0] = face
            store[base + number * send + entry, EDGE - 1] = face
        at = send * PLANE
        for step_y in steps_y:
            number = direction(step_x, step_y)
            edges = box[at : at + send * EDGE].astype(F32)
            at += send * EDGE
            for entry in range(send):
                rows = edges[entry * EDGE : (entry + 1) * EDGE]
                twice = jnp.concatenate([rows, rows], axis=0).astype(BF16)
                for plane in (0, EDGE - 1):
                    store[base + number * send + entry, plane, 0:16, :] = twice
                    store[base + number * send + entry, plane, PLANE - 16 : PLANE, :] = twice


def view_of(store, entry, off_x, source):
    middle = store[entry(off_x, 0), source]
    before = low_or_high(store[entry(off_x, -1), source, PLANE - 16 : PLANE, :], True)
    after = low_or_high(store[entry(off_x, 1), source, 0:16, :], False)
    wide = middle.astype(F32)
    axis = wide.ndim - 2
    left = jnp.concatenate([before, wide[..., : PLANE - EDGE, :]], axis=axis).astype(BF16)
    right = jnp.concatenate([wide[..., EDGE:, :], after], axis=axis).astype(BF16)
    return jnp.concatenate([left, middle, right], axis=axis + 1)


def fill_views(views, store, entry):
    views[0] = view_of(store, entry, -1, EDGE - 1)
    views[1 : EDGE + 1] = view_of(store, entry, 0, slice(0, EDGE))
    views[EDGE + 1] = view_of(store, entry, 1, 0)


def lookup(table, slot, first, last, zero_at):
    def entry(off_x, off_y):
        listed = table[slot, 9 * (off_x + 1) + 3 * (off_y + 1) + 1]
        return jnp.where((listed >= first) & (listed < last), listed - first, zero_at)

    return entry


def lhs_of(views):
    return jnp.concatenate(
        [views[dx : dx + EDGE].reshape(EDGE * PLANE, 384) for dx in range(3)], axis=1
    )


def shift_rows(wide, step):
    row = lax.broadcasted_iota(jnp.int32, wide.shape, 1)
    moved = pltpu.roll(wide, (-step) % EDGE, 1)
    return jnp.where(row == (EDGE - 1 if step > 0 else 0), 0.0, moved)


def join_taps(parts):
    shape = (parts.shape[0] // EDGE, EDGE, 128)
    blocks = [parts[:, 128 * dz : 128 * dz + 128].reshape(shape) for dz in range(3)]
    return blocks[1] + shift_rows(blocks[0], -1) + shift_rows(blocks[2], 1)


def steps_here(counts):
    steps_x = [step_of(lax.axis_index("gx"), phase) for phase in swap_phases(counts[0])]
    steps_y = [step_of(lax.axis_index("gy"), phase) for phase in swap_phases(counts[1])]
    return steps_x, steps_y


def pack_y_kernel(counts, send, lists, bricks, *boxes):
    for step_y, box in zip(steps_here(counts)[1], boxes):
        pack_along_y(bricks, lists, box, step_y, send)


def pack_x_kernel(counts, send, lists, bricks, *rest):
    steps_x, steps_y = steps_here(counts)
    y_boxes, x_boxes = rest[: len(steps_y)], rest[len(steps_y) :]
    for step_x, box in zip(steps_x, x_boxes):
        pack_along_x(bricks, lists, box, y_boxes, step_x, send)


def layout_kernel(table, bricks, weight, forward, backward, views, store):
    slots = bricks.shape[0]
    for tap in range(27):
        far, near = tap // 3 * 128, tap % 3 * 128
        forward[far : far + 128, near : near + 128] = weight[tap]
        backward[near : near + 128, far : far + 128] = weight[26 - tap]
    store[0:slots] = bricks[...]
    store[slots] = jnp.zeros(store.shape[1:], BF16)
    for slot in range(slots):
        fill_views(views.at[slot], store, lookup(table, slot, 0, slots, slots))


def own_kernel(views, taps, preact):
    for slot in range(views.shape[0]):
        parts = jnp.dot(lhs_of(views.at[slot]), taps[...], preferred_element_type=F32)
        preact[slot] = join_taps(parts).reshape(EDGE, EDGE, EDGE, 128)


def forward_kernel(counts, send, factor, table, lists, own_views, own_preact, cotangent, taps, *rest):
    steps_x, steps_y = steps_here(counts)
    number_x, number_y = len(steps_x), len(steps_y)
    x_boxes, y_boxes, rest = rest[:number_x], rest[number_x : number_x + number_y], rest[number_x + number_y :]
    views, preacts, activated, grads, kept_term, sent_term = rest[:6]
    boxes_out, (store, sides) = rest[6 : 6 + number_y], rest[6 + number_y :]
    core = lax.axis_index("dp") % CORES
    slots = cotangent.shape[0]
    fill_remote(store, 0, x_boxes, y_boxes, steps_x, steps_y, send)
    nothing = jnp.zeros((EDGE, EDGE, 128), F32)
    for slot in range(slots):
        rows = slice(slot * PLANE, (slot + 1) * PLANE)
        entry = lookup(table, slot, slots, slots + 8 * send, store.shape[0] - 1)
        for side, off_x, source, target in ((0, -1, EDGE - 1, 0), (1, 1, 0, EDGE + 1)):
            plane = view_of(store, entry, off_x, source)
            sides[side, rows] = plane
            views[slot, target] = views[slot, target] + plane
        for side, off_y, base, lanes in ((2, -1, 0, 0), (3, 1, PLANE - 16, 256)):
            group = slice(PLANE - 16, PLANE) if off_y < 0 else slice(0, 16)
            edge = low_or_high(store[entry(0, off_y), :, group, :], off_y < 0)
            padded = jnp.concatenate([nothing[:1], edge, nothing[:1]], axis=0)
            for dx in range(3):
                sides[side, rows, 128 * dx : 128 * dx + 128] = (
                    padded[dx : dx + EDGE].reshape(PLANE, 128).astype(BF16)
                )
            both = [edge, nothing] if off_y < 0 else [nothing, edge]
            wide = jnp.concatenate(both, axis=1).astype(BF16)
            at = (slot, slice(1, EDGE + 1), slice(base, base + 16), slice(lanes, lanes + 128))
            views[at] = views[at] + wide
    added = []
    for side in range(4):
        if side < 2:
            part = taps[768 * side : 768 * side + 384]
        else:
            dy = 0 if side == 2 else 2
            part = jnp.concatenate(
                [taps[(3 * dx + dy) * 128 : (3 * dx + dy) * 128 + 128] for dx in range(3)], axis=0
            )
        product = join_taps(jnp.dot(sides[side], part, preferred_element_type=F32))
        added.append(product.reshape(slots, EDGE, EDGE, 128))
    for slot in range(slots):
        preacts[slot, 0] = preacts[slot, 0] + added[0][slot]
        preacts[slot, EDGE - 1] = preacts[slot, EDGE - 1] + added[1][slot]
        preacts[slot, :, 0] = preacts[slot, :, 0] + added[2][slot]
        preacts[slot, :, EDGE - 1] = preacts[slot, :, EDGE - 1] + added[3][slot]
        preact = preacts[slot].reshape(PLANE, EDGE, 128)
        sigmoid = jax.nn.sigmoid(preact)
        activated[slot] = (preact * sigmoid).reshape(EDGE, PLANE, 128).astype(BF16)
        slope = sigmoid * (1.0 + preact * (1.0 - sigmoid))
        wide = cotangent[slot].astype(F32).reshape(PLANE, EDGE, 128) * slope
        wide = jnp.where(table[slot, 13] >= 0, wide, 0.0)
        grads[slot] = wide.reshape(EDGE, PLANE, 128).astype(BF16)
    for step_y, box in zip(steps_y, boxes_out):
        pack_along_y(grads, lists, box, step_y, send)
    total = None
    for slot in range(slots):
        grad = grads[slot].astype(F32).reshape(PLANE, EDGE, 128)
        shifted = [shift_rows(grad, 1), grad, shift_rows(grad, -1)]
        rhs = jnp.concatenate([s.reshape(EDGE * PLANE, 128) for s in shifted], axis=1).astype(BF16)
        term = lax.dot_general(
            lhs_of(views.at[slot]), rhs, (((0,), (0,)), ((), ())), preferred_element_type=F32
        )
        total = term if total is None else total + term
    half = 128 // CORES
    for tap in range(27):
        far, near = tap // 3 * 128, tap % 3 * 128
        block = total[far : far + 128, near : near + 128] * factor
        first, second = block[:half], block[half:]
        rows = slice(tap * half, (tap + 1) * half)
        kept_term[rows] = jnp.where(core == 0, first, second)
        sent_term[rows] = jnp.where(core == 0, second, first).astype(BF16)
    for term in (kept_term, sent_term):
        if term.shape[0] > 27 * half:
            term[27 * half :] = jnp.zeros((term.shape[0] - 27 * half, 128), term.dtype)


def backward_kernel(counts, send, table, bricks, taps, *rest):
    steps_x, steps_y = steps_here(counts)
    x_boxes, y_boxes = rest[: len(steps_x)], rest[len(steps_x) : len(steps_x) + len(steps_y)]
    result, ready, store, views = rest[-4:]
    slots = bricks.shape[0]
    store[0:slots] = bricks[...]
    fill_remote(store, slots, x_boxes, y_boxes, steps_x, steps_y, send)
    zero_at = store.shape[0] - 1
    for slot in range(slots):
        fill_views(views.at[slot], store, lookup(table, slot, 0, zero_at, zero_at))
        parts = lax.dot_general(
            lhs_of(views.at[slot]), taps[...], (((1,), (1,)), ((), ())), preferred_element_type=F32
        )
        result[slot] = join_taps(parts).reshape(EDGE, PLANE, 128).astype(BF16)
    ready[...] = jnp.zeros(ready.shape, F32)


VMEM = pl.BlockSpec(memory_space=pltpu.VMEM)
SMEM = pl.BlockSpec(memory_space=pltpu.SMEM)
ANY = pl.BlockSpec(memory_space=pl.ANY)
PARAMS = pltpu.CompilerParams(vmem_limit_bytes=VMEM_BYTES)


def run(kernel, out_shape, ins, outs, scratch=(), aliases=None, micros=1.0):
    cost = pl.CostEstimate(flops=int(micros * 1e9), bytes_accessed=2**16, transcendentals=0)
    return pl.pallas_call(
        kernel,
        out_shape=out_shape,
        in_specs=ins,
        out_specs=outs,
        scratch_shapes=list(scratch),
        input_output_aliases=aliases or {},
        compiler_params=PARAMS,
        cost_estimate=cost,
    )


class Groups:
    def __init__(self):
        self.sizes = tuple(lax.axis_size(name) for name in ("dp", "gx", "gy"))
        dp, gx, gy = self.sizes
        self.plane, self.line = dp // CORES * gy, gx
        self.turned = self.plane == self.line
        at = lax.axis_index("dp")
        in_plane = at // CORES * gy + lax.axis_index("gy")
        self.core = at % CORES
        if self.turned:
            first = jnp.where(self.core == 0, in_plane, lax.axis_index("gx"))
        else:
            first = in_plane
        self.mine = first.astype(jnp.int32)

    def pairs(self, place):
        dp, gx, gy = self.sizes
        out = []
        for a in range(dp):
            for b in range(gx):
                for c in range(gy):
                    to = place(a, b, c)
                    out.append(((a * gx + b) * gy + c, (to[0] * gx + to[1]) * gy + to[2]))
        return out

    def swap(self, x, stage, mask):
        gy = self.sizes[2]

        def place(a, b, c):
            if self.turned and a % CORES == 1:
                plane = stage == 1
            else:
                plane = stage == 0
            if plane:
                return a ^ (mask // gy * CORES), b, c ^ (mask % gy)
            return a, b ^ mask, c

        return lax.ppermute(x, ("dp", "gx", "gy"), self.pairs(place))

    def swap_cores(self, x):
        return lax.ppermute(x, ("dp", "gx", "gy"), self.pairs(lambda a, b, c: (a ^ 1, b, c)))


def tree_sum(terms):
    while len(terms) > 1:
        terms = [a + b for a, b in zip(terms[::2], terms[1::2])]
    return terms[0]


def share_kernel(mine, kept, arrived, own, *boxes):
    own[...] = kept[mine[0]] + arrived[mine[0]].astype(F32)
    for mask, box in enumerate(boxes, 1):
        at = mine[0] ^ mask
        box[...] = (kept[at] + arrived[at].astype(F32)).astype(BF16)


def first_sum_kernel(own, *rest):
    total = own[...]
    for box in rest[:-2]:
        total = total + box[...].astype(F32)
    rest[-1][...] = total.astype(BF16)


def second_sum_kernel(*rest):
    rest[-1][...] = tree_sum([box[...].astype(F32) for box in rest[:-2]]).astype(BF16)


def gather_kernel(mine, *rest):
    for mask, box in enumerate(rest[:-1]):
        rest[-1][mine[0] ^ mask] = box[...]


def spread_kernel(core, own, other, out):
    half = out.shape[1] // CORES
    for tap in range(27):
        rows = slice(tap * half, (tap + 1) * half)
        out[tap, pl.ds(pl.multiple_of(core[0] * half, half), half)] = own[rows].astype(F32)
        out[tap, pl.ds(pl.multiple_of((1 - core[0]) * half, half), half)] = other[rows].astype(F32)


def summed_everywhere(groups, kept, sent, early, late):
    group, line = groups.plane, groups.line
    rows = kept.shape[0] // group
    shares = (group, rows, 128)
    share_type = jax.ShapeDtypeStruct((rows, 128), BF16)
    mine = groups.mine.reshape(1)
    arrived = groups.swap_cores(sent)
    own, *boxes = run(
        share_kernel,
        [jax.ShapeDtypeStruct((rows, 128), F32)] + [share_type] * (group - 1),
        [SMEM, VMEM, VMEM],
        [VMEM] * group,
    )(mine, kept.reshape(shares), arrived.reshape(shares))
    boxes = [groups.swap(box, 0, mask) for mask, box in enumerate(boxes, 1)]
    rounded = run(first_sum_kernel, share_type, [VMEM] * group + [ANY], VMEM)(own, *boxes, early)
    boxes = [rounded] + [groups.swap(rounded, 1, mask) for mask in range(1, line)]
    rounded = run(second_sum_kernel, share_type, [VMEM] * line + [ANY], VMEM)(*boxes, late)
    boxes = [rounded] + [groups.swap(rounded, 0, mask) for mask in range(1, group)]
    half = run(
        gather_kernel, jax.ShapeDtypeStruct(shares, BF16), [SMEM] + [VMEM] * group, VMEM
    )(mine, *boxes).reshape(kept.shape)
    other = groups.swap_cores(half)
    return run(
        spread_kernel, jax.ShapeDtypeStruct((27, 128, 128), F32), [SMEM, VMEM, VMEM], VMEM
    )(groups.core.astype(jnp.int32).reshape(1), half, other)


def body(features, weight, cotangent, neighbours, send_slots):
    slots, _, channels = features.shape[3:]
    send = send_slots.shape[-1]
    counts = (lax.axis_size("gx"), lax.axis_size("gy"))
    devices = lax.axis_size("dp") * counts[0] * counts[1]
    bricks = features.reshape(slots, EDGE, PLANE, channels)
    cot = cotangent.reshape(slots, EDGE, PLANE, channels)
    table = neighbours.reshape(slots, 27)
    lists = send_slots.reshape(8, send).T
    factor = 1.0 / math.sqrt(float(devices * slots * EDGE * PLANE))
    phases_x, phases_y = swap_phases(counts[0]), swap_phases(counts[1])
    number_x, number_y = len(phases_x), len(phases_y)
    y_type = jax.ShapeDtypeStruct((send * (PLANE + 2 * EDGE), 128), BF16)
    x_type = jax.ShapeDtypeStruct((send * (PLANE + number_y * EDGE), 128), BF16)
    bricks_type = jax.ShapeDtypeStruct(bricks.shape, BF16)
    views_type = jax.ShapeDtypeStruct((slots, EDGE + 2, PLANE, 384), BF16)
    preact_type = jax.ShapeDtypeStruct((slots, EDGE, EDGE, EDGE, 128), F32)
    groups = Groups()
    block = 16 * groups.plane
    half_shape = (-(-27 * channels // CORES // block) * block, channels)

    def swapped(boxes, axis, phases):
        size = lax.axis_size(axis)
        return [
            lax.ppermute(box, axis, swap_pairs(size, phase)) for box, phase in zip(boxes, phases)
        ]

    def store_of(entries):
        return pltpu.VMEM((entries, EDGE, PLANE, 128), BF16)

    pack_x = run(
        functools.partial(pack_x_kernel, counts, send),
        [x_type] * number_x,
        [SMEM, VMEM] + [VMEM] * number_y,
        [VMEM] * number_x,
    )

    y_boxes = run(
        functools.partial(pack_y_kernel, counts, send), [y_type] * number_y, [SMEM, VMEM], [VMEM] * number_y
    )(lists, bricks)
    y_boxes = swapped(y_boxes, "gy", phases_y)
    taps, back_taps, views = run(
        layout_kernel,
        [
            jax.ShapeDtypeStruct((1152, 384), BF16),
            jax.ShapeDtypeStruct((384, 1152), BF16),
            views_type,
        ],
        [SMEM, VMEM, VMEM],
        [VMEM] * 3,
        [store_of(slots + 1)],
        micros=2.0,
    )(table, bricks, weight.reshape(27, channels, channels))
    x_boxes = swapped(pack_x(lists, bricks, *y_boxes), "gx", phases_x)
    preacts = run(own_kernel, preact_type, [VMEM, VMEM], VMEM, micros=4.0)(views, taps)
    _, _, activated, grads, kept, sent, *y_boxes = run(
        functools.partial(forward_kernel, counts, send, factor),
        [
            views_type,
            preact_type,
            bricks_type,
            bricks_type,
            jax.ShapeDtypeStruct(half_shape, F32),
            jax.ShapeDtypeStruct(half_shape, BF16),
        ]
        + [y_type] * number_y,
        [SMEM, SMEM] + [VMEM] * (4 + number_x + number_y),
        [VMEM] * (6 + number_y),
        [store_of(8 * send + 1), pltpu.VMEM((4, slots * PLANE, 384), BF16)],
        aliases={2: 0, 3: 1},
        micros=5.0,
    )(table, lists, views, preacts, cot, taps, *x_boxes, *y_boxes)
    y_boxes = swapped(y_boxes, "gy", phases_y)
    packed = pack_x(lists, grads, *y_boxes)
    x_boxes = swapped(packed, "gx", phases_x)
    input_grad, ready = run(
        functools.partial(backward_kernel, counts, send),
        [bricks_type, jax.ShapeDtypeStruct((8, 128), F32)],
        [SMEM, VMEM, VMEM] + [VMEM] * (number_x + number_y),
        [VMEM, VMEM],
        [store_of(slots + 8 * send + 1), pltpu.VMEM(views_type.shape, BF16)],
        micros=5.0,
    )(table, grads, back_taps, *x_boxes, *y_boxes)
    weight_grad = summed_everywhere(groups, kept, sent, packed[-1], ready)
    return (
        activated.reshape(features.shape),
        input_grad.reshape(features.shape),
        weight_grad.reshape(weight.shape),
    )


def solution(mesh):
    split = P("dp", "gx", "gy", None, None, None)
    table = P("dp", "gx", "gy", None, None)
    return jax.shard_map(
        body,
        mesh=mesh,
        in_specs=(split, P(), split, table, table),
        out_specs=(split, split, P()),
        check_vma=False,
    )
```

```python
import functools
import math

import jax
import jax.numpy as jnp
from jax import lax
from jax.experimental import pallas as pl
from jax.experimental.pallas import tpu as pltpu
from jax.sharding import PartitionSpec as P

EDGE = 8
PLANE = EDGE * EDGE
VMEM_BYTES = 28 * 2**20
CORES = 2

F32 = jnp.float32
BF16 = jnp.bfloat16


def swap_phases(size):
    return ([0] if size > 1 else []) + ([1] if size > 2 else [])


def partner_of(at, size, phase):
    other = at + 1 if at % 2 == phase else at - 1
    return other if 0 <= other < size else at


def swap(x, axis, phase):
    sizes = [lax.axis_size(name) for name in ("dp", axis)]
    pairs = []
    for at in range(sizes[0]):
        for tile in range(sizes[1]):
            other = partner_of(tile, sizes[1], phase)
            to = (at ^ 1 if other == tile else at) * sizes[1] + other
            pairs.append((at * sizes[1] + tile, to))
    return lax.ppermute(x, ("dp", axis), pairs)


def inside(at, size, step):
    return (at + step >= 0) & (at + step < size)


def step_of(at, phase):
    return jnp.where(at % 2 == phase, 1, -1)


def direction(step_x, step_y):
    flat = 3 * (step_x + 1) + step_y + 1
    return flat - jnp.where(flat > 4, 1, 0)


def low_or_high(group, upper):
    wide = group.astype(F32)
    return wide[..., EDGE:, :] if upper else wide[..., :EDGE, :]


def y_edge(bricks, slot, plane, step_y):
    low = low_or_high(bricks[slot, plane, 0:16, :], False)
    high = low_or_high(bricks[slot, plane, PLANE - 16 : PLANE, :], True)
    return jnp.where(step_y > 0, high, low)


def pack_along_y(bricks, lists, box, step_y, send):
    number = direction(0, step_y)
    for entry in range(send):
        listed = lists[entry, number]
        face = y_edge(bricks, jnp.maximum(listed, 0), slice(0, EDGE), step_y)
        face = jnp.where(listed >= 0, face, 0.0).reshape(PLANE, 128)
        box[entry * PLANE : (entry + 1) * PLANE] = face.astype(BF16)
    at = send * PLANE
    for step_x in (-1, 1):
        number = direction(step_x, step_y)
        pieces = []
        for entry in range(send):
            listed = lists[entry, number]
            plane = EDGE - 1 if step_x > 0 else 0
            edge = y_edge(bricks, jnp.maximum(listed, 0), plane, step_y)
            pieces.append(jnp.where(listed >= 0, edge, 0.0))
        box[at : at + send * EDGE] = jnp.concatenate(pieces, axis=0).astype(BF16)
        at += send * EDGE


def pack_along_x(bricks, lists, box, step_x, send):
    number = direction(step_x, 0)
    for entry in range(send):
        listed = lists[entry, number]
        face = bricks[jnp.maximum(listed, 0), jnp.where(step_x > 0, EDGE - 1, 0)]
        box[entry * PLANE : (entry + 1) * PLANE] = jnp.where(listed >= 0, face, jnp.zeros_like(face))


def join_along_x(faces, box, y_boxes, step_x, send):
    at = send * PLANE
    box[:at] = faces[...]
    for y_box in y_boxes:
        first = y_box[send * PLANE : send * PLANE + send * EDGE]
        second = y_box[send * PLANE + send * EDGE : send * PLANE + 2 * send * EDGE]
        box[at : at + send * EDGE] = jnp.where(step_x > 0, second, first)
        at += send * EDGE


def fill_remote(store, base, x_boxes, y_boxes, tiles_x, tiles_y, send):
    store[store.shape[0] - 1] = jnp.zeros(store.shape[1:], BF16)
    for (step_y, in_y), box in zip(tiles_y, y_boxes):
        number = direction(0, step_y)
        for entry in range(send):
            rows = box[entry * PLANE : (entry + 1) * PLANE].astype(F32).reshape(EDGE, EDGE, 128)
            rows = jnp.where(in_y, rows, 0.0)
            twice = jnp.concatenate([rows, rows], axis=1).astype(BF16)
            store[base + number * send + entry, :, 0:16, :] = twice
            store[base + number * send + entry, :, PLANE - 16 : PLANE, :] = twice
    for (step_x, in_x), box in zip(tiles_x, x_boxes):
        number = direction(step_x, 0)
        for entry in range(send):
            face = box[entry * PLANE : (entry + 1) * PLANE]
            face = jnp.where(in_x, face, jnp.zeros_like(face))
            store[base + number * send + entry, 0] = face
            store[base + number * send + entry, EDGE - 1] = face
        at = send * PLANE
        for step_y, in_y in tiles_y:
            number = direction(step_x, step_y)
            edges = jnp.where(in_x & in_y, box[at : at + send * EDGE].astype(F32), 0.0)
            at += send * EDGE
            for entry in range(send):
                rows = edges[entry * EDGE : (entry + 1) * EDGE]
                twice = jnp.concatenate([rows, rows], axis=0).astype(BF16)
                for plane in (0, EDGE - 1):
                    store[base + number * send + entry, plane, 0:16, :] = twice
                    store[base + number * send + entry, plane, PLANE - 16 : PLANE, :] = twice


def view_of(store, entry, off_x, source):
    middle = store[entry(off_x, 0), source]
    before = low_or_high(store[entry(off_x, -1), source, PLANE - 16 : PLANE, :], True)
    after = low_or_high(store[entry(off_x, 1), source, 0:16, :], False)
    wide = middle.astype(F32)
    axis = wide.ndim - 2
    left = jnp.concatenate([before, wide[..., : PLANE - EDGE, :]], axis=axis).astype(BF16)
    right = jnp.concatenate([wide[..., EDGE:, :], after], axis=axis).astype(BF16)
    return jnp.concatenate([left, middle, right], axis=axis + 1)


def fill_views(views, store, entry):
    views[0] = view_of(store, entry, -1, EDGE - 1)
    views[1 : EDGE + 1] = view_of(store, entry, 0, slice(0, EDGE))
    views[EDGE + 1] = view_of(store, entry, 1, 0)


def lookup(table, slot, first, last, zero_at):
    def entry(off_x, off_y):
        listed = table[slot, 9 * (off_x + 1) + 3 * (off_y + 1) + 1]
        return jnp.where((listed >= first) & (listed < last), listed - first, zero_at)

    return entry


def lhs_of(views):
    return jnp.concatenate(
        [views[dx : dx + EDGE].reshape(EDGE * PLANE, 384) for dx in range(3)], axis=1
    )


def shift_rows(wide, step):
    row = lax.broadcasted_iota(jnp.int32, wide.shape, 1)
    moved = pltpu.roll(wide, (-step) % EDGE, 1)
    return jnp.where(row == (EDGE - 1 if step > 0 else 0), 0.0, moved)


def join_taps(parts):
    shape = (parts.shape[0] // EDGE, EDGE, 128)
    blocks = [parts[:, 128 * dz : 128 * dz + 128].reshape(shape) for dz in range(3)]
    return blocks[1] + shift_rows(blocks[0], -1) + shift_rows(blocks[2], 1)


def tiles_here(counts):
    out = []
    for name, size in zip(("gx", "gy"), counts):
        at = lax.axis_index(name)
        steps = [step_of(at, phase) for phase in swap_phases(size)]
        out.append([(step, inside(at, size, step)) for step in steps])
    return out


def pack_all(bricks, lists, x_boxes, y_boxes, counts, send):
    tiles_x, tiles_y = tiles_here(counts)
    for (step_y, _), box in zip(tiles_y, y_boxes):
        pack_along_y(bricks, lists, box, step_y, send)
    for (step_x, _), box in zip(tiles_x, x_boxes):
        pack_along_x(bricks, lists, box, step_x, send)


def start_kernel(counts, send, lists_hbm, bricks_hbm, bricks, *rest):
    boxes, (lists, sems) = rest[:-2], rest[-2:]
    copies = [
        pltpu.make_async_copy(bricks_hbm, bricks, sems.at[0]),
        pltpu.make_async_copy(lists_hbm, lists, sems.at[1]),
    ]
    for copy in copies:
        copy.start()
    for copy in copies:
        copy.wait()
    number_x = len(swap_phases(counts[0]))
    pack_all(bricks, lists, boxes[:number_x], boxes[number_x:], counts, send)


def join_kernel(counts, send, *rest):
    tiles_x, tiles_y = tiles_here(counts)
    number_x, number_y = len(tiles_x), len(tiles_y)
    faces, y_boxes, x_boxes = rest[:number_x], rest[number_x : number_x + number_y], rest[number_x + number_y :]
    for (step_x, _), face, box in zip(tiles_x, faces, x_boxes):
        join_along_x(face, box, y_boxes, step_x, send)


def layout_kernel(table, bricks, weight, forward, backward, views, store):
    slots = bricks.shape[0]
    for tap in range(27):
        far, near = tap // 3 * 128, tap % 3 * 128
        forward[far : far + 128, near : near + 128] = weight[tap]
        backward[near : near + 128, far : far + 128] = weight[26 - tap]
    store[0:slots] = bricks[...]
    store[slots] = jnp.zeros(store.shape[1:], BF16)
    for slot in range(slots):
        fill_views(views.at[slot], store, lookup(table, slot, 0, slots, slots))


def own_kernel(views, taps, preact):
    for slot in range(views.shape[0]):
        parts = jnp.dot(lhs_of(views.at[slot]), taps[...], preferred_element_type=F32)
        preact[slot] = join_taps(parts).reshape(EDGE, EDGE, EDGE, 128)


def forward_kernel(counts, send, factor, table_vmem, lists_vmem, own_views, own_preact, cotangent, taps, *rest):
    tiles_x, tiles_y = tiles_here(counts)
    number_x, number_y = len(tiles_x), len(tiles_y)
    x_boxes, y_boxes, rest = rest[:number_x], rest[number_x : number_x + number_y], rest[number_x + number_y :]
    views, preacts, activated, grads, kept_term, sent_term = rest[:6]
    faces_out, boxes_out = rest[6 : 6 + number_x], rest[6 + number_x : 6 + number_x + number_y]
    store, sides, table, lists, sems = rest[6 + number_x + number_y :]
    copies = [
        pltpu.make_async_copy(table_vmem, table, sems.at[0]),
        pltpu.make_async_copy(lists_vmem, lists, sems.at[1]),
    ]
    for copy in copies:
        copy.start()
    core = lax.axis_index("dp") % CORES
    slots = cotangent.shape[0]
    fill_remote(store, 0, x_boxes, y_boxes, tiles_x, tiles_y, send)
    for copy in copies:
        copy.wait()
    nothing = jnp.zeros((EDGE, EDGE, 128), F32)
    for slot in range(slots):
        rows = slice(slot * PLANE, (slot + 1) * PLANE)
        entry = lookup(table, slot, slots, slots + 8 * send, store.shape[0] - 1)
        for side, off_x, source, target in ((0, -1, EDGE - 1, 0), (1, 1, 0, EDGE + 1)):
            plane = view_of(store, entry, off_x, source)
            sides[side, rows] = plane
            views[slot, target] = views[slot, target] + plane
        for side, off_y, base, lanes in ((2, -1, 0, 0), (3, 1, PLANE - 16, 256)):
            group = slice(PLANE - 16, PLANE) if off_y < 0 else slice(0, 16)
            edge = low_or_high(store[entry(0, off_y), :, group, :], off_y < 0)
            padded = jnp.concatenate([nothing[:1], edge, nothing[:1]], axis=0)
            for dx in range(3):
                sides[side, rows, 128 * dx : 128 * dx + 128] = (
                    padded[dx : dx + EDGE].reshape(PLANE, 128).astype(BF16)
                )
            both = [edge, nothing] if off_y < 0 else [nothing, edge]
            wide = jnp.concatenate(both, axis=1).astype(BF16)
            at = (slot, slice(1, EDGE + 1), slice(base, base + 16), slice(lanes, lanes + 128))
            views[at] = views[at] + wide
    added = []
    for side in range(4):
        if side < 2:
            part = taps[768 * side : 768 * side + 384]
        else:
            dy = 0 if side == 2 else 2
            part = jnp.concatenate(
                [taps[(3 * dx + dy) * 128 : (3 * dx + dy) * 128 + 128] for dx in range(3)], axis=0
            )
        product = join_taps(jnp.dot(sides[side], part, preferred_element_type=F32))
        added.append(product.reshape(slots, EDGE, EDGE, 128))
    for slot in range(slots):
        preacts[slot, 0] = preacts[slot, 0] + added[0][slot]
        preacts[slot, EDGE - 1] = preacts[slot, EDGE - 1] + added[1][slot]
        preacts[slot, :, 0] = preacts[slot, :, 0] + added[2][slot]
        preacts[slot, :, EDGE - 1] = preacts[slot, :, EDGE - 1] + added[3][slot]
        preact = preacts[slot].reshape(PLANE, EDGE, 128)
        sigmoid = jax.nn.sigmoid(preact)
        activated[slot] = (preact * sigmoid).reshape(EDGE, PLANE, 128).astype(BF16)
        slope = sigmoid * (1.0 + preact * (1.0 - sigmoid))
        wide = cotangent[slot].astype(F32).reshape(PLANE, EDGE, 128) * slope
        wide = jnp.where(table[slot, 13] >= 0, wide, 0.0)
        grads[slot] = wide.reshape(EDGE, PLANE, 128).astype(BF16)
    pack_all(grads, lists, faces_out, boxes_out, counts, send)
    total = None
    for slot in range(slots):
        grad = grads[slot].astype(F32).reshape(PLANE, EDGE, 128)
        shifted = [shift_rows(grad, 1), grad, shift_rows(grad, -1)]
        rhs = jnp.concatenate([s.reshape(EDGE * PLANE, 128) for s in shifted], axis=1).astype(BF16)
        term = lax.dot_general(
            lhs_of(views.at[slot]), rhs, (((0,), (0,)), ((), ())), preferred_element_type=F32
        )
        total = term if total is None else total + term
    half = 128 // CORES
    for tap in range(27):
        far, near = tap // 3 * 128, tap % 3 * 128
        block = total[far : far + 128, near : near + 128] * factor
        first, second = block[:half], block[half:]
        rows = slice(tap * half, (tap + 1) * half)
        kept_term[rows] = jnp.where(core == 0, first, second)
        sent_term[rows] = jnp.where(core == 0, second, first).astype(BF16)
    for term in (kept_term, sent_term):
        if term.shape[0] > 27 * half:
            term[27 * half :] = jnp.zeros((term.shape[0] - 27 * half, 128), term.dtype)


def backward_kernel(counts, send, table, bricks, taps, *rest):
    tiles_x, tiles_y = tiles_here(counts)
    x_boxes, y_boxes = rest[: len(tiles_x)], rest[len(tiles_x) : len(tiles_x) + len(tiles_y)]
    result, ready, store, views = rest[-4:]
    slots = bricks.shape[0]
    store[0:slots] = bricks[...]
    fill_remote(store, slots, x_boxes, y_boxes, tiles_x, tiles_y, send)
    zero_at = store.shape[0] - 1
    for slot in range(slots):
        fill_views(views.at[slot], store, lookup(table, slot, 0, zero_at, zero_at))
        parts = lax.dot_general(
            lhs_of(views.at[slot]), taps[...], (((1,), (1,)), ((), ())), preferred_element_type=F32
        )
        result[slot] = join_taps(parts).reshape(EDGE, PLANE, 128).astype(BF16)
    ready[...] = jnp.zeros(ready.shape, F32)


VMEM = pl.BlockSpec(memory_space=pltpu.VMEM)
SMEM = pl.BlockSpec(memory_space=pltpu.SMEM)
ANY = pl.BlockSpec(memory_space=pl.ANY)
HBM = pl.BlockSpec(memory_space=pltpu.HBM)
PARAMS = pltpu.CompilerParams(vmem_limit_bytes=VMEM_BYTES)


def run(kernel, out_shape, ins, outs, scratch=(), aliases=None, micros=1.0):
    cost = pl.CostEstimate(flops=int(micros * 1e9), bytes_accessed=2**16, transcendentals=0)
    return pl.pallas_call(
        kernel,
        out_shape=out_shape,
        in_specs=ins,
        out_specs=outs,
        scratch_shapes=list(scratch),
        input_output_aliases=aliases or {},
        compiler_params=PARAMS,
        cost_estimate=cost,
    )


class Groups:
    def __init__(self):
        self.sizes = tuple(lax.axis_size(name) for name in ("dp", "gx", "gy"))
        dp, gx, gy = self.sizes
        self.plane, self.line = dp // CORES * gy, gx
        self.turned = self.plane == self.line
        at = lax.axis_index("dp")
        in_plane = at // CORES * gy + lax.axis_index("gy")
        self.core = at % CORES
        if self.turned:
            first = jnp.where(self.core == 0, in_plane, lax.axis_index("gx"))
        else:
            first = in_plane
        self.mine = first.astype(jnp.int32)

    def pairs(self, place):
        dp, gx, gy = self.sizes
        out = []
        for a in range(dp):
            for b in range(gx):
                for c in range(gy):
                    to = place(a, b, c)
                    out.append(((a * gx + b) * gy + c, (to[0] * gx + to[1]) * gy + to[2]))
        return out

    def swap(self, x, stage, mask):
        gy = self.sizes[2]

        def place(a, b, c):
            if self.turned and a % CORES == 1:
                plane = stage == 1
            else:
                plane = stage == 0
            if plane:
                return a ^ (mask // gy * CORES), b, c ^ (mask % gy)
            return a, b ^ mask, c

        return lax.ppermute(x, ("dp", "gx", "gy"), self.pairs(place))

    def swaps(self, boxes, stage):
        return [self.swap(box, stage, len(boxes) - at) for at, box in enumerate(boxes)]

    def swap_cores(self, x):
        return lax.ppermute(x, ("dp", "gx", "gy"), self.pairs(lambda a, b, c: (a ^ 1, b, c)))


def tree_sum(terms):
    while len(terms) > 1:
        terms = [a + b for a, b in zip(terms[::2], terms[1::2])]
    return terms[0]


def share_kernel(mine, kept, arrived, own, *boxes):
    own[...] = kept[mine[0]] + arrived[mine[0]].astype(F32)
    for mask, box in enumerate(reversed(boxes), 1):
        at = mine[0] ^ mask
        box[...] = (kept[at] + arrived[at].astype(F32)).astype(BF16)


def first_sum_kernel(own, *rest):
    total = own[...]
    for box in rest[:-2]:
        total = total + box[...].astype(F32)
    rest[-1][...] = total.astype(BF16)


def second_sum_kernel(*rest):
    terms = [box[...].astype(F32) for box in rest[-3::-1]]
    rest[-1][...] = tree_sum(terms).astype(BF16)


def gather_kernel(mine, *rest):
    for mask, box in enumerate(rest[-2::-1]):
        rest[-1][mine[0] ^ mask] = box[...]


def spread_kernel(at, half, *rest):
    out, wide, sem = rest[-3:]
    wide[...] = half[0 : wide.shape[0] * wide.shape[1]].astype(F32).reshape(wide.shape)
    copy = pltpu.make_async_copy(wide, out.at[:, at[0]], sem)
    copy.start()
    copy.wait()


def summed_everywhere(groups, kept, sent, early, late):
    group, line = groups.plane, groups.line
    rows = kept.shape[0] // group
    shares = (group, rows, 128)
    share_type = jax.ShapeDtypeStruct((rows, 128), BF16)
    mine = groups.mine.reshape(1)
    arrived = groups.swap_cores(sent)
    own, *boxes = run(
        share_kernel,
        [jax.ShapeDtypeStruct((rows, 128), F32)] + [share_type] * (group - 1),
        [SMEM, VMEM, VMEM],
        [VMEM] * group,
    )(mine, kept.reshape(shares), arrived.reshape(shares))
    boxes = groups.swaps(boxes, 0)
    rounded = run(first_sum_kernel, share_type, [VMEM] * group + [ANY], VMEM)(own, *boxes, early)
    boxes = groups.swaps([rounded] * (line - 1), 1) + [rounded]
    rounded = run(second_sum_kernel, share_type, [VMEM] * line + [ANY], VMEM)(*boxes, late)
    boxes = groups.swaps([rounded] * (group - 1), 0) + [rounded]
    half = run(
        gather_kernel, jax.ShapeDtypeStruct(shares, BF16), [SMEM] + [VMEM] * group, VMEM
    )(mine, *boxes).reshape(kept.shape)
    other = groups.swap_cores(half)
    rows = 128 // CORES
    out_type = jax.ShapeDtypeStruct((27, CORES, rows, 128), F32)
    scratch = [pltpu.VMEM((27, rows, 128), F32), pltpu.SemaphoreType.DMA]
    core = groups.core.astype(jnp.int32).reshape(1)
    out = run(spread_kernel, out_type, [SMEM, VMEM], ANY, scratch)(core, half)
    return run(spread_kernel, out_type, [SMEM, VMEM, ANY], ANY, scratch, aliases={2: 0})(1 - core, other, out)


def body(features, weight, cotangent, neighbours, send_slots):
    slots, _, channels = features.shape[3:]
    send = send_slots.shape[-1]
    counts = (lax.axis_size("gx"), lax.axis_size("gy"))
    devices = lax.axis_size("dp") * counts[0] * counts[1]
    bricks = features.reshape(slots, EDGE, PLANE, channels)
    cot = cotangent.reshape(slots, EDGE, PLANE, channels)
    table = neighbours.reshape(slots, 27)
    lists = send_slots.reshape(8, send).T
    factor = 1.0 / math.sqrt(float(devices * slots * EDGE * PLANE))
    phases_x, phases_y = swap_phases(counts[0]), swap_phases(counts[1])
    number_x, number_y = len(phases_x), len(phases_y)
    y_type = jax.ShapeDtypeStruct((send * (PLANE + 2 * EDGE), 128), BF16)
    x_type = jax.ShapeDtypeStruct((send * (PLANE + number_y * EDGE), 128), BF16)
    bricks_type = jax.ShapeDtypeStruct(bricks.shape, BF16)
    views_type = jax.ShapeDtypeStruct((slots, EDGE + 2, PLANE, 384), BF16)
    preact_type = jax.ShapeDtypeStruct((slots, EDGE, EDGE, EDGE, 128), F32)
    groups = Groups()
    block = 16 * groups.plane
    half_shape = (-(-27 * channels // CORES // block) * block, channels)

    def swapped(boxes, axis, phases):
        return [swap(box, axis, phase) for box, phase in zip(boxes, phases)]

    def store_of(entries):
        return pltpu.VMEM((entries, EDGE, PLANE, 128), BF16)

    face_type = jax.ShapeDtypeStruct((send * PLANE, 128), BF16)
    join = run(
        functools.partial(join_kernel, counts, send),
        [x_type] * number_x,
        [VMEM] * (number_x + number_y),
        [VMEM] * number_x,
    )

    bricks, *boxes = run(
        functools.partial(start_kernel, counts, send),
        [bricks_type] + [face_type] * number_x + [y_type] * number_y,
        [HBM, HBM],
        [VMEM] * (1 + number_x + number_y),
        [pltpu.SMEM((send, 8), jnp.int32), pltpu.SemaphoreType.DMA((2,))],
    )(*[pltpu.with_memory_space_constraint(x, pltpu.HBM) for x in (lists, bricks)])
    faces, y_boxes = boxes[:number_x], boxes[number_x:]
    y_boxes = swapped(y_boxes, "gy", phases_y)
    taps, back_taps, views = run(
        layout_kernel,
        [
            jax.ShapeDtypeStruct((1152, 384), BF16),
            jax.ShapeDtypeStruct((384, 1152), BF16),
            views_type,
        ],
        [SMEM, VMEM, VMEM],
        [VMEM] * 3,
        [store_of(slots + 1)],
        micros=2.0,
    )(table, bricks, weight.reshape(27, channels, channels))
    x_boxes = swapped(join(*faces, *y_boxes), "gx", phases_x)
    preacts = run(own_kernel, preact_type, [VMEM, VMEM], VMEM, micros=4.0)(views, taps)
    _, _, activated, grads, kept, sent, *boxes = run(
        functools.partial(forward_kernel, counts, send, factor),
        [
            views_type,
            preact_type,
            bricks_type,
            bricks_type,
            jax.ShapeDtypeStruct(half_shape, F32),
            jax.ShapeDtypeStruct(half_shape, BF16),
        ]
        + [face_type] * number_x
        + [y_type] * number_y,
        [VMEM] * (6 + number_x + number_y),
        [VMEM] * (6 + number_x + number_y),
        [
            store_of(8 * send + 1),
            pltpu.VMEM((4, slots * PLANE, 384), BF16),
            pltpu.SMEM(table.shape, jnp.int32),
            pltpu.SMEM(lists.shape, jnp.int32),
            pltpu.SemaphoreType.DMA((2,)),
        ],
        aliases={2: 0, 3: 1},
        micros=5.0,
    )(table, lists, views, preacts, cot, taps, *x_boxes, *y_boxes)
    faces, y_boxes = boxes[:number_x], swapped(boxes[number_x:], "gy", phases_y)
    packed = join(*faces, *y_boxes)
    x_boxes = swapped(packed, "gx", phases_x)
    input_grad, ready = run(
        functools.partial(backward_kernel, counts, send),
        [bricks_type, jax.ShapeDtypeStruct((8, 128), F32)],
        [SMEM, VMEM, VMEM] + [VMEM] * (number_x + number_y),
        [VMEM, VMEM],
        [store_of(slots + 8 * send + 1), pltpu.VMEM(views_type.shape, BF16)],
        micros=5.0,
    )(table, grads, back_taps, *x_boxes, *y_boxes)
    weight_grad = summed_everywhere(groups, kept, sent, packed[-1], ready)
    return (
        activated.reshape(features.shape),
        input_grad.reshape(features.shape),
        weight_grad.reshape(weight.shape),
    )


def solution(mesh):
    split = P("dp", "gx", "gy", None, None, None)
    table = P("dp", "gx", "gy", None, None)
    return jax.shard_map(
        body,
        mesh=mesh,
        in_specs=(split, P(), split, table, table),
        out_specs=(split, split, P()),
        check_vma=False,
    )
```

```python
import functools
import math

import jax
import jax.numpy as jnp
from jax import lax
from jax.experimental import pallas as pl
from jax.experimental.pallas import tpu as pltpu
from jax.sharding import PartitionSpec as P

EDGE = 8
PLANE = EDGE * EDGE
VMEM_BYTES = 28 * 2**20
CORES = 2

F32 = jnp.float32
BF16 = jnp.bfloat16


def swap_phases(size):
    return ([0] if size > 1 else []) + ([1] if size > 2 else [])


def partner_of(at, size, phase):
    other = at + 1 if at % 2 == phase else at - 1
    return other if 0 <= other < size else at


def swap(x, axis, phase):
    sizes = [lax.axis_size(name) for name in ("dp", axis)]
    pairs = []
    for at in range(sizes[0]):
        for tile in range(sizes[1]):
            other = partner_of(tile, sizes[1], phase)
            to = (at ^ 1 if other == tile else at) * sizes[1] + other
            pairs.append((at * sizes[1] + tile, to))
    return lax.ppermute(x, ("dp", axis), pairs)


def inside(at, size, step):
    return (at + step >= 0) & (at + step < size)


def step_of(at, phase):
    return jnp.where(at % 2 == phase, 1, -1)


def direction(step_x, step_y):
    flat = 3 * (step_x + 1) + step_y + 1
    return flat - jnp.where(flat > 4, 1, 0)


def low_or_high(group, upper):
    wide = group.astype(F32)
    return wide[..., EDGE:, :] if upper else wide[..., :EDGE, :]


def y_edge(bricks, slot, plane, step_y):
    low = low_or_high(bricks[slot, plane, 0:16, :], False)
    high = low_or_high(bricks[slot, plane, PLANE - 16 : PLANE, :], True)
    return jnp.where(step_y > 0, high, low)


def pack_along_y(bricks, lists, box, step_y, send):
    number = direction(0, step_y)
    for entry in range(send):
        listed = lists[entry, number]
        face = y_edge(bricks, jnp.maximum(listed, 0), slice(0, EDGE), step_y)
        face = jnp.where(listed >= 0, face, 0.0).reshape(PLANE, 128)
        box[entry * PLANE : (entry + 1) * PLANE] = face.astype(BF16)
    at = send * PLANE
    for step_x in (-1, 1):
        number = direction(step_x, step_y)
        pieces = []
        for entry in range(send):
            listed = lists[entry, number]
            plane = EDGE - 1 if step_x > 0 else 0
            edge = y_edge(bricks, jnp.maximum(listed, 0), plane, step_y)
            pieces.append(jnp.where(listed >= 0, edge, 0.0))
        box[at : at + send * EDGE] = jnp.concatenate(pieces, axis=0).astype(BF16)
        at += send * EDGE


def pack_along_x(bricks, lists, box, step_x, send):
    number = direction(step_x, 0)
    for entry in range(send):
        listed = lists[entry, number]
        face = bricks[jnp.maximum(listed, 0), jnp.where(step_x > 0, EDGE - 1, 0)]
        box[entry * PLANE : (entry + 1) * PLANE] = jnp.where(listed >= 0, face, jnp.zeros_like(face))


def join_along_x(faces, box, y_boxes, step_x, send):
    at = send * PLANE
    box[:at] = faces[...]
    for y_box in y_boxes:
        first = y_box[send * PLANE : send * PLANE + send * EDGE]
        second = y_box[send * PLANE + send * EDGE : send * PLANE + 2 * send * EDGE]
        box[at : at + send * EDGE] = jnp.where(step_x > 0, second, first)
        at += send * EDGE


def fill_remote(store, base, x_boxes, y_boxes, tiles_x, tiles_y, send):
    store[store.shape[0] - 1] = jnp.zeros(store.shape[1:], BF16)
    for (step_y, in_y), box in zip(tiles_y, y_boxes):
        number = direction(0, step_y)
        for entry in range(send):
            rows = box[entry * PLANE : (entry + 1) * PLANE].astype(F32).reshape(EDGE, EDGE, 128)
            rows = jnp.where(in_y, rows, 0.0)
            twice = jnp.concatenate([rows, rows], axis=1).astype(BF16)
            store[base + number * send + entry, :, 0:16, :] = twice
            store[base + number * send + entry, :, PLANE - 16 : PLANE, :] = twice
    for (step_x, in_x), box in zip(tiles_x, x_boxes):
        number = direction(step_x, 0)
        for entry in range(send):
            face = box[entry * PLANE : (entry + 1) * PLANE]
            face = jnp.where(in_x, face, jnp.zeros_like(face))
            store[base + number * send + entry, 0] = face
            store[base + number * send + entry, EDGE - 1] = face
        at = send * PLANE
        for step_y, in_y in tiles_y:
            number = direction(step_x, step_y)
            edges = jnp.where(in_x & in_y, box[at : at + send * EDGE].astype(F32), 0.0)
            at += send * EDGE
            for entry in range(send):
                rows = edges[entry * EDGE : (entry + 1) * EDGE]
                twice = jnp.concatenate([rows, rows], axis=0).astype(BF16)
                for plane in (0, EDGE - 1):
                    store[base + number * send + entry, plane, 0:16, :] = twice
                    store[base + number * send + entry, plane, PLANE - 16 : PLANE, :] = twice


def view_of(store, entry, off_x, source):
    middle = store[entry(off_x, 0), source]
    before = low_or_high(store[entry(off_x, -1), source, PLANE - 16 : PLANE, :], True)
    after = low_or_high(store[entry(off_x, 1), source, 0:16, :], False)
    wide = middle.astype(F32)
    axis = wide.ndim - 2
    left = jnp.concatenate([before, wide[..., : PLANE - EDGE, :]], axis=axis).astype(BF16)
    right = jnp.concatenate([wide[..., EDGE:, :], after], axis=axis).astype(BF16)
    return jnp.concatenate([left, middle, right], axis=axis + 1)


def fill_views(views, store, entry):
    views[0] = view_of(store, entry, -1, EDGE - 1)
    views[1 : EDGE + 1] = view_of(store, entry, 0, slice(0, EDGE))
    views[EDGE + 1] = view_of(store, entry, 1, 0)


def lookup(table, slot, first, last, zero_at):
    def entry(off_x, off_y):
        listed = table[slot, 9 * (off_x + 1) + 3 * (off_y + 1) + 1]
        return jnp.where((listed >= first) & (listed < last), listed - first, zero_at)

    return entry


def lhs_of(views):
    return jnp.concatenate(
        [views[dx : dx + EDGE].reshape(EDGE * PLANE, 384) for dx in range(3)], axis=1
    )


def shift_rows(wide, step):
    row = lax.broadcasted_iota(jnp.int32, wide.shape, 1)
    moved = pltpu.roll(wide, (-step) % EDGE, 1)
    return jnp.where(row == (EDGE - 1 if step > 0 else 0), 0.0, moved)


def join_taps(parts):
    shape = (parts.shape[0] // EDGE, EDGE, 128)
    blocks = [parts[:, 128 * dz : 128 * dz + 128].reshape(shape) for dz in range(3)]
    return blocks[1] + shift_rows(blocks[0], -1) + shift_rows(blocks[2], 1)


def tiles_here(counts):
    out = []
    for name, size in zip(("gx", "gy"), counts):
        at = lax.axis_index(name)
        steps = [step_of(at, phase) for phase in swap_phases(size)]
        out.append([(step, inside(at, size, step)) for step in steps])
    return out


def pack_all(bricks, lists, x_boxes, y_boxes, counts, send):
    tiles_x, tiles_y = tiles_here(counts)
    for (step_y, _), box in zip(tiles_y, y_boxes):
        pack_along_y(bricks, lists, box, step_y, send)
    for (step_x, _), box in zip(tiles_x, x_boxes):
        pack_along_x(bricks, lists, box, step_x, send)


def start_kernel(counts, send, lists_hbm, bricks_hbm, bricks, *rest):
    boxes, (lists, sems) = rest[:-2], rest[-2:]
    copies = [
        pltpu.make_async_copy(bricks_hbm, bricks, sems.at[0]),
        pltpu.make_async_copy(lists_hbm, lists, sems.at[1]),
    ]
    for copy in copies:
        copy.start()
    for copy in copies:
        copy.wait()
    number_x = len(swap_phases(counts[0]))
    pack_all(bricks, lists, boxes[:number_x], boxes[number_x:], counts, send)


def join_kernel(counts, send, *rest):
    tiles_x, tiles_y = tiles_here(counts)
    number_x, number_y = len(tiles_x), len(tiles_y)
    faces, y_boxes, x_boxes = rest[:number_x], rest[number_x : number_x + number_y], rest[number_x + number_y :]
    for (step_x, _), face, box in zip(tiles_x, faces, x_boxes):
        join_along_x(face, box, y_boxes, step_x, send)


def layout_kernel(table, bricks, weight, forward, views, preact, store):
    slots = bricks.shape[0]
    for tap in range(27):
        far, near = tap // 3 * 128, tap % 3 * 128
        forward[far : far + 128, near : near + 128] = weight[tap]
    store[0:slots] = bricks[...]
    store[slots] = jnp.zeros(store.shape[1:], BF16)
    for slot in range(slots):
        fill_views(views.at[slot], store, lookup(table, slot, 0, slots, slots))
    own_products(views, forward, preact, range(slots // 2))


def own_products(views, taps, preact, which):
    for slot in which:
        parts = jnp.dot(lhs_of(views.at[slot]), taps[...], preferred_element_type=F32)
        preact[slot] = join_taps(parts).reshape(EDGE, EDGE, EDGE, 128)


def own_kernel(views, taps, begun, preact):
    own_products(views, taps, preact, range(views.shape[0] // 2, views.shape[0]))


def add_remote(views, store, table, send, sides=None):
    slots = views.shape[0]
    nothing = jnp.zeros((EDGE, EDGE, 128), F32)
    for slot in range(slots):
        rows = slice(slot * PLANE, (slot + 1) * PLANE)
        entry = lookup(table, slot, slots, slots + 8 * send, store.shape[0] - 1)
        for side, off_x, source, target in ((0, -1, EDGE - 1, 0), (1, 1, 0, EDGE + 1)):
            plane = view_of(store, entry, off_x, source)
            if sides is not None:
                sides[side, rows] = plane
            views[slot, target] = views[slot, target] + plane
        for side, off_y, base, lanes in ((2, -1, 0, 0), (3, 1, PLANE - 16, 256)):
            group = slice(PLANE - 16, PLANE) if off_y < 0 else slice(0, 16)
            edge = low_or_high(store[entry(0, off_y), :, group, :], off_y < 0)
            padded = jnp.concatenate([nothing[:1], edge, nothing[:1]], axis=0)
            for dx in range(3 if sides is not None else 0):
                sides[side, rows, 128 * dx : 128 * dx + 128] = (
                    padded[dx : dx + EDGE].reshape(PLANE, 128).astype(BF16)
                )
            both = [edge, nothing] if off_y < 0 else [nothing, edge]
            wide = jnp.concatenate(both, axis=1).astype(BF16)
            at = (slot, slice(1, EDGE + 1), slice(base, base + 16), slice(lanes, lanes + 128))
            views[at] = views[at] + wide


def forward_kernel(counts, send, factor, table, lists, own_views, own_preact, cotangent, taps, *rest):
    tiles_x, tiles_y = tiles_here(counts)
    number_x, number_y = len(tiles_x), len(tiles_y)
    x_boxes, y_boxes, rest = rest[:number_x], rest[number_x : number_x + number_y], rest[number_x + number_y :]
    views, preacts, activated, grads, kept_term, sent_term = rest[:6]
    faces_out, boxes_out = rest[6 : 6 + number_x], rest[6 + number_x : 6 + number_x + number_y]
    store, sides = rest[6 + number_x + number_y :]
    core = lax.axis_index("dp") % CORES
    slots = cotangent.shape[0]
    fill_remote(store, 0, x_boxes, y_boxes, tiles_x, tiles_y, send)
    add_remote(views, store, table, send, sides)
    added = []
    for side in range(4):
        if side < 2:
            part = taps[768 * side : 768 * side + 384]
        else:
            dy = 0 if side == 2 else 2
            part = jnp.concatenate(
                [taps[(3 * dx + dy) * 128 : (3 * dx + dy) * 128 + 128] for dx in range(3)], axis=0
            )
        product = join_taps(jnp.dot(sides[side], part, preferred_element_type=F32))
        added.append(product.reshape(slots, EDGE, EDGE, 128))
    for slot in range(slots):
        preacts[slot, 0] = preacts[slot, 0] + added[0][slot]
        preacts[slot, EDGE - 1] = preacts[slot, EDGE - 1] + added[1][slot]
        preacts[slot, :, 0] = preacts[slot, :, 0] + added[2][slot]
        preacts[slot, :, EDGE - 1] = preacts[slot, :, EDGE - 1] + added[3][slot]
        preact = preacts[slot].reshape(PLANE, EDGE, 128)
        sigmoid = jax.nn.sigmoid(preact)
        activated[slot] = (preact * sigmoid).reshape(EDGE, PLANE, 128).astype(BF16)
        slope = sigmoid * (1.0 + preact * (1.0 - sigmoid))
        wide = cotangent[slot].astype(F32).reshape(PLANE, EDGE, 128) * slope
        wide = jnp.where(table[slot, 13] >= 0, wide, 0.0)
        grads[slot] = wide.reshape(EDGE, PLANE, 128).astype(BF16)
    pack_all(grads, lists, faces_out, boxes_out, counts, send)
    total = None
    for slot in range(slots):
        grad = grads[slot].astype(F32).reshape(PLANE, EDGE, 128)
        shifted = [shift_rows(grad, 1), grad, shift_rows(grad, -1)]
        rhs = jnp.concatenate([s.reshape(EDGE * PLANE, 128) for s in shifted], axis=1).astype(BF16)
        term = lax.dot_general(
            lhs_of(views.at[slot]), rhs, (((0,), (0,)), ((), ())), preferred_element_type=F32
        )
        total = term if total is None else total + term
    half = 128 // CORES
    for tap in range(27):
        far, near = tap // 3 * 128, tap % 3 * 128
        block = total[far : far + 128, near : near + 128] * factor
        first, second = block[:half], block[half:]
        rows = slice(tap * half, (tap + 1) * half)
        kept_term[rows] = jnp.where(core == 0, first, second)
        sent_term[rows] = jnp.where(core == 0, second, first).astype(BF16)
    for term in (kept_term, sent_term):
        if term.shape[0] > 27 * half:
            term[27 * half :] = jnp.zeros((term.shape[0] - 27 * half, 128), term.dtype)


def back_layout_kernel(table, bricks, weight, backward, views, store):
    slots = bricks.shape[0]
    for tap in range(27):
        far, near = tap // 3 * 128, tap % 3 * 128
        backward[far : far + 128, near : near + 128] = weight[26 - tap].T
    store[0:slots] = bricks[...]
    store[slots] = jnp.zeros(store.shape[1:], BF16)
    for slot in range(slots):
        fill_views(views.at[slot], store, lookup(table, slot, 0, slots, slots))


def backward_kernel(counts, send, table, own_views, taps, *rest):
    tiles_x, tiles_y = tiles_here(counts)
    x_boxes, y_boxes = rest[: len(tiles_x)], rest[len(tiles_x) : len(tiles_x) + len(tiles_y)]
    views, result, ready, store = rest[-4:]
    fill_remote(store, 0, x_boxes, y_boxes, tiles_x, tiles_y, send)
    add_remote(views, store, table, send)
    for slot in range(views.shape[0]):
        parts = jnp.dot(lhs_of(views.at[slot]), taps[...], preferred_element_type=F32)
        result[slot] = join_taps(parts).reshape(EDGE, PLANE, 128).astype(BF16)
    ready[...] = jnp.zeros(ready.shape, F32)


VMEM = pl.BlockSpec(memory_space=pltpu.VMEM)
SMEM = pl.BlockSpec(memory_space=pltpu.SMEM)
ANY = pl.BlockSpec(memory_space=pl.ANY)
HBM = pl.BlockSpec(memory_space=pltpu.HBM)
PARAMS = pltpu.CompilerParams(vmem_limit_bytes=VMEM_BYTES)


def run(kernel, out_shape, ins, outs, scratch=(), aliases=None, micros=1.0):
    cost = pl.CostEstimate(flops=int(micros * 1e9), bytes_accessed=2**16, transcendentals=0)
    return pl.pallas_call(
        kernel,
        out_shape=out_shape,
        in_specs=ins,
        out_specs=outs,
        scratch_shapes=list(scratch),
        input_output_aliases=aliases or {},
        compiler_params=PARAMS,
        cost_estimate=cost,
    )


class Groups:
    def __init__(self):
        self.sizes = tuple(lax.axis_size(name) for name in ("dp", "gx", "gy"))
        dp, gx, gy = self.sizes
        self.plane, self.line = dp // CORES * gy, gx
        self.turned = self.plane == self.line
        at = lax.axis_index("dp")
        in_plane = at // CORES * gy + lax.axis_index("gy")
        self.core = at % CORES
        if self.turned:
            first = jnp.where(self.core == 0, in_plane, lax.axis_index("gx"))
        else:
            first = in_plane
        self.mine = first.astype(jnp.int32)

    def pairs(self, place):
        dp, gx, gy = self.sizes
        out = []
        for a in range(dp):
            for b in range(gx):
                for c in range(gy):
                    to = place(a, b, c)
                    out.append(((a * gx + b) * gy + c, (to[0] * gx + to[1]) * gy + to[2]))
        return out

    def swap(self, x, stage, mask):
        gy = self.sizes[2]

        def place(a, b, c):
            if self.turned and a % CORES == 1:
                plane = stage == 1
            else:
                plane = stage == 0
            if plane:
                return a ^ (mask // gy * CORES), b, c ^ (mask % gy)
            return a, b ^ mask, c

        return lax.ppermute(x, ("dp", "gx", "gy"), self.pairs(place))

    def swaps(self, boxes, stage):
        return [self.swap(box, stage, len(boxes) - at) for at, box in enumerate(boxes)]

    def swap_cores(self, x):
        return lax.ppermute(x, ("dp", "gx", "gy"), self.pairs(lambda a, b, c: (a ^ 1, b, c)))


def tree_sum(terms):
    while len(terms) > 1:
        terms = [a + b for a, b in zip(terms[::2], terms[1::2])]
    return terms[0]


def share_kernel(mine, kept, arrived, own, *boxes):
    own[...] = kept[mine[0]] + arrived[mine[0]].astype(F32)
    for mask, box in enumerate(reversed(boxes), 1):
        at = mine[0] ^ mask
        box[...] = (kept[at] + arrived[at].astype(F32)).astype(BF16)


def first_sum_kernel(boxes, own, *rest):
    total = own[...]
    for box in rest[:boxes]:
        total = total + box[...].astype(F32)
    rest[-1][...] = total.astype(BF16)


def second_sum_kernel(*rest):
    terms = [box[...].astype(F32) for box in rest[-3::-1]]
    rest[-1][...] = tree_sum(terms).astype(BF16)


def gather_kernel(mine, *rest):
    for mask, box in enumerate(rest[-2::-1]):
        rest[-1][mine[0] ^ mask] = box[...]


def spread_kernel(at, half, *rest):
    out, wide, sem = rest[-3:]
    wide[...] = half[0 : wide.shape[0] * wide.shape[1]].astype(F32).reshape(wide.shape)
    copy = pltpu.make_async_copy(wide, out.at[:, at[0]], sem)
    copy.start()
    copy.wait()


def summed_everywhere(groups, kept, sent, early, late):
    group, line = groups.plane, groups.line
    rows = kept.shape[0] // group
    shares = (group, rows, 128)
    share_type = jax.ShapeDtypeStruct((rows, 128), BF16)
    mine = groups.mine.reshape(1)
    arrived = groups.swap_cores(sent)
    own, *boxes = run(
        share_kernel,
        [jax.ShapeDtypeStruct((rows, 128), F32)] + [share_type] * (group - 1),
        [SMEM, VMEM, VMEM],
        [VMEM] * group,
    )(mine, kept.reshape(shares), arrived.reshape(shares))
    boxes = groups.swaps(boxes, 0)
    first_sum = functools.partial(first_sum_kernel, group - 1)
    rounded = run(first_sum, share_type, [VMEM] * group + [ANY] * len(early), VMEM)(
        own, *boxes, *early
    )
    boxes = groups.swaps([rounded] * (line - 1), 1) + [rounded]
    rounded = run(second_sum_kernel, share_type, [VMEM] * line + [ANY], VMEM)(*boxes, late)
    boxes = groups.swaps([rounded] * (group - 1), 0) + [rounded]
    half = run(
        gather_kernel, jax.ShapeDtypeStruct(shares, BF16), [SMEM] + [VMEM] * group, VMEM
    )(mine, *boxes).reshape(kept.shape)
    other = groups.swap_cores(half)
    rows = 128 // CORES
    out_type = jax.ShapeDtypeStruct((27, CORES, rows, 128), F32)
    scratch = [pltpu.VMEM((27, rows, 128), F32), pltpu.SemaphoreType.DMA]
    core = groups.core.astype(jnp.int32).reshape(1)
    out = run(spread_kernel, out_type, [SMEM, VMEM], ANY, scratch)(core, half)
    return run(spread_kernel, out_type, [SMEM, VMEM, ANY], ANY, scratch, aliases={2: 0})(1 - core, other, out)


def body(features, weight, cotangent, neighbours, send_slots):
    slots, _, channels = features.shape[3:]
    send = send_slots.shape[-1]
    counts = (lax.axis_size("gx"), lax.axis_size("gy"))
    devices = lax.axis_size("dp") * counts[0] * counts[1]
    bricks = features.reshape(slots, EDGE, PLANE, channels)
    cot = cotangent.reshape(slots, EDGE, PLANE, channels)
    blocks = weight.reshape(27, channels, channels)
    table = neighbours.reshape(slots, 27)
    lists = send_slots.reshape(8, send).T
    factor = 1.0 / math.sqrt(float(devices * slots * EDGE * PLANE))
    phases_x, phases_y = swap_phases(counts[0]), swap_phases(counts[1])
    number_x, number_y = len(phases_x), len(phases_y)
    y_type = jax.ShapeDtypeStruct((send * (PLANE + 2 * EDGE), 128), BF16)
    x_type = jax.ShapeDtypeStruct((send * (PLANE + number_y * EDGE), 128), BF16)
    bricks_type = jax.ShapeDtypeStruct(bricks.shape, BF16)
    views_type = jax.ShapeDtypeStruct((slots, EDGE + 2, PLANE, 384), BF16)
    taps_type = jax.ShapeDtypeStruct((1152, 384), BF16)
    preact_type = jax.ShapeDtypeStruct((slots, EDGE, EDGE, EDGE, 128), F32)
    groups = Groups()
    block = 16 * groups.plane
    half_shape = (-(-27 * channels // CORES // block) * block, channels)

    def swapped(boxes, axis, phases):
        return [swap(box, axis, phase) for box, phase in zip(boxes, phases)]

    def store_of(entries):
        return pltpu.VMEM((entries, EDGE, PLANE, 128), BF16)

    face_type = jax.ShapeDtypeStruct((send * PLANE, 128), BF16)
    join = run(
        functools.partial(join_kernel, counts, send),
        [x_type] * number_x,
        [VMEM] * (number_x + number_y),
        [VMEM] * number_x,
    )

    bricks, *boxes = run(
        functools.partial(start_kernel, counts, send),
        [bricks_type] + [face_type] * number_x + [y_type] * number_y,
        [HBM, HBM],
        [VMEM] * (1 + number_x + number_y),
        [pltpu.SMEM((send, 8), jnp.int32), pltpu.SemaphoreType.DMA((2,))],
    )(*[pltpu.with_memory_space_constraint(x, pltpu.HBM) for x in (lists, bricks)])
    faces, y_boxes = boxes[:number_x], boxes[number_x:]
    y_boxes = swapped(y_boxes, "gy", phases_y)
    taps, views, preacts = run(
        layout_kernel,
        [
            taps_type,
            views_type,
            preact_type,
        ],
        [SMEM, VMEM, VMEM],
        [VMEM] * 3,
        [store_of(slots + 1)],
        micros=2.0,
    )(table, bricks, blocks)
    x_boxes = swapped(join(*faces, *y_boxes), "gx", phases_x)
    preacts = run(own_kernel, preact_type, [VMEM] * 3, VMEM, aliases={2: 0}, micros=4.0)(
        views, taps, preacts
    )
    _, _, activated, grads, kept, sent, *boxes = run(
        functools.partial(forward_kernel, counts, send, factor),
        [
            views_type,
            preact_type,
            bricks_type,
            bricks_type,
            jax.ShapeDtypeStruct(half_shape, F32),
            jax.ShapeDtypeStruct(half_shape, BF16),
        ]
        + [face_type] * number_x
        + [y_type] * number_y,
        [SMEM, SMEM] + [VMEM] * (4 + number_x + number_y),
        [VMEM] * (6 + number_x + number_y),
        [store_of(8 * send + 1), pltpu.VMEM((4, slots * PLANE, 384), BF16)],
        aliases={2: 0, 3: 1},
        micros=5.0,
    )(table, lists, views, preacts, cot, taps, *x_boxes, *y_boxes)
    faces, y_boxes = boxes[:number_x], swapped(boxes[number_x:], "gy", phases_y)
    packed = join(*faces, *y_boxes)
    x_boxes = swapped(packed, "gx", phases_x)
    back_taps, views = run(
        back_layout_kernel, [taps_type, views_type], [SMEM, VMEM, VMEM], [VMEM, VMEM], [store_of(slots + 1)]
    )(table, grads, blocks)
    _, input_grad, ready = run(
        functools.partial(backward_kernel, counts, send),
        [views_type, bricks_type, jax.ShapeDtypeStruct((8, 128), F32)],
        [SMEM, VMEM, VMEM] + [VMEM] * (number_x + number_y),
        [VMEM] * 3,
        [store_of(8 * send + 1)],
        aliases={1: 0},
        micros=5.0,
    )(table, views, back_taps, *x_boxes, *y_boxes)
    weight_grad = summed_everywhere(groups, kept, sent, [packed[-1], views], ready)
    return (
        activated.reshape(features.shape),
        input_grad.reshape(features.shape),
        weight_grad.reshape(weight.shape),
    )


def solution(mesh):
    split = P("dp", "gx", "gy", None, None, None)
    table = P("dp", "gx", "gy", None, None)
    return jax.shard_map(
        body,
        mesh=mesh,
        in_specs=(split, P(), split, table, table),
        out_specs=(split, split, P()),
        check_vma=False,
    )
```

```python
import functools
import math

import jax
import jax.numpy as jnp
from jax import lax
from jax.experimental import pallas as pl
from jax.experimental.pallas import tpu as pltpu
from jax.sharding import PartitionSpec as P

EDGE = 8
PLANE = EDGE * EDGE
VMEM_BYTES = 28 * 2**20
CORES = 2

F32 = jnp.float32
BF16 = jnp.bfloat16


def swap_phases(size):
    return ([0] if size > 1 else []) + ([1] if size > 2 else [])


def partner_of(at, size, phase):
    other = at + 1 if at % 2 == phase else at - 1
    return other if 0 <= other < size else at


def swap(x, axis, phase):
    sizes = [lax.axis_size(name) for name in ("dp", axis)]
    pairs = []
    for at in range(sizes[0]):
        for tile in range(sizes[1]):
            other = partner_of(tile, sizes[1], phase)
            to = (at ^ 1 if other == tile else at) * sizes[1] + other
            pairs.append((at * sizes[1] + tile, to))
    return lax.ppermute(x, ("dp", axis), pairs)


def inside(at, size, step):
    return (at + step >= 0) & (at + step < size)


def step_of(at, phase):
    return jnp.where(at % 2 == phase, 1, -1)


def direction(step_x, step_y):
    flat = 3 * (step_x + 1) + step_y + 1
    return flat - jnp.where(flat > 4, 1, 0)


def low_or_high(group, upper):
    wide = group.astype(F32)
    return wide[..., EDGE:, :] if upper else wide[..., :EDGE, :]


def y_edge(bricks, slot, plane, step_y):
    low = low_or_high(bricks[slot, plane, 0:16, :], False)
    high = low_or_high(bricks[slot, plane, PLANE - 16 : PLANE, :], True)
    return jnp.where(step_y > 0, high, low)


def pack_along_y(bricks, lists, box, step_y, send):
    number = direction(0, step_y)
    for entry in range(send):
        listed = lists[entry, number]
        face = y_edge(bricks, jnp.maximum(listed, 0), slice(0, EDGE), step_y)
        face = jnp.where(listed >= 0, face, 0.0).reshape(PLANE, 128)
        box[entry * PLANE : (entry + 1) * PLANE] = face.astype(BF16)
    at = send * PLANE
    for step_x in (-1, 1):
        number = direction(step_x, step_y)
        pieces = []
        for entry in range(send):
            listed = lists[entry, number]
            plane = EDGE - 1 if step_x > 0 else 0
            edge = y_edge(bricks, jnp.maximum(listed, 0), plane, step_y)
            pieces.append(jnp.where(listed >= 0, edge, 0.0))
        box[at : at + send * EDGE] = jnp.concatenate(pieces, axis=0).astype(BF16)
        at += send * EDGE


def pack_along_x(bricks, lists, box, step_x, send):
    number = direction(step_x, 0)
    for entry in range(send):
        listed = lists[entry, number]
        face = bricks[jnp.maximum(listed, 0), jnp.where(step_x > 0, EDGE - 1, 0)]
        box[entry * PLANE : (entry + 1) * PLANE] = jnp.where(listed >= 0, face, jnp.zeros_like(face))


def join_along_x(faces, box, y_boxes, step_x, send):
    at = send * PLANE
    box[:at] = faces[...]
    for y_box in y_boxes:
        first = y_box[send * PLANE : send * PLANE + send * EDGE]
        second = y_box[send * PLANE + send * EDGE : send * PLANE + 2 * send * EDGE]
        box[at : at + send * EDGE] = jnp.where(step_x > 0, second, first)
        at += send * EDGE


def fill_remote(store, base, x_boxes, y_boxes, tiles_x, tiles_y, send):
    store[store.shape[0] - 1] = jnp.zeros(store.shape[1:], BF16)
    for (step_y, in_y), box in zip(tiles_y, y_boxes):
        number = direction(0, step_y)
        for entry in range(send):
            rows = box[entry * PLANE : (entry + 1) * PLANE].astype(F32).reshape(EDGE, EDGE, 128)
            rows = jnp.where(in_y, rows, 0.0)
            twice = jnp.concatenate([rows, rows], axis=1).astype(BF16)
            store[base + number * send + entry, :, 0:16, :] = twice
            store[base + number * send + entry, :, PLANE - 16 : PLANE, :] = twice
    for (step_x, in_x), box in zip(tiles_x, x_boxes):
        number = direction(step_x, 0)
        for entry in range(send):
            face = box[entry * PLANE : (entry + 1) * PLANE]
            face = jnp.where(in_x, face, jnp.zeros_like(face))
            store[base + number * send + entry, 0] = face
            store[base + number * send + entry, EDGE - 1] = face
        at = send * PLANE
        for step_y, in_y in tiles_y:
            number = direction(step_x, step_y)
            edges = jnp.where(in_x & in_y, box[at : at + send * EDGE].astype(F32), 0.0)
            at += send * EDGE
            for entry in range(send):
                rows = edges[entry * EDGE : (entry + 1) * EDGE]
                twice = jnp.concatenate([rows, rows], axis=0).astype(BF16)
                for plane in (0, EDGE - 1):
                    store[base + number * send + entry, plane, 0:16, :] = twice
                    store[base + number * send + entry, plane, PLANE - 16 : PLANE, :] = twice


def view_of(store, entry, off_x, source):
    middle = store[entry(off_x, 0), source]
    before = low_or_high(store[entry(off_x, -1), source, PLANE - 16 : PLANE, :], True)
    after = low_or_high(store[entry(off_x, 1), source, 0:16, :], False)
    wide = middle.astype(F32)
    axis = wide.ndim - 2
    left = jnp.concatenate([before, wide[..., : PLANE - EDGE, :]], axis=axis).astype(BF16)
    right = jnp.concatenate([wide[..., EDGE:, :], after], axis=axis).astype(BF16)
    return jnp.concatenate([left, middle, right], axis=axis + 1)


def fill_views(views, store, entry):
    views[0] = view_of(store, entry, -1, EDGE - 1)
    views[1 : EDGE + 1] = view_of(store, entry, 0, slice(0, EDGE))
    views[EDGE + 1] = view_of(store, entry, 1, 0)


def lookup(table, slot, first, last, zero_at):
    def entry(off_x, off_y):
        listed = table[slot, 9 * (off_x + 1) + 3 * (off_y + 1) + 1]
        return jnp.where((listed >= first) & (listed < last), listed - first, zero_at)

    return entry


def lhs_of(views):
    return jnp.concatenate(
        [views[dx : dx + EDGE].reshape(EDGE * PLANE, 384) for dx in range(3)], axis=1
    )


def shift_rows(wide, step):
    row = lax.broadcasted_iota(jnp.int32, wide.shape, 1)
    moved = pltpu.roll(wide, (-step) % EDGE, 1)
    return jnp.where(row == (EDGE - 1 if step > 0 else 0), 0.0, moved)


def join_taps(parts):
    shape = (parts.shape[0] // EDGE, EDGE, 128)
    blocks = [parts[:, 128 * dz : 128 * dz + 128].reshape(shape) for dz in range(3)]
    return blocks[1] + shift_rows(blocks[0], -1) + shift_rows(blocks[2], 1)


def tiles_here(counts):
    out = []
    for name, size in zip(("gx", "gy"), counts):
        at = lax.axis_index(name)
        steps = [step_of(at, phase) for phase in swap_phases(size)]
        out.append([(step, inside(at, size, step)) for step in steps])
    return out


def pack_all(bricks, lists, x_boxes, y_boxes, counts, send):
    tiles_x, tiles_y = tiles_here(counts)
    for (step_y, _), box in zip(tiles_y, y_boxes):
        pack_along_y(bricks, lists, box, step_y, send)
    for (step_x, _), box in zip(tiles_x, x_boxes):
        pack_along_x(bricks, lists, box, step_x, send)


def start_kernel(counts, send, lists_hbm, bricks_hbm, bricks, *rest):
    boxes, (lists, sems) = rest[:-2], rest[-2:]
    copies = [
        pltpu.make_async_copy(bricks_hbm, bricks, sems.at[0]),
        pltpu.make_async_copy(lists_hbm, lists, sems.at[1]),
    ]
    for copy in copies:
        copy.start()
    for copy in copies:
        copy.wait()
    number_x = len(swap_phases(counts[0]))
    pack_all(bricks, lists, boxes[:number_x], boxes[number_x:], counts, send)


def join_kernel(counts, send, *rest):
    tiles_x, tiles_y = tiles_here(counts)
    number_x, number_y = len(tiles_x), len(tiles_y)
    faces, y_boxes, x_boxes = rest[:number_x], rest[number_x : number_x + number_y], rest[number_x + number_y :]
    for (step_x, _), face, box in zip(tiles_x, faces, x_boxes):
        join_along_x(face, box, y_boxes, step_x, send)


def layout_kernel(table, bricks, weight, forward, views, preact, store):
    slots = bricks.shape[0]
    for tap in range(27):
        far, near = tap // 3 * 128, tap % 3 * 128
        forward[far : far + 128, near : near + 128] = weight[tap]
    store[0:slots] = bricks[...]
    store[slots] = jnp.zeros(store.shape[1:], BF16)
    for slot in range(slots):
        fill_views(views.at[slot], store, lookup(table, slot, 0, slots, slots))
    own_products(views, forward, preact, range(slots // 2))


def own_products(views, taps, preact, which):
    for slot in which:
        parts = jnp.dot(lhs_of(views.at[slot]), taps[...], preferred_element_type=F32)
        preact[slot] = join_taps(parts).reshape(EDGE, EDGE, EDGE, 128)


def own_kernel(views, taps, begun, preact):
    own_products(views, taps, preact, range(views.shape[0] // 2, views.shape[0]))


def add_remote(views, store, table, send, sides=None):
    slots = views.shape[0]
    nothing = jnp.zeros((EDGE, EDGE, 128), F32)
    for slot in range(slots):
        rows = slice(slot * PLANE, (slot + 1) * PLANE)
        entry = lookup(table, slot, slots, slots + 8 * send, store.shape[0] - 1)
        for side, off_x, source, target in ((0, -1, EDGE - 1, 0), (1, 1, 0, EDGE + 1)):
            plane = view_of(store, entry, off_x, source)
            if sides is not None:
                sides[side, rows] = plane
            views[slot, target] = views[slot, target] + plane
        for side, off_y, base, lanes in ((2, -1, 0, 0), (3, 1, PLANE - 16, 256)):
            group = slice(PLANE - 16, PLANE) if off_y < 0 else slice(0, 16)
            edge = low_or_high(store[entry(0, off_y), :, group, :], off_y < 0)
            padded = jnp.concatenate([nothing[:1], edge, nothing[:1]], axis=0)
            for dx in range(3 if sides is not None else 0):
                sides[side, rows, 128 * dx : 128 * dx + 128] = (
                    padded[dx : dx + EDGE].reshape(PLANE, 128).astype(BF16)
                )
            both = [edge, nothing] if off_y < 0 else [nothing, edge]
            wide = jnp.concatenate(both, axis=1).astype(BF16)
            at = (slot, slice(1, EDGE + 1), slice(base, base + 16), slice(lanes, lanes + 128))
            views[at] = views[at] + wide


def forward_kernel(counts, send, factor, table, lists, own_views, own_preact, cotangent, taps, *rest):
    tiles_x, tiles_y = tiles_here(counts)
    number_x, number_y = len(tiles_x), len(tiles_y)
    x_boxes, y_boxes, rest = rest[:number_x], rest[number_x : number_x + number_y], rest[number_x + number_y :]
    views, preacts, activated, grads, kept_term, sent_term = rest[:6]
    faces_out, boxes_out = rest[6 : 6 + number_x], rest[6 + number_x : 6 + number_x + number_y]
    store, sides = rest[6 + number_x + number_y :]
    core = lax.axis_index("dp") % CORES
    slots = cotangent.shape[0]
    fill_remote(store, 0, x_boxes, y_boxes, tiles_x, tiles_y, send)
    add_remote(views, store, table, send, sides)
    added = []
    for side in range(4):
        if side < 2:
            part = taps[768 * side : 768 * side + 384]
        else:
            dy = 0 if side == 2 else 2
            part = jnp.concatenate(
                [taps[(3 * dx + dy) * 128 : (3 * dx + dy) * 128 + 128] for dx in range(3)], axis=0
            )
        product = join_taps(jnp.dot(sides[side], part, preferred_element_type=F32))
        added.append(product.reshape(slots, EDGE, EDGE, 128))
    for slot in range(slots):
        preacts[slot, 0] = preacts[slot, 0] + added[0][slot]
        preacts[slot, EDGE - 1] = preacts[slot, EDGE - 1] + added[1][slot]
        preacts[slot, :, 0] = preacts[slot, :, 0] + added[2][slot]
        preacts[slot, :, EDGE - 1] = preacts[slot, :, EDGE - 1] + added[3][slot]
        preact = preacts[slot].reshape(PLANE, EDGE, 128)
        sigmoid = jax.nn.sigmoid(preact)
        activated[slot] = (preact * sigmoid).reshape(EDGE, PLANE, 128).astype(BF16)
        slope = sigmoid * (1.0 + preact * (1.0 - sigmoid))
        wide = cotangent[slot].astype(F32).reshape(PLANE, EDGE, 128) * slope
        wide = jnp.where(table[slot, 13] >= 0, wide, 0.0)
        grads[slot] = wide.reshape(EDGE, PLANE, 128).astype(BF16)
    pack_all(grads, lists, faces_out, boxes_out, counts, send)
    total = None
    for slot in range(slots):
        grad = grads[slot].astype(F32).reshape(PLANE, EDGE, 128)
        shifted = [shift_rows(grad, 1), grad, shift_rows(grad, -1)]
        rhs = jnp.concatenate([s.reshape(EDGE * PLANE, 128) for s in shifted], axis=1).astype(BF16)
        term = lax.dot_general(
            lhs_of(views.at[slot]), rhs, (((0,), (0,)), ((), ())), preferred_element_type=F32
        )
        total = term if total is None else total + term
    half = 128 // CORES

    def piece(at):
        far, near, low = at // CORES // 3 * 128, at // CORES % 3 * 128, at % CORES * half
        return total[far + low : far + low + half, near : near + 128] * factor

    for at in range(27):
        first, second = piece(at), piece(27 + at)
        rows = slice(at * half, (at + 1) * half)
        kept_term[rows] = jnp.where(core == 0, first, second)
        sent_term[rows] = jnp.where(core == 0, second, first).astype(BF16)
    for term in (kept_term, sent_term):
        if term.shape[0] > 27 * half:
            term[27 * half :] = jnp.zeros((term.shape[0] - 27 * half, 128), term.dtype)


def back_layout_kernel(table, bricks, weight, backward, views, store):
    slots = bricks.shape[0]
    for tap in range(27):
        far, near = tap // 3 * 128, tap % 3 * 128
        backward[far : far + 128, near : near + 128] = weight[26 - tap].T
    store[0:slots] = bricks[...]
    store[slots] = jnp.zeros(store.shape[1:], BF16)
    for slot in range(slots):
        fill_views(views.at[slot], store, lookup(table, slot, 0, slots, slots))


def backward_kernel(counts, send, table, own_views, taps, *rest):
    tiles_x, tiles_y = tiles_here(counts)
    x_boxes, y_boxes = rest[: len(tiles_x)], rest[len(tiles_x) : len(tiles_x) + len(tiles_y)]
    views, result, ready, store = rest[-4:]
    fill_remote(store, 0, x_boxes, y_boxes, tiles_x, tiles_y, send)
    add_remote(views, store, table, send)
    for slot in range(views.shape[0]):
        parts = jnp.dot(lhs_of(views.at[slot]), taps[...], preferred_element_type=F32)
        result[slot] = join_taps(parts).reshape(EDGE, PLANE, 128).astype(BF16)
    ready[...] = jnp.zeros(ready.shape, F32)


VMEM = pl.BlockSpec(memory_space=pltpu.VMEM)
SMEM = pl.BlockSpec(memory_space=pltpu.SMEM)
ANY = pl.BlockSpec(memory_space=pl.ANY)
HBM = pl.BlockSpec(memory_space=pltpu.HBM)
PARAMS = pltpu.CompilerParams(vmem_limit_bytes=VMEM_BYTES)


def run(kernel, out_shape, ins, outs, scratch=(), aliases=None, micros=1.0):
    cost = pl.CostEstimate(flops=int(micros * 1e9), bytes_accessed=2**16, transcendentals=0)
    return pl.pallas_call(
        kernel,
        out_shape=out_shape,
        in_specs=ins,
        out_specs=outs,
        scratch_shapes=list(scratch),
        input_output_aliases=aliases or {},
        compiler_params=PARAMS,
        cost_estimate=cost,
    )


class Groups:
    def __init__(self):
        self.sizes = tuple(lax.axis_size(name) for name in ("dp", "gx", "gy"))
        dp, gx, gy = self.sizes
        self.plane, self.line = dp // CORES * gy, gx
        self.turned = self.plane == self.line
        at = lax.axis_index("dp")
        in_plane = at // CORES * gy + lax.axis_index("gy")
        self.core = at % CORES
        in_line = lax.axis_index("gx") if self.turned else in_plane
        self.mine = jnp.where(self.core == 0, in_plane, in_line).astype(jnp.int32)
        self.others = jnp.where(self.core == 0, in_line, in_plane).astype(jnp.int32)

    def places(self):
        masks = [0] + list(range(self.plane - 1, 0, -1))
        own = [(self.core, self.mine ^ mask) for mask in masks]
        return own + [(1 - self.core, self.others ^ mask) for mask in masks]

    def pairs(self, place):
        dp, gx, gy = self.sizes
        out = []
        for a in range(dp):
            for b in range(gx):
                for c in range(gy):
                    to = place(a, b, c)
                    out.append(((a * gx + b) * gy + c, (to[0] * gx + to[1]) * gy + to[2]))
        return out

    def swap(self, x, stage, mask):
        gy = self.sizes[2]

        def place(a, b, c):
            if self.turned and a % CORES == 1:
                plane = stage == 1
            else:
                plane = stage == 0
            if plane:
                return a ^ (mask // gy * CORES), b, c ^ (mask % gy)
            return a, b ^ mask, c

        return lax.ppermute(x, ("dp", "gx", "gy"), self.pairs(place))

    def swaps(self, boxes, stage):
        return [self.swap(box, stage, len(boxes) - at) for at, box in enumerate(boxes)]

    def swap_cores(self, x):
        return lax.ppermute(x, ("dp", "gx", "gy"), self.pairs(lambda a, b, c: (a ^ 1, b, c)))


def tree_sum(terms):
    while len(terms) > 1:
        terms = [a + b for a, b in zip(terms[::2], terms[1::2])]
    return terms[0]


def share_kernel(mine, kept, arrived, own, *boxes):
    own[...] = kept[mine[0]] + arrived[mine[0]].astype(F32)
    for mask, box in enumerate(reversed(boxes), 1):
        at = mine[0] ^ mask
        box[...] = (kept[at] + arrived[at].astype(F32)).astype(BF16)


def first_sum_kernel(boxes, own, *rest):
    total = own[...]
    for box in rest[:boxes]:
        total = total + box[...].astype(F32)
    rest[-1][...] = total.astype(BF16)


def second_sum_kernel(*rest):
    terms = [box[...].astype(F32) for box in rest[-3::-1]]
    rest[-1][...] = tree_sum(terms).astype(BF16)


def spread_kernel(count, first, *rest):
    out, wide, sems = rest[-3:]
    places = Groups().places()[first : first + count]
    copies = []
    for number, box in enumerate(rest[:count]):
        wide[number] = box[...].astype(F32)
        place = out.at[places[number]]
        copies.append(pltpu.make_async_copy(wide.at[number], place, sems.at[number]))
        copies[-1].start()
    for copy in copies:
        copy.wait()


def summed_everywhere(groups, kept, sent, early, late):
    group, line = groups.plane, groups.line
    rows = kept.shape[0] // group
    shares = (group, rows, 128)
    share_type = jax.ShapeDtypeStruct((rows, 128), BF16)
    mine = groups.mine.reshape(1)
    arrived = groups.swap_cores(sent)
    own, *boxes = run(
        share_kernel,
        [jax.ShapeDtypeStruct((rows, 128), F32)] + [share_type] * (group - 1),
        [SMEM, VMEM, VMEM],
        [VMEM] * group,
    )(mine, kept.reshape(shares), arrived.reshape(shares))
    boxes = groups.swaps(boxes, 0)
    first_sum = functools.partial(first_sum_kernel, group - 1)
    rounded = run(first_sum, share_type, [VMEM] * group + [ANY] * len(early), VMEM)(
        own, *boxes, *early
    )
    boxes = groups.swaps([rounded] * (line - 1), 1) + [rounded]
    rounded = run(second_sum_kernel, share_type, [VMEM] * line + [ANY], VMEM)(*boxes, late)
    boxes = [rounded] + groups.swaps([rounded] * (group - 1), 0)
    passed = [groups.swap_cores(box) for box in boxes]
    out_type = jax.ShapeDtypeStruct((CORES, group, rows, 128), F32)

    def spread(boxes, first, *out):
        count = len(boxes)
        return run(
            functools.partial(spread_kernel, count, first),
            out_type,
            [VMEM] * count + [ANY] * len(out),
            ANY,
            [pltpu.VMEM((count, rows, 128), F32), pltpu.SemaphoreType.DMA((count,))],
            aliases={count: 0} if out else None,
        )(*boxes, *out)

    out = spread(boxes + passed[:-2], 0)
    out = spread(passed[-2:], len(boxes + passed[:-2]), out)
    return out.reshape(CORES, group * rows, 128)[:, : 27 * 128 // CORES]


def body(features, weight, cotangent, neighbours, send_slots):
    slots, _, channels = features.shape[3:]
    send = send_slots.shape[-1]
    counts = (lax.axis_size("gx"), lax.axis_size("gy"))
    devices = lax.axis_size("dp") * counts[0] * counts[1]
    bricks = features.reshape(slots, EDGE, PLANE, channels)
    cot = cotangent.reshape(slots, EDGE, PLANE, channels)
    blocks = weight.reshape(27, channels, channels)
    table = neighbours.reshape(slots, 27)
    lists = send_slots.reshape(8, send).T
    factor = 1.0 / math.sqrt(float(devices * slots * EDGE * PLANE))
    phases_x, phases_y = swap_phases(counts[0]), swap_phases(counts[1])
    number_x, number_y = len(phases_x), len(phases_y)
    y_type = jax.ShapeDtypeStruct((send * (PLANE + 2 * EDGE), 128), BF16)
    x_type = jax.ShapeDtypeStruct((send * (PLANE + number_y * EDGE), 128), BF16)
    bricks_type = jax.ShapeDtypeStruct(bricks.shape, BF16)
    views_type = jax.ShapeDtypeStruct((slots, EDGE + 2, PLANE, 384), BF16)
    taps_type = jax.ShapeDtypeStruct((1152, 384), BF16)
    preact_type = jax.ShapeDtypeStruct((slots, EDGE, EDGE, EDGE, 128), F32)
    groups = Groups()
    block = 16 * groups.plane
    half_shape = (-(-27 * channels // CORES // block) * block, channels)

    def swapped(boxes, axis, phases):
        return [swap(box, axis, phase) for box, phase in zip(boxes, phases)]

    def store_of(entries):
        return pltpu.VMEM((entries, EDGE, PLANE, 128), BF16)

    face_type = jax.ShapeDtypeStruct((send * PLANE, 128), BF16)
    join = run(
        functools.partial(join_kernel, counts, send),
        [x_type] * number_x,
        [VMEM] * (number_x + number_y),
        [VMEM] * number_x,
    )

    bricks, *boxes = run(
        functools.partial(start_kernel, counts, send),
        [bricks_type] + [face_type] * number_x + [y_type] * number_y,
        [HBM, HBM],
        [VMEM] * (1 + number_x + number_y),
        [pltpu.SMEM((send, 8), jnp.int32), pltpu.SemaphoreType.DMA((2,))],
    )(*[pltpu.with_memory_space_constraint(x, pltpu.HBM) for x in (lists, bricks)])
    faces, y_boxes = boxes[:number_x], boxes[number_x:]
    y_boxes = swapped(y_boxes, "gy", phases_y)
    taps, views, preacts = run(
        layout_kernel,
        [
            taps_type,
            views_type,
            preact_type,
        ],
        [SMEM, VMEM, VMEM],
        [VMEM] * 3,
        [store_of(slots + 1)],
        micros=2.0,
    )(table, bricks, blocks)
    x_boxes = swapped(join(*faces, *y_boxes), "gx", phases_x)
    preacts = run(own_kernel, preact_type, [VMEM] * 3, VMEM, aliases={2: 0}, micros=4.0)(
        views, taps, preacts
    )
    _, _, activated, grads, kept, sent, *boxes = run(
        functools.partial(forward_kernel, counts, send, factor),
        [
            views_type,
            preact_type,
            bricks_type,
            bricks_type,
            jax.ShapeDtypeStruct(half_shape, F32),
            jax.ShapeDtypeStruct(half_shape, BF16),
        ]
        + [face_type] * number_x
        + [y_type] * number_y,
        [SMEM, SMEM] + [VMEM] * (4 + number_x + number_y),
        [VMEM] * (6 + number_x + number_y),
        [store_of(8 * send + 1), pltpu.VMEM((4, slots * PLANE, 384), BF16)],
        aliases={2: 0, 3: 1},
        micros=5.0,
    )(table, lists, views, preacts, cot, taps, *x_boxes, *y_boxes)
    faces, y_boxes = boxes[:number_x], swapped(boxes[number_x:], "gy", phases_y)
    packed = join(*faces, *y_boxes)
    x_boxes = swapped(packed, "gx", phases_x)
    back_taps, views = run(
        back_layout_kernel, [taps_type, views_type], [SMEM, VMEM, VMEM], [VMEM, VMEM], [store_of(slots + 1)]
    )(table, grads, blocks)
    _, input_grad, ready = run(
        functools.partial(backward_kernel, counts, send),
        [views_type, bricks_type, jax.ShapeDtypeStruct((8, 128), F32)],
        [SMEM, VMEM, VMEM] + [VMEM] * (number_x + number_y),
        [VMEM] * 3,
        [store_of(8 * send + 1)],
        aliases={1: 0},
        micros=5.0,
    )(table, views, back_taps, *x_boxes, *y_boxes)
    weight_grad = summed_everywhere(groups, kept, sent, [packed[-1], views], ready)
    return (
        activated.reshape(features.shape),
        input_grad.reshape(features.shape),
        weight_grad.reshape(weight.shape),
    )


def solution(mesh):
    split = P("dp", "gx", "gy", None, None, None)
    table = P("dp", "gx", "gy", None, None)
    return jax.shard_map(
        body,
        mesh=mesh,
        in_specs=(split, P(), split, table, table),
        out_specs=(split, split, P()),
        check_vma=False,
    )
```

```python
import functools
import math

import jax
import jax.numpy as jnp
from jax import lax
from jax.experimental import pallas as pl
from jax.experimental.pallas import tpu as pltpu
from jax.sharding import PartitionSpec as P

EDGE = 8
PLANE = EDGE * EDGE
VMEM_BYTES = 28 * 2**20
CORES = 2

F32 = jnp.float32
BF16 = jnp.bfloat16


def swap_phases(size):
    return ([0] if size > 1 else []) + ([1] if size > 2 else [])


def partner_of(at, size, phase):
    other = at + 1 if at % 2 == phase else at - 1
    return other if 0 <= other < size else at


def swap(x, axis, phase):
    sizes = [lax.axis_size(name) for name in ("dp", axis)]
    pairs = []
    for at in range(sizes[0]):
        for tile in range(sizes[1]):
            other = partner_of(tile, sizes[1], phase)
            to = (at ^ 1 if other == tile else at) * sizes[1] + other
            pairs.append((at * sizes[1] + tile, to))
    return lax.ppermute(x, ("dp", axis), pairs)


def inside(at, size, step):
    return (at + step >= 0) & (at + step < size)


def step_of(at, phase):
    return jnp.where(at % 2 == phase, 1, -1)


def direction(step_x, step_y):
    flat = 3 * (step_x + 1) + step_y + 1
    return flat - jnp.where(flat > 4, 1, 0)


def low_or_high(group, upper):
    wide = group.astype(F32)
    return wide[..., EDGE:, :] if upper else wide[..., :EDGE, :]


def y_edge(bricks, slot, plane, step_y):
    low = low_or_high(bricks[slot, plane, 0:16, :], False)
    high = low_or_high(bricks[slot, plane, PLANE - 16 : PLANE, :], True)
    return jnp.where(step_y > 0, high, low)


def pack_along_y(bricks, lists, box, step_y, send):
    number = direction(0, step_y)
    for entry in range(send):
        listed = lists[entry, number]
        face = y_edge(bricks, jnp.maximum(listed, 0), slice(0, EDGE), step_y)
        face = jnp.where(listed >= 0, face, 0.0).reshape(PLANE, 128)
        box[entry * PLANE : (entry + 1) * PLANE] = face.astype(BF16)
    at = send * PLANE
    for step_x in (-1, 1):
        number = direction(step_x, step_y)
        pieces = []
        for entry in range(send):
            listed = lists[entry, number]
            plane = EDGE - 1 if step_x > 0 else 0
            edge = y_edge(bricks, jnp.maximum(listed, 0), plane, step_y)
            pieces.append(jnp.where(listed >= 0, edge, 0.0))
        box[at : at + send * EDGE] = jnp.concatenate(pieces, axis=0).astype(BF16)
        at += send * EDGE


def pack_along_x(bricks, lists, box, step_x, send):
    number = direction(step_x, 0)
    for entry in range(send):
        listed = lists[entry, number]
        face = bricks[jnp.maximum(listed, 0), jnp.where(step_x > 0, EDGE - 1, 0)]
        box[entry * PLANE : (entry + 1) * PLANE] = jnp.where(listed >= 0, face, jnp.zeros_like(face))


def join_along_x(faces, box, y_boxes, step_x, send):
    at = send * PLANE
    box[:at] = faces[...]
    for y_box in y_boxes:
        first = y_box[send * PLANE : send * PLANE + send * EDGE]
        second = y_box[send * PLANE + send * EDGE : send * PLANE + 2 * send * EDGE]
        box[at : at + send * EDGE] = jnp.where(step_x > 0, second, first)
        at += send * EDGE


def fill_remote(store, base, x_boxes, y_boxes, tiles_x, tiles_y, send):
    store[store.shape[0] - 1] = jnp.zeros(store.shape[1:], BF16)
    for (step_y, in_y), box in zip(tiles_y, y_boxes):
        number = direction(0, step_y)
        for entry in range(send):
            rows = box[entry * PLANE : (entry + 1) * PLANE].astype(F32).reshape(EDGE, EDGE, 128)
            rows = jnp.where(in_y, rows, 0.0)
            twice = jnp.concatenate([rows, rows], axis=1).astype(BF16)
            store[base + number * send + entry, :, 0:16, :] = twice
            store[base + number * send + entry, :, PLANE - 16 : PLANE, :] = twice
    for (step_x, in_x), box in zip(tiles_x, x_boxes):
        number = direction(step_x, 0)
        for entry in range(send):
            face = box[entry * PLANE : (entry + 1) * PLANE]
            face = jnp.where(in_x, face, jnp.zeros_like(face))
            store[base + number * send + entry, 0] = face
            store[base + number * send + entry, EDGE - 1] = face
        at = send * PLANE
        for step_y, in_y in tiles_y:
            number = direction(step_x, step_y)
            edges = jnp.where(in_x & in_y, box[at : at + send * EDGE].astype(F32), 0.0)
            at += send * EDGE
            for entry in range(send):
                rows = edges[entry * EDGE : (entry + 1) * EDGE]
                twice = jnp.concatenate([rows, rows], axis=0).astype(BF16)
                for plane in (0, EDGE - 1):
                    store[base + number * send + entry, plane, 0:16, :] = twice
                    store[base + number * send + entry, plane, PLANE - 16 : PLANE, :] = twice


def view_of(store, entry, off_x, source):
    middle = store[entry(off_x, 0), source]
    before = low_or_high(store[entry(off_x, -1), source, PLANE - 16 : PLANE, :], True)
    after = low_or_high(store[entry(off_x, 1), source, 0:16, :], False)
    wide = middle.astype(F32)
    axis = wide.ndim - 2
    left = jnp.concatenate([before, wide[..., : PLANE - EDGE, :]], axis=axis).astype(BF16)
    right = jnp.concatenate([wide[..., EDGE:, :], after], axis=axis).astype(BF16)
    return jnp.concatenate([left, middle, right], axis=axis + 1)


def fill_views(views, store, entry):
    views[0] = view_of(store, entry, -1, EDGE - 1)
    views[1 : EDGE + 1] = view_of(store, entry, 0, slice(0, EDGE))
    views[EDGE + 1] = view_of(store, entry, 1, 0)


def lookup(table, slot, first, last, zero_at):
    def entry(off_x, off_y):
        listed = table[slot, 9 * (off_x + 1) + 3 * (off_y + 1) + 1]
        return jnp.where((listed >= first) & (listed < last), listed - first, zero_at)

    return entry


def lhs_of(views):
    return jnp.concatenate(
        [views[dx : dx + EDGE].reshape(EDGE * PLANE, 384) for dx in range(3)], axis=1
    )


def shift_rows(wide, step):
    row = lax.broadcasted_iota(jnp.int32, wide.shape, 1)
    moved = pltpu.roll(wide, (-step) % EDGE, 1)
    return jnp.where(row == (EDGE - 1 if step > 0 else 0), 0.0, moved)


def join_taps(parts):
    shape = (parts.shape[0] // EDGE, EDGE, 128)
    blocks = [parts[:, 128 * dz : 128 * dz + 128].reshape(shape) for dz in range(3)]
    return blocks[1] + shift_rows(blocks[0], -1) + shift_rows(blocks[2], 1)


def tiles_here(counts):
    out = []
    for name, size in zip(("gx", "gy"), counts):
        at = lax.axis_index(name)
        steps = [step_of(at, phase) for phase in swap_phases(size)]
        out.append([(step, inside(at, size, step)) for step in steps])
    return out


def pack_all(bricks, lists, x_boxes, y_boxes, counts, send):
    tiles_x, tiles_y = tiles_here(counts)
    for (step_y, _), box in zip(tiles_y, y_boxes):
        pack_along_y(bricks, lists, box, step_y, send)
    for (step_x, _), box in zip(tiles_x, x_boxes):
        pack_along_x(bricks, lists, box, step_x, send)


def start_kernel(counts, send, lists_hbm, bricks_hbm, bricks, *rest):
    boxes, (lists, sems) = rest[:-2], rest[-2:]
    copies = [
        pltpu.make_async_copy(bricks_hbm, bricks, sems.at[0]),
        pltpu.make_async_copy(lists_hbm, lists, sems.at[1]),
    ]
    for copy in copies:
        copy.start()
    for copy in copies:
        copy.wait()
    number_x = len(swap_phases(counts[0]))
    pack_all(bricks, lists, boxes[:number_x], boxes[number_x:], counts, send)


def join_kernel(counts, send, *rest):
    tiles_x, tiles_y = tiles_here(counts)
    number_x, number_y = len(tiles_x), len(tiles_y)
    faces, y_boxes, x_boxes = rest[:number_x], rest[number_x : number_x + number_y], rest[number_x + number_y :]
    for (step_x, _), face, box in zip(tiles_x, faces, x_boxes):
        join_along_x(face, box, y_boxes, step_x, send)


def layout_kernel(table, bricks, weight, forward, views, preact, store):
    slots = bricks.shape[0]
    for tap in range(27):
        far, near = tap // 3 * 128, tap % 3 * 128
        forward[far : far + 128, near : near + 128] = weight[tap]
    store[0:slots] = bricks[...]
    store[slots] = jnp.zeros(store.shape[1:], BF16)
    for slot in range(slots):
        fill_views(views.at[slot], store, lookup(table, slot, 0, slots, slots))
    own_products(views, forward, preact, range(slots // 2))


def own_products(views, taps, preact, which):
    for slot in which:
        parts = jnp.dot(lhs_of(views.at[slot]), taps[...], preferred_element_type=F32)
        preact[slot] = join_taps(parts).reshape(EDGE, EDGE, EDGE, 128)


def own_kernel(views, taps, begun, preact):
    own_products(views, taps, preact, range(views.shape[0] // 2, views.shape[0]))


def add_remote(views, store, table, send, sides=None):
    slots = views.shape[0]
    nothing = jnp.zeros((EDGE, EDGE, 128), F32)
    for slot in range(slots):
        rows = slice(slot * PLANE, (slot + 1) * PLANE)
        entry = lookup(table, slot, slots, slots + 8 * send, store.shape[0] - 1)
        for side, off_x, source, target in ((0, -1, EDGE - 1, 0), (1, 1, 0, EDGE + 1)):
            plane = view_of(store, entry, off_x, source)
            if sides is not None:
                sides[side, rows] = plane
            views[slot, target] = views[slot, target] + plane
        for side, off_y, base, lanes in ((2, -1, 0, 0), (3, 1, PLANE - 16, 256)):
            group = slice(PLANE - 16, PLANE) if off_y < 0 else slice(0, 16)
            edge = low_or_high(store[entry(0, off_y), :, group, :], off_y < 0)
            padded = jnp.concatenate([nothing[:1], edge, nothing[:1]], axis=0)
            for dx in range(3 if sides is not None else 0):
                sides[side, rows, 128 * dx : 128 * dx + 128] = (
                    padded[dx : dx + EDGE].reshape(PLANE, 128).astype(BF16)
                )
            both = [edge, nothing] if off_y < 0 else [nothing, edge]
            wide = jnp.concatenate(both, axis=1).astype(BF16)
            at = (slot, slice(1, EDGE + 1), slice(base, base + 16), slice(lanes, lanes + 128))
            views[at] = views[at] + wide


def forward_kernel(counts, send, factor, table, lists, own_views, own_preact, cotangent, taps, *rest):
    tiles_x, tiles_y = tiles_here(counts)
    number_x, number_y = len(tiles_x), len(tiles_y)
    x_boxes, y_boxes, rest = rest[:number_x], rest[number_x : number_x + number_y], rest[number_x + number_y :]
    views, preacts, activated, grads, kept_term, sent_term = rest[:6]
    faces_out, boxes_out = rest[6 : 6 + number_x], rest[6 + number_x : 6 + number_x + number_y]
    store, sides = rest[6 + number_x + number_y :]
    core = lax.axis_index("dp") % CORES
    slots = cotangent.shape[0]
    fill_remote(store, 0, x_boxes, y_boxes, tiles_x, tiles_y, send)
    add_remote(views, store, table, send, sides)
    added = []
    for side in range(4):
        if side < 2:
            part = taps[768 * side : 768 * side + 384]
        else:
            dy = 0 if side == 2 else 2
            part = jnp.concatenate(
                [taps[(3 * dx + dy) * 128 : (3 * dx + dy) * 128 + 128] for dx in range(3)], axis=0
            )
        product = join_taps(jnp.dot(sides[side], part, preferred_element_type=F32))
        added.append(product.reshape(slots, EDGE, EDGE, 128))
    for slot in range(slots):
        preacts[slot, 0] = preacts[slot, 0] + added[0][slot]
        preacts[slot, EDGE - 1] = preacts[slot, EDGE - 1] + added[1][slot]
        preacts[slot, :, 0] = preacts[slot, :, 0] + added[2][slot]
        preacts[slot, :, EDGE - 1] = preacts[slot, :, EDGE - 1] + added[3][slot]
        preact = preacts[slot].reshape(PLANE, EDGE, 128)
        sigmoid = jax.nn.sigmoid(preact)
        activated[slot] = (preact * sigmoid).reshape(EDGE, PLANE, 128).astype(BF16)
        slope = sigmoid * (1.0 + preact * (1.0 - sigmoid))
        wide = cotangent[slot].astype(F32).reshape(PLANE, EDGE, 128) * slope
        wide = jnp.where(table[slot, 13] >= 0, wide, 0.0)
        grads[slot] = wide.reshape(EDGE, PLANE, 128).astype(BF16)
    pack_all(grads, lists, faces_out, boxes_out, counts, send)
    parts = []
    for slot in range(slots):
        grad = grads[slot].astype(F32).reshape(PLANE, EDGE, 128)
        shifted = [shift_rows(grad, 1), grad, shift_rows(grad, -1)]
        parts.append(
            jnp.concatenate([part.reshape(EDGE * PLANE, 128) for part in shifted], axis=1).astype(BF16)
        )
    total = lax.dot_general(
        jnp.concatenate([lhs_of(views.at[slot]) for slot in range(slots)], axis=0),
        jnp.concatenate(parts, axis=0),
        (((0,), (0,)), ((), ())),
        preferred_element_type=F32,
    )
    half = 128 // CORES

    def piece(at):
        far, near, low = at // CORES // 3 * 128, at // CORES % 3 * 128, at % CORES * half
        return total[far + low : far + low + half, near : near + 128] * factor

    for at in range(27):
        first, second = piece(at), piece(27 + at)
        rows = slice(at * half, (at + 1) * half)
        kept_term[rows] = jnp.where(core == 0, first, second)
        sent_term[rows] = jnp.where(core == 0, second, first).astype(BF16)
    for term in (kept_term, sent_term):
        if term.shape[0] > 27 * half:
            term[27 * half :] = jnp.zeros((term.shape[0] - 27 * half, 128), term.dtype)


def back_layout_kernel(table, bricks, weight, backward, views, store):
    slots = bricks.shape[0]
    for tap in range(27):
        far, near = tap // 3 * 128, tap % 3 * 128
        backward[far : far + 128, near : near + 128] = weight[26 - tap].T
    store[0:slots] = bricks[...]
    store[slots] = jnp.zeros(store.shape[1:], BF16)
    for slot in range(slots):
        fill_views(views.at[slot], store, lookup(table, slot, 0, slots, slots))


def backward_kernel(counts, send, table, own_views, taps, *rest):
    tiles_x, tiles_y = tiles_here(counts)
    x_boxes, y_boxes = rest[: len(tiles_x)], rest[len(tiles_x) : len(tiles_x) + len(tiles_y)]
    views, result, ready, store = rest[-4:]
    fill_remote(store, 0, x_boxes, y_boxes, tiles_x, tiles_y, send)
    add_remote(views, store, table, send)
    for slot in range(views.shape[0]):
        parts = jnp.dot(lhs_of(views.at[slot]), taps[...], preferred_element_type=F32)
        result[slot] = join_taps(parts).reshape(EDGE, PLANE, 128).astype(BF16)
    ready[...] = jnp.zeros(ready.shape, F32)


VMEM = pl.BlockSpec(memory_space=pltpu.VMEM)
SMEM = pl.BlockSpec(memory_space=pltpu.SMEM)
ANY = pl.BlockSpec(memory_space=pl.ANY)
HBM = pl.BlockSpec(memory_space=pltpu.HBM)
PARAMS = pltpu.CompilerParams(vmem_limit_bytes=VMEM_BYTES)


def run(kernel, out_shape, ins, outs, scratch=(), aliases=None, micros=1.0):
    cost = pl.CostEstimate(flops=int(micros * 1e9), bytes_accessed=2**16, transcendentals=0)
    return pl.pallas_call(
        kernel,
        out_shape=out_shape,
        in_specs=ins,
        out_specs=outs,
        scratch_shapes=list(scratch),
        input_output_aliases=aliases or {},
        compiler_params=PARAMS,
        cost_estimate=cost,
    )


class Groups:
    def __init__(self):
        self.sizes = tuple(lax.axis_size(name) for name in ("dp", "gx", "gy"))
        dp, gx, gy = self.sizes
        self.plane, self.line = dp // CORES * gy, gx
        self.turned = self.plane == self.line
        at = lax.axis_index("dp")
        in_plane = at // CORES * gy + lax.axis_index("gy")
        self.core = at % CORES
        in_line = lax.axis_index("gx") if self.turned else in_plane
        self.mine = jnp.where(self.core == 0, in_plane, in_line).astype(jnp.int32)
        self.others = jnp.where(self.core == 0, in_line, in_plane).astype(jnp.int32)

    def places(self):
        masks = [0] + list(range(self.plane - 1, 0, -1))
        own = [(self.core, self.mine ^ mask) for mask in masks]
        return own + [(1 - self.core, self.others ^ mask) for mask in masks]

    def pairs(self, place):
        dp, gx, gy = self.sizes
        out = []
        for a in range(dp):
            for b in range(gx):
                for c in range(gy):
                    to = place(a, b, c)
                    out.append(((a * gx + b) * gy + c, (to[0] * gx + to[1]) * gy + to[2]))
        return out

    def swap(self, x, stage, mask):
        gy = self.sizes[2]

        def place(a, b, c):
            if self.turned and a % CORES == 1:
                plane = stage == 1
            else:
                plane = stage == 0
            if plane:
                return a ^ (mask // gy * CORES), b, c ^ (mask % gy)
            return a, b ^ mask, c

        return lax.ppermute(x, ("dp", "gx", "gy"), self.pairs(place))

    def swaps(self, boxes, stage):
        return [self.swap(box, stage, len(boxes) - at) for at, box in enumerate(boxes)]

    def swap_cores(self, x):
        return lax.ppermute(x, ("dp", "gx", "gy"), self.pairs(lambda a, b, c: (a ^ 1, b, c)))


def tree_sum(terms):
    while len(terms) > 1:
        terms = [a + b for a, b in zip(terms[::2], terms[1::2])]
    return terms[0]


def share_kernel(mine, kept, arrived, own, *boxes):
    own[...] = kept[mine[0]] + arrived[mine[0]].astype(F32)
    for mask, box in enumerate(reversed(boxes), 1):
        at = mine[0] ^ mask
        box[...] = (kept[at] + arrived[at].astype(F32)).astype(BF16)


def first_sum_kernel(boxes, own, *rest):
    total = own[...]
    for box in rest[:boxes]:
        total = total + box[...].astype(F32)
    rest[-1][...] = total.astype(BF16)


def second_sum_kernel(*rest):
    terms = [box[...].astype(F32) for box in rest[-3::-1]]
    rest[-1][...] = tree_sum(terms).astype(BF16)


def spread_kernel(count, first, *rest):
    out, wide, sems = rest[-3:]
    places = Groups().places()[first : first + count]
    copies = []
    for number, box in enumerate(rest[:count]):
        wide[number] = box[...].astype(F32)
        place = out.at[places[number]]
        copies.append(pltpu.make_async_copy(wide.at[number], place, sems.at[number]))
        copies[-1].start()
    for copy in copies:
        copy.wait()


def summed_everywhere(groups, kept, sent, early, late):
    group, line = groups.plane, groups.line
    rows = kept.shape[0] // group
    shares = (group, rows, 128)
    share_type = jax.ShapeDtypeStruct((rows, 128), BF16)
    mine = groups.mine.reshape(1)
    arrived = groups.swap_cores(sent)
    own, *boxes = run(
        share_kernel,
        [jax.ShapeDtypeStruct((rows, 128), F32)] + [share_type] * (group - 1),
        [SMEM, VMEM, VMEM],
        [VMEM] * group,
    )(mine, kept.reshape(shares), arrived.reshape(shares))
    boxes = groups.swaps(boxes, 0)
    first_sum = functools.partial(first_sum_kernel, group - 1)
    rounded = run(first_sum, share_type, [VMEM] * group + [ANY] * len(early), VMEM)(
        own, *boxes, *early
    )
    boxes = groups.swaps([rounded] * (line - 1), 1) + [rounded]
    rounded = run(second_sum_kernel, share_type, [VMEM] * line + [ANY], VMEM)(*boxes, late)
    boxes = [rounded] + groups.swaps([rounded] * (group - 1), 0)
    passed = [groups.swap_cores(box) for box in boxes]
    out_type = jax.ShapeDtypeStruct((CORES, group, rows, 128), F32)

    def spread(boxes, first, *out):
        count = len(boxes)
        return run(
            functools.partial(spread_kernel, count, first),
            out_type,
            [VMEM] * count + [ANY] * len(out),
            ANY,
            [pltpu.VMEM((count, rows, 128), F32), pltpu.SemaphoreType.DMA((count,))],
            aliases={count: 0} if out else None,
        )(*boxes, *out)

    out = spread(boxes + passed[:-2], 0)
    out = spread(passed[-2:], len(boxes + passed[:-2]), out)
    return out.reshape(CORES, group * rows, 128)[:, : 27 * 128 // CORES]


def body(features, weight, cotangent, neighbours, send_slots):
    slots, _, channels = features.shape[3:]
    send = send_slots.shape[-1]
    counts = (lax.axis_size("gx"), lax.axis_size("gy"))
    devices = lax.axis_size("dp") * counts[0] * counts[1]
    bricks = features.reshape(slots, EDGE, PLANE, channels)
    cot = cotangent.reshape(slots, EDGE, PLANE, channels)
    blocks = weight.reshape(27, channels, channels)
    table = neighbours.reshape(slots, 27)
    lists = send_slots.reshape(8, send).T
    factor = 1.0 / math.sqrt(float(devices * slots * EDGE * PLANE))
    phases_x, phases_y = swap_phases(counts[0]), swap_phases(counts[1])
    number_x, number_y = len(phases_x), len(phases_y)
    y_type = jax.ShapeDtypeStruct((send * (PLANE + 2 * EDGE), 128), BF16)
    x_type = jax.ShapeDtypeStruct((send * (PLANE + number_y * EDGE), 128), BF16)
    bricks_type = jax.ShapeDtypeStruct(bricks.shape, BF16)
    views_type = jax.ShapeDtypeStruct((slots, EDGE + 2, PLANE, 384), BF16)
    taps_type = jax.ShapeDtypeStruct((1152, 384), BF16)
    preact_type = jax.ShapeDtypeStruct((slots, EDGE, EDGE, EDGE, 128), F32)
    groups = Groups()
    block = 16 * groups.plane
    half_shape = (-(-27 * channels // CORES // block) * block, channels)

    def swapped(boxes, axis, phases):
        return [swap(box, axis, phase) for box, phase in zip(boxes, phases)]

    def store_of(entries):
        return pltpu.VMEM((entries, EDGE, PLANE, 128), BF16)

    face_type = jax.ShapeDtypeStruct((send * PLANE, 128), BF16)
    join = run(
        functools.partial(join_kernel, counts, send),
        [x_type] * number_x,
        [VMEM] * (number_x + number_y),
        [VMEM] * number_x,
    )

    bricks, *boxes = run(
        functools.partial(start_kernel, counts, send),
        [bricks_type] + [face_type] * number_x + [y_type] * number_y,
        [HBM, HBM],
        [VMEM] * (1 + number_x + number_y),
        [pltpu.SMEM((send, 8), jnp.int32), pltpu.SemaphoreType.DMA((2,))],
    )(*[pltpu.with_memory_space_constraint(x, pltpu.HBM) for x in (lists, bricks)])
    faces, y_boxes = boxes[:number_x], boxes[number_x:]
    y_boxes = swapped(y_boxes, "gy", phases_y)
    taps, views, preacts = run(
        layout_kernel,
        [
            taps_type,
            views_type,
            preact_type,
        ],
        [SMEM, VMEM, VMEM],
        [VMEM] * 3,
        [store_of(slots + 1)],
        micros=2.0,
    )(table, bricks, blocks)
    x_boxes = swapped(join(*faces, *y_boxes), "gx", phases_x)
    preacts = run(own_kernel, preact_type, [VMEM] * 3, VMEM, aliases={2: 0}, micros=4.0)(
        views, taps, preacts
    )
    _, _, activated, grads, kept, sent, *boxes = run(
        functools.partial(forward_kernel, counts, send, factor),
        [
            views_type,
            preact_type,
            bricks_type,
            bricks_type,
            jax.ShapeDtypeStruct(half_shape, F32),
            jax.ShapeDtypeStruct(half_shape, BF16),
        ]
        + [face_type] * number_x
        + [y_type] * number_y,
        [SMEM, SMEM] + [VMEM] * (4 + number_x + number_y),
        [VMEM] * (6 + number_x + number_y),
        [store_of(8 * send + 1), pltpu.VMEM((4, slots * PLANE, 384), BF16)],
        aliases={2: 0, 3: 1},
        micros=5.0,
    )(table, lists, views, preacts, cot, taps, *x_boxes, *y_boxes)
    faces, y_boxes = boxes[:number_x], swapped(boxes[number_x:], "gy", phases_y)
    packed = join(*faces, *y_boxes)
    x_boxes = swapped(packed, "gx", phases_x)
    back_taps, views = run(
        back_layout_kernel, [taps_type, views_type], [SMEM, VMEM, VMEM], [VMEM, VMEM], [store_of(slots + 1)]
    )(table, grads, blocks)
    _, input_grad, ready = run(
        functools.partial(backward_kernel, counts, send),
        [views_type, bricks_type, jax.ShapeDtypeStruct((8, 128), F32)],
        [SMEM, VMEM, VMEM] + [VMEM] * (number_x + number_y),
        [VMEM] * 3,
        [store_of(8 * send + 1)],
        aliases={1: 0},
        micros=5.0,
    )(table, views, back_taps, *x_boxes, *y_boxes)
    weight_grad = summed_everywhere(groups, kept, sent, [packed[-1], views], ready)
    return (
        activated.reshape(features.shape),
        input_grad.reshape(features.shape),
        weight_grad.reshape(weight.shape),
    )


def solution(mesh):
    split = P("dp", "gx", "gy", None, None, None)
    table = P("dp", "gx", "gy", None, None)
    return jax.shard_map(
        body,
        mesh=mesh,
        in_specs=(split, P(), split, table, table),
        out_specs=(split, split, P()),
        check_vma=False,
    )
```

```python
import functools
import math

import jax
import jax.numpy as jnp
from jax import lax
from jax.experimental import pallas as pl
from jax.experimental.pallas import tpu as pltpu
from jax.sharding import PartitionSpec as P

EDGE = 8
PLANE = EDGE * EDGE
VMEM_BYTES = 28 * 2**20
CORES = 2

F32 = jnp.float32
BF16 = jnp.bfloat16


def swap_phases(size):
    return ([0] if size > 1 else []) + ([1] if size > 2 else [])


def partner_of(at, size, phase):
    other = at + 1 if at % 2 == phase else at - 1
    return other if 0 <= other < size else at


def swap(x, axis, phase):
    sizes = [lax.axis_size(name) for name in ("dp", axis)]
    pairs = []
    for at in range(sizes[0]):
        for tile in range(sizes[1]):
            other = partner_of(tile, sizes[1], phase)
            to = (at ^ 1 if other == tile else at) * sizes[1] + other
            pairs.append((at * sizes[1] + tile, to))
    return lax.ppermute(x, ("dp", axis), pairs)


def inside(at, size, step):
    return (at + step >= 0) & (at + step < size)


def step_of(at, phase):
    return jnp.where(at % 2 == phase, 1, -1)


def direction(step_x, step_y):
    flat = 3 * (step_x + 1) + step_y + 1
    return flat - jnp.where(flat > 4, 1, 0)


def low_or_high(group, upper):
    wide = group.astype(F32)
    return wide[..., EDGE:, :] if upper else wide[..., :EDGE, :]


def y_edge(bricks, slot, plane, step_y):
    low = low_or_high(bricks[slot, plane, 0:16, :], False)
    high = low_or_high(bricks[slot, plane, PLANE - 16 : PLANE, :], True)
    return jnp.where(step_y > 0, high, low)


def pack_along_y(bricks, lists, box, step_y, send):
    number = direction(0, step_y)
    for entry in range(send):
        listed = lists[entry, number]
        face = y_edge(bricks, jnp.maximum(listed, 0), slice(0, EDGE), step_y)
        face = jnp.where(listed >= 0, face, 0.0).reshape(PLANE, 128)
        box[entry * PLANE : (entry + 1) * PLANE] = face.astype(BF16)
    at = send * PLANE
    for step_x in (-1, 1):
        number = direction(step_x, step_y)
        pieces = []
        for entry in range(send):
            listed = lists[entry, number]
            plane = EDGE - 1 if step_x > 0 else 0
            edge = y_edge(bricks, jnp.maximum(listed, 0), plane, step_y)
            pieces.append(jnp.where(listed >= 0, edge, 0.0))
        box[at : at + send * EDGE] = jnp.concatenate(pieces, axis=0).astype(BF16)
        at += send * EDGE


def pack_along_x(bricks, lists, box, step_x, send):
    number = direction(step_x, 0)
    for entry in range(send):
        listed = lists[entry, number]
        face = bricks[jnp.maximum(listed, 0), jnp.where(step_x > 0, EDGE - 1, 0)]
        box[entry * PLANE : (entry + 1) * PLANE] = jnp.where(listed >= 0, face, jnp.zeros_like(face))


def join_along_x(faces, box, y_boxes, step_x, send):
    at = send * PLANE
    box[:at] = faces[...]
    for y_box in y_boxes:
        first = y_box[send * PLANE : send * PLANE + send * EDGE]
        second = y_box[send * PLANE + send * EDGE : send * PLANE + 2 * send * EDGE]
        box[at : at + send * EDGE] = jnp.where(step_x > 0, second, first)
        at += send * EDGE


def fill_remote(store, base, x_boxes, y_boxes, tiles_x, tiles_y, send):
    store[store.shape[0] - 1] = jnp.zeros(store.shape[1:], BF16)
    for (step_y, in_y), box in zip(tiles_y, y_boxes):
        number = direction(0, step_y)
        for entry in range(send):
            rows = box[entry * PLANE : (entry + 1) * PLANE].astype(F32).reshape(EDGE, EDGE, 128)
            rows = jnp.where(in_y, rows, 0.0)
            twice = jnp.concatenate([rows, rows], axis=1).astype(BF16)
            store[base + number * send + entry, :, 0:16, :] = twice
            store[base + number * send + entry, :, PLANE - 16 : PLANE, :] = twice
    for (step_x, in_x), box in zip(tiles_x, x_boxes):
        number = direction(step_x, 0)
        for entry in range(send):
            face = box[entry * PLANE : (entry + 1) * PLANE]
            face = jnp.where(in_x, face, jnp.zeros_like(face))
            store[base + number * send + entry, 0] = face
            store[base + number * send + entry, EDGE - 1] = face
        at = send * PLANE
        for step_y, in_y in tiles_y:
            number = direction(step_x, step_y)
            edges = jnp.where(in_x & in_y, box[at : at + send * EDGE].astype(F32), 0.0)
            at += send * EDGE
            for entry in range(send):
                rows = edges[entry * EDGE : (entry + 1) * EDGE]
                twice = jnp.concatenate([rows, rows], axis=0).astype(BF16)
                for plane in (0, EDGE - 1):
                    store[base + number * send + entry, plane, 0:16, :] = twice
                    store[base + number * send + entry, plane, PLANE - 16 : PLANE, :] = twice


def view_of(store, entry, off_x, source):
    middle = store[entry(off_x, 0), source]
    before = low_or_high(store[entry(off_x, -1), source, PLANE - 16 : PLANE, :], True)
    after = low_or_high(store[entry(off_x, 1), source, 0:16, :], False)
    wide = middle.astype(F32)
    axis = wide.ndim - 2
    left = jnp.concatenate([before, wide[..., : PLANE - EDGE, :]], axis=axis).astype(BF16)
    right = jnp.concatenate([wide[..., EDGE:, :], after], axis=axis).astype(BF16)
    return jnp.concatenate([left, middle, right], axis=axis + 1)


def fill_views(views, store, entry):
    views[0] = view_of(store, entry, -1, EDGE - 1)
    views[1 : EDGE + 1] = view_of(store, entry, 0, slice(0, EDGE))
    views[EDGE + 1] = view_of(store, entry, 1, 0)


def lookup(table, slot, first, last, zero_at):
    def entry(off_x, off_y):
        listed = table[slot, 9 * (off_x + 1) + 3 * (off_y + 1) + 1]
        return jnp.where((listed >= first) & (listed < last), listed - first, zero_at)

    return entry


def lhs_of(views):
    return jnp.concatenate(
        [views[dx : dx + EDGE].reshape(EDGE * PLANE, 384) for dx in range(3)], axis=1
    )


def shift_rows(wide, step):
    row = lax.broadcasted_iota(jnp.int32, wide.shape, 1)
    moved = pltpu.roll(wide, (-step) % EDGE, 1)
    return jnp.where(row == (EDGE - 1 if step > 0 else 0), 0.0, moved)


def join_taps(parts):
    shape = (parts.shape[0] // EDGE, EDGE, 128)
    blocks = [parts[:, 128 * dz : 128 * dz + 128].reshape(shape) for dz in range(3)]
    return blocks[1] + shift_rows(blocks[0], -1) + shift_rows(blocks[2], 1)


def tiles_here(counts):
    out = []
    for name, size in zip(("gx", "gy"), counts):
        at = lax.axis_index(name)
        steps = [step_of(at, phase) for phase in swap_phases(size)]
        out.append([(step, inside(at, size, step)) for step in steps])
    return out


def pack_all(bricks, lists, x_boxes, y_boxes, counts, send):
    tiles_x, tiles_y = tiles_here(counts)
    for (step_y, _), box in zip(tiles_y, y_boxes):
        pack_along_y(bricks, lists, box, step_y, send)
    for (step_x, _), box in zip(tiles_x, x_boxes):
        pack_along_x(bricks, lists, box, step_x, send)


def start_kernel(counts, send, lists_hbm, bricks_hbm, bricks, *rest):
    boxes, (lists, sems) = rest[:-2], rest[-2:]
    copies = [
        pltpu.make_async_copy(bricks_hbm, bricks, sems.at[0]),
        pltpu.make_async_copy(lists_hbm, lists, sems.at[1]),
    ]
    for copy in copies:
        copy.start()
    for copy in copies:
        copy.wait()
    number_x = len(swap_phases(counts[0]))
    pack_all(bricks, lists, boxes[:number_x], boxes[number_x:], counts, send)


def join_kernel(counts, send, *rest):
    tiles_x, tiles_y = tiles_here(counts)
    number_x, number_y = len(tiles_x), len(tiles_y)
    faces, y_boxes, x_boxes = rest[:number_x], rest[number_x : number_x + number_y], rest[number_x + number_y :]
    for (step_x, _), face, box in zip(tiles_x, faces, x_boxes):
        join_along_x(face, box, y_boxes, step_x, send)


def layout_kernel(table, bricks, weight, forward, views, preact, store):
    slots = bricks.shape[0]
    for tap in range(27):
        far, near = tap // 3 * 128, tap % 3 * 128
        forward[far : far + 128, near : near + 128] = weight[tap]
    store[0:slots] = bricks[...]
    store[slots] = jnp.zeros(store.shape[1:], BF16)
    for slot in range(slots):
        fill_views(views.at[slot], store, lookup(table, slot, 0, slots, slots))
    own_products(views, forward, preact, range(slots // 2))


def own_products(views, taps, preact, which):
    for slot in which:
        parts = jnp.dot(lhs_of(views.at[slot]), taps[...], preferred_element_type=F32)
        preact[slot] = join_taps(parts).reshape(EDGE, EDGE, EDGE, 128)


def own_kernel(counts, send, table, own_views, taps, begun, *rest):
    tiles_y = tiles_here(counts)[1]
    y_boxes, (views, preacts, store, sides) = rest[: len(tiles_y)], rest[len(tiles_y) :]
    slots = views.shape[0]
    own_products(views, taps, preacts, range(slots // 2, slots))
    fill_remote(store, 0, [], y_boxes, [], tiles_y, send)
    add_remote(views, store, table, send, sides, "y")
    for side, at in ((0, 0), (1, EDGE - 1)):
        part = jnp.concatenate(
            [taps[(3 * dx + 2 * side) * 128 : (3 * dx + 2 * side) * 128 + 128] for dx in range(3)], axis=0
        )
        product = join_taps(jnp.dot(sides[side], part, preferred_element_type=F32))
        product = product.reshape(slots, EDGE, EDGE, 128)
        for slot in range(slots):
            preacts[slot, :, at] = preacts[slot, :, at] + product[slot]


PLANES = ((0, -1, EDGE - 1, 0), (1, 1, 0, EDGE + 1))
ROWS = ((0, -1, 0, 0), (1, 1, PLANE - 16, 256))


def add_remote(views, store, table, send, sides=None, along="xy"):
    slots = views.shape[0]
    nothing = jnp.zeros((EDGE, EDGE, 128), F32)
    for slot in range(slots):
        rows = slice(slot * PLANE, (slot + 1) * PLANE)
        entry = lookup(table, slot, slots, slots + 8 * send, store.shape[0] - 1)
        for side, off_x, source, target in PLANES if "x" in along else ():
            plane = view_of(store, entry, off_x, source)
            if sides is not None:
                sides[side, rows] = plane
            views[slot, target] = views[slot, target] + plane
        for side, off_y, base, lanes in ROWS if "y" in along else ():
            group = slice(PLANE - 16, PLANE) if off_y < 0 else slice(0, 16)
            edge = low_or_high(store[entry(0, off_y), :, group, :], off_y < 0)
            padded = jnp.concatenate([nothing[:1], edge, nothing[:1]], axis=0)
            for dx in range(3 if sides is not None else 0):
                sides[side, rows, 128 * dx : 128 * dx + 128] = (
                    padded[dx : dx + EDGE].reshape(PLANE, 128).astype(BF16)
                )
            both = [edge, nothing] if off_y < 0 else [nothing, edge]
            wide = jnp.concatenate(both, axis=1).astype(BF16)
            at = (slot, slice(1, EDGE + 1), slice(base, base + 16), slice(lanes, lanes + 128))
            views[at] = views[at] + wide


def forward_kernel(counts, send, factor, table, lists, own_views, own_preact, cotangent, taps, *rest):
    tiles_x, tiles_y = tiles_here(counts)
    number_x, number_y = len(tiles_x), len(tiles_y)
    x_boxes, y_boxes, rest = rest[:number_x], rest[number_x : number_x + number_y], rest[number_x + number_y :]
    views, preacts, activated, grads, kept_term, sent_term = rest[:6]
    faces_out, boxes_out = rest[6 : 6 + number_x], rest[6 + number_x : 6 + number_x + number_y]
    store, sides = rest[6 + number_x + number_y :]
    core = lax.axis_index("dp") % CORES
    slots = cotangent.shape[0]
    fill_remote(store, 0, x_boxes, y_boxes, tiles_x, tiles_y, send)
    add_remote(views, store, table, send, sides, "x")
    added = []
    for side in range(2):
        part = taps[768 * side : 768 * side + 384]
        product = join_taps(jnp.dot(sides[side], part, preferred_element_type=F32))
        added.append(product.reshape(slots, EDGE, EDGE, 128))
    for slot in range(slots):
        preacts[slot, 0] = preacts[slot, 0] + added[0][slot]
        preacts[slot, EDGE - 1] = preacts[slot, EDGE - 1] + added[1][slot]
        preact = preacts[slot].reshape(PLANE, EDGE, 128)
        sigmoid = jax.nn.sigmoid(preact)
        activated[slot] = (preact * sigmoid).reshape(EDGE, PLANE, 128).astype(BF16)
        slope = sigmoid * (1.0 + preact * (1.0 - sigmoid))
        wide = cotangent[slot].astype(F32).reshape(PLANE, EDGE, 128) * slope
        wide = jnp.where(table[slot, 13] >= 0, wide, 0.0)
        grads[slot] = wide.reshape(EDGE, PLANE, 128).astype(BF16)
    pack_all(grads, lists, faces_out, boxes_out, counts, send)
    total = None
    for slot in range(slots):
        grad = grads[slot].astype(F32).reshape(PLANE, EDGE, 128)
        shifted = [shift_rows(grad, 1), grad, shift_rows(grad, -1)]
        rhs = jnp.concatenate([s.reshape(EDGE * PLANE, 128) for s in shifted], axis=1).astype(BF16)
        term = lax.dot_general(
            lhs_of(views.at[slot]), rhs, (((0,), (0,)), ((), ())), preferred_element_type=F32
        )
        total = term if total is None else total + term
    half = 128 // CORES

    def piece(at):
        far, near, low = at // CORES // 3 * 128, at // CORES % 3 * 128, at % CORES * half
        return total[far + low : far + low + half, near : near + 128] * factor

    for at in range(27):
        first, second = piece(at), piece(27 + at)
        rows = slice(at * half, (at + 1) * half)
        kept_term[rows] = jnp.where(core == 0, first, second)
        sent_term[rows] = jnp.where(core == 0, second, first).astype(BF16)
    for term in (kept_term, sent_term):
        if term.shape[0] > 27 * half:
            term[27 * half :] = jnp.zeros((term.shape[0] - 27 * half, 128), term.dtype)


def back_layout_kernel(table, bricks, weight, backward, views, store):
    slots = bricks.shape[0]
    for tap in range(27):
        far, near = tap // 3 * 128, tap % 3 * 128
        backward[far : far + 128, near : near + 128] = weight[26 - tap].T
    store[0:slots] = bricks[...]
    store[slots] = jnp.zeros(store.shape[1:], BF16)
    for slot in range(slots):
        fill_views(views.at[slot], store, lookup(table, slot, 0, slots, slots))


def backward_kernel(counts, send, table, own_views, taps, *rest):
    tiles_x, tiles_y = tiles_here(counts)
    x_boxes, y_boxes = rest[: len(tiles_x)], rest[len(tiles_x) : len(tiles_x) + len(tiles_y)]
    views, result, ready, store = rest[-4:]
    fill_remote(store, 0, x_boxes, y_boxes, tiles_x, tiles_y, send)
    add_remote(views, store, table, send)
    for slot in range(views.shape[0]):
        parts = jnp.dot(lhs_of(views.at[slot]), taps[...], preferred_element_type=F32)
        result[slot] = join_taps(parts).reshape(EDGE, PLANE, 128).astype(BF16)
    ready[...] = jnp.zeros(ready.shape, F32)


VMEM = pl.BlockSpec(memory_space=pltpu.VMEM)
SMEM = pl.BlockSpec(memory_space=pltpu.SMEM)
ANY = pl.BlockSpec(memory_space=pl.ANY)
HBM = pl.BlockSpec(memory_space=pltpu.HBM)
PARAMS = pltpu.CompilerParams(vmem_limit_bytes=VMEM_BYTES)


def run(kernel, out_shape, ins, outs, scratch=(), aliases=None, micros=1.0):
    cost = pl.CostEstimate(flops=int(micros * 1e9), bytes_accessed=2**16, transcendentals=0)
    return pl.pallas_call(
        kernel,
        out_shape=out_shape,
        in_specs=ins,
        out_specs=outs,
        scratch_shapes=list(scratch),
        input_output_aliases=aliases or {},
        compiler_params=PARAMS,
        cost_estimate=cost,
    )


class Groups:
    def __init__(self):
        self.sizes = tuple(lax.axis_size(name) for name in ("dp", "gx", "gy"))
        dp, gx, gy = self.sizes
        self.plane, self.line = dp // CORES * gy, gx
        self.turned = self.plane == self.line
        at = lax.axis_index("dp")
        in_plane = at // CORES * gy + lax.axis_index("gy")
        self.core = at % CORES
        in_line = lax.axis_index("gx") if self.turned else in_plane
        self.mine = jnp.where(self.core == 0, in_plane, in_line).astype(jnp.int32)
        self.others = jnp.where(self.core == 0, in_line, in_plane).astype(jnp.int32)

    def places(self):
        masks = [0] + list(range(self.plane - 1, 0, -1))
        own = [(self.core, self.mine ^ mask) for mask in masks]
        return own + [(1 - self.core, self.others ^ mask) for mask in masks]

    def pairs(self, place):
        dp, gx, gy = self.sizes
        out = []
        for a in range(dp):
            for b in range(gx):
                for c in range(gy):
                    to = place(a, b, c)
                    out.append(((a * gx + b) * gy + c, (to[0] * gx + to[1]) * gy + to[2]))
        return out

    def swap(self, x, stage, mask):
        gy = self.sizes[2]

        def place(a, b, c):
            if self.turned and a % CORES == 1:
                plane = stage == 1
            else:
                plane = stage == 0
            if plane:
                return a ^ (mask // gy * CORES), b, c ^ (mask % gy)
            return a, b ^ mask, c

        return lax.ppermute(x, ("dp", "gx", "gy"), self.pairs(place))

    def swaps(self, boxes, stage):
        return [self.swap(box, stage, len(boxes) - at) for at, box in enumerate(boxes)]

    def swap_cores(self, x):
        return lax.ppermute(x, ("dp", "gx", "gy"), self.pairs(lambda a, b, c: (a ^ 1, b, c)))


def tree_sum(terms):
    while len(terms) > 1:
        terms = [a + b for a, b in zip(terms[::2], terms[1::2])]
    return terms[0]


def share_kernel(mine, kept, arrived, own, *boxes):
    own[...] = kept[mine[0]] + arrived[mine[0]].astype(F32)
    for mask, box in enumerate(reversed(boxes), 1):
        at = mine[0] ^ mask
        box[...] = (kept[at] + arrived[at].astype(F32)).astype(BF16)


def first_sum_kernel(boxes, own, *rest):
    total = own[...]
    for box in rest[:boxes]:
        total = total + box[...].astype(F32)
    rest[-1][...] = total.astype(BF16)


def second_sum_kernel(*rest):
    terms = [box[...].astype(F32) for box in rest[-3::-1]]
    rest[-1][...] = tree_sum(terms).astype(BF16)


def spread_kernel(count, first, *rest):
    out, wide, sems = rest[-3:]
    places = Groups().places()[first : first + count]
    copies = []
    for number, box in enumerate(rest[:count]):
        wide[number] = box[...].astype(F32)
        place = out.at[places[number]]
        copies.append(pltpu.make_async_copy(wide.at[number], place, sems.at[number]))
        copies[-1].start()
    for copy in copies:
        copy.wait()


def summed_everywhere(groups, kept, sent, early, late):
    group, line = groups.plane, groups.line
    rows = kept.shape[0] // group
    shares = (group, rows, 128)
    share_type = jax.ShapeDtypeStruct((rows, 128), BF16)
    mine = groups.mine.reshape(1)
    arrived = groups.swap_cores(sent)
    own, *boxes = run(
        share_kernel,
        [jax.ShapeDtypeStruct((rows, 128), F32)] + [share_type] * (group - 1),
        [SMEM, VMEM, VMEM],
        [VMEM] * group,
    )(mine, kept.reshape(shares), arrived.reshape(shares))
    boxes = groups.swaps(boxes, 0)
    first_sum = functools.partial(first_sum_kernel, group - 1)
    rounded = run(first_sum, share_type, [VMEM] * group + [ANY] * len(early), VMEM)(
        own, *boxes, *early
    )
    boxes = groups.swaps([rounded] * (line - 1), 1) + [rounded]
    rounded = run(second_sum_kernel, share_type, [VMEM] * line + [ANY], VMEM)(*boxes, late)
    boxes = [rounded] + groups.swaps([rounded] * (group - 1), 0)
    passed = [groups.swap_cores(box) for box in boxes]
    out_type = jax.ShapeDtypeStruct((CORES, group, rows, 128), F32)

    def spread(boxes, first, *out):
        count = len(boxes)
        return run(
            functools.partial(spread_kernel, count, first),
            out_type,
            [VMEM] * count + [ANY] * len(out),
            ANY,
            [pltpu.VMEM((count, rows, 128), F32), pltpu.SemaphoreType.DMA((count,))],
            aliases={count: 0} if out else None,
        )(*boxes, *out)

    out = spread(boxes + passed[:-2], 0)
    out = spread(passed[-2:], len(boxes + passed[:-2]), out)
    return out.reshape(CORES, group * rows, 128)[:, : 27 * 128 // CORES]


def body(features, weight, cotangent, neighbours, send_slots):
    slots, _, channels = features.shape[3:]
    send = send_slots.shape[-1]
    counts = (lax.axis_size("gx"), lax.axis_size("gy"))
    devices = lax.axis_size("dp") * counts[0] * counts[1]
    bricks = features.reshape(slots, EDGE, PLANE, channels)
    cot = cotangent.reshape(slots, EDGE, PLANE, channels)
    blocks = weight.reshape(27, channels, channels)
    table = neighbours.reshape(slots, 27)
    lists = send_slots.reshape(8, send).T
    factor = 1.0 / math.sqrt(float(devices * slots * EDGE * PLANE))
    phases_x, phases_y = swap_phases(counts[0]), swap_phases(counts[1])
    number_x, number_y = len(phases_x), len(phases_y)
    y_type = jax.ShapeDtypeStruct((send * (PLANE + 2 * EDGE), 128), BF16)
    x_type = jax.ShapeDtypeStruct((send * (PLANE + number_y * EDGE), 128), BF16)
    bricks_type = jax.ShapeDtypeStruct(bricks.shape, BF16)
    views_type = jax.ShapeDtypeStruct((slots, EDGE + 2, PLANE, 384), BF16)
    taps_type = jax.ShapeDtypeStruct((1152, 384), BF16)
    preact_type = jax.ShapeDtypeStruct((slots, EDGE, EDGE, EDGE, 128), F32)
    groups = Groups()
    block = 16 * groups.plane
    half_shape = (-(-27 * channels // CORES // block) * block, channels)

    def swapped(boxes, axis, phases):
        return [swap(box, axis, phase) for box, phase in zip(boxes, phases)]

    sides_of = pltpu.VMEM((2, slots * PLANE, 384), BF16)

    def store_of(entries):
        return pltpu.VMEM((entries, EDGE, PLANE, 128), BF16)

    face_type = jax.ShapeDtypeStruct((send * PLANE, 128), BF16)
    join = run(
        functools.partial(join_kernel, counts, send),
        [x_type] * number_x,
        [VMEM] * (number_x + number_y),
        [VMEM] * number_x,
    )

    bricks, *boxes = run(
        functools.partial(start_kernel, counts, send),
        [bricks_type] + [face_type] * number_x + [y_type] * number_y,
        [HBM, HBM],
        [VMEM] * (1 + number_x + number_y),
        [pltpu.SMEM((send, 8), jnp.int32), pltpu.SemaphoreType.DMA((2,))],
    )(*[pltpu.with_memory_space_constraint(x, pltpu.HBM) for x in (lists, bricks)])
    faces, y_boxes = boxes[:number_x], boxes[number_x:]
    y_boxes = swapped(y_boxes, "gy", phases_y)
    taps, views, preacts = run(
        layout_kernel,
        [
            taps_type,
            views_type,
            preact_type,
        ],
        [SMEM, VMEM, VMEM],
        [VMEM] * 3,
        [store_of(slots + 1)],
        micros=2.0,
    )(table, bricks, blocks)
    x_boxes = swapped(join(*faces, *y_boxes), "gx", phases_x)
    views, preacts = run(
        functools.partial(own_kernel, counts, send),
        [views_type, preact_type],
        [SMEM] + [VMEM] * (3 + number_y),
        [VMEM, VMEM],
        [store_of(8 * send + 1), sides_of],
        aliases={1: 0, 3: 1},
        micros=4.0,
    )(table, views, taps, preacts, *y_boxes)
    _, _, activated, grads, kept, sent, *boxes = run(
        functools.partial(forward_kernel, counts, send, factor),
        [
            views_type,
            preact_type,
            bricks_type,
            bricks_type,
            jax.ShapeDtypeStruct(half_shape, F32),
            jax.ShapeDtypeStruct(half_shape, BF16),
        ]
        + [face_type] * number_x
        + [y_type] * number_y,
        [SMEM, SMEM] + [VMEM] * (4 + number_x + number_y),
        [VMEM] * (6 + number_x + number_y),
        [store_of(8 * send + 1), sides_of],
        aliases={2: 0, 3: 1},
        micros=5.0,
    )(table, lists, views, preacts, cot, taps, *x_boxes, *y_boxes)
    faces, y_boxes = boxes[:number_x], swapped(boxes[number_x:], "gy", phases_y)
    packed = join(*faces, *y_boxes)
    x_boxes = swapped(packed, "gx", phases_x)
    back_taps, views = run(
        back_layout_kernel, [taps_type, views_type], [SMEM, VMEM, VMEM], [VMEM, VMEM], [store_of(slots + 1)]
    )(table, grads, blocks)
    _, input_grad, ready = run(
        functools.partial(backward_kernel, counts, send),
        [views_type, bricks_type, jax.ShapeDtypeStruct((8, 128), F32)],
        [SMEM, VMEM, VMEM] + [VMEM] * (number_x + number_y),
        [VMEM] * 3,
        [store_of(8 * send + 1)],
        aliases={1: 0},
        micros=5.0,
    )(table, views, back_taps, *x_boxes, *y_boxes)
    weight_grad = summed_everywhere(groups, kept, sent, [packed[-1], views], ready)
    return (
        activated.reshape(features.shape),
        input_grad.reshape(features.shape),
        weight_grad.reshape(weight.shape),
    )


def solution(mesh):
    split = P("dp", "gx", "gy", None, None, None)
    table = P("dp", "gx", "gy", None, None)
    return jax.shard_map(
        body,
        mesh=mesh,
        in_specs=(split, P(), split, table, table),
        out_specs=(split, split, P()),
        check_vma=False,
    )
```

```python
import functools
import math

import jax
import jax.numpy as jnp
from jax import lax
from jax.experimental import pallas as pl
from jax.experimental.pallas import tpu as pltpu
from jax.sharding import PartitionSpec as P

EDGE = 8
PLANE = EDGE * EDGE
VMEM_BYTES = 28 * 2**20
CORES = 2

F32 = jnp.float32
BF16 = jnp.bfloat16


def swap_phases(size):
    return ([0] if size > 1 else []) + ([1] if size > 2 else [])


def partner_of(at, size, phase):
    other = at + 1 if at % 2 == phase else at - 1
    return other if 0 <= other < size else at


def swap(x, axis, phase):
    sizes = [lax.axis_size(name) for name in ("dp", axis)]
    pairs = []
    for at in range(sizes[0]):
        for tile in range(sizes[1]):
            other = partner_of(tile, sizes[1], phase)
            to = (at ^ 1 if other == tile else at) * sizes[1] + other
            pairs.append((at * sizes[1] + tile, to))
    return lax.ppermute(x, ("dp", axis), pairs)


def inside(at, size, step):
    return (at + step >= 0) & (at + step < size)


def step_of(at, phase):
    return jnp.where(at % 2 == phase, 1, -1)


def direction(step_x, step_y):
    flat = 3 * (step_x + 1) + step_y + 1
    return flat - jnp.where(flat > 4, 1, 0)


def low_or_high(group, upper):
    wide = group.astype(F32)
    return wide[..., EDGE:, :] if upper else wide[..., :EDGE, :]


def y_edge(bricks, slot, plane, step_y):
    low = low_or_high(bricks[slot, plane, 0:16, :], False)
    high = low_or_high(bricks[slot, plane, PLANE - 16 : PLANE, :], True)
    return jnp.where(step_y > 0, high, low)


def pack_along_y(bricks, lists, box, step_y, send):
    number = direction(0, step_y)
    for entry in range(send):
        listed = lists[entry, number]
        face = y_edge(bricks, jnp.maximum(listed, 0), slice(0, EDGE), step_y)
        face = jnp.where(listed >= 0, face, 0.0).reshape(PLANE, 128)
        box[entry * PLANE : (entry + 1) * PLANE] = face.astype(BF16)
    at = send * PLANE
    for step_x in (-1, 1):
        number = direction(step_x, step_y)
        pieces = []
        for entry in range(send):
            listed = lists[entry, number]
            plane = EDGE - 1 if step_x > 0 else 0
            edge = y_edge(bricks, jnp.maximum(listed, 0), plane, step_y)
            pieces.append(jnp.where(listed >= 0, edge, 0.0))
        box[at : at + send * EDGE] = jnp.concatenate(pieces, axis=0).astype(BF16)
        at += send * EDGE


def pack_along_x(bricks, lists, box, step_x, send):
    number = direction(step_x, 0)
    for entry in range(send):
        listed = lists[entry, number]
        face = bricks[jnp.maximum(listed, 0), jnp.where(step_x > 0, EDGE - 1, 0)]
        box[entry * PLANE : (entry + 1) * PLANE] = jnp.where(listed >= 0, face, jnp.zeros_like(face))


def join_along_x(faces, box, y_boxes, step_x, send):
    at = send * PLANE
    box[:at] = faces[...]
    for y_box in y_boxes:
        first = y_box[send * PLANE : send * PLANE + send * EDGE]
        second = y_box[send * PLANE + send * EDGE : send * PLANE + 2 * send * EDGE]
        box[at : at + send * EDGE] = jnp.where(step_x > 0, second, first)
        at += send * EDGE


def fill_remote(store, base, x_boxes, y_boxes, tiles_x, tiles_y, send):
    store[store.shape[0] - 1] = jnp.zeros(store.shape[1:], BF16)
    for (step_y, in_y), box in zip(tiles_y, y_boxes):
        number = direction(0, step_y)
        for entry in range(send):
            rows = box[entry * PLANE : (entry + 1) * PLANE].astype(F32).reshape(EDGE, EDGE, 128)
            rows = jnp.where(in_y, rows, 0.0)
            twice = jnp.concatenate([rows, rows], axis=1).astype(BF16)
            store[base + number * send + entry, :, 0:16, :] = twice
            store[base + number * send + entry, :, PLANE - 16 : PLANE, :] = twice
    for (step_x, in_x), box in zip(tiles_x, x_boxes):
        number = direction(step_x, 0)
        for entry in range(send):
            face = box[entry * PLANE : (entry + 1) * PLANE]
            face = jnp.where(in_x, face, jnp.zeros_like(face))
            store[base + number * send + entry, 0] = face
            store[base + number * send + entry, EDGE - 1] = face
        at = send * PLANE
        for step_y, in_y in tiles_y:
            number = direction(step_x, step_y)
            edges = jnp.where(in_x & in_y, box[at : at + send * EDGE].astype(F32), 0.0)
            at += send * EDGE
            for entry in range(send):
                rows = edges[entry * EDGE : (entry + 1) * EDGE]
                twice = jnp.concatenate([rows, rows], axis=0).astype(BF16)
                for plane in (0, EDGE - 1):
                    store[base + number * send + entry, plane, 0:16, :] = twice
                    store[base + number * send + entry, plane, PLANE - 16 : PLANE, :] = twice


def view_of(store, entry, off_x, source):
    middle = store[entry(off_x, 0), source]
    before = low_or_high(store[entry(off_x, -1), source, PLANE - 16 : PLANE, :], True)
    after = low_or_high(store[entry(off_x, 1), source, 0:16, :], False)
    wide = middle.astype(F32)
    axis = wide.ndim - 2
    left = jnp.concatenate([before, wide[..., : PLANE - EDGE, :]], axis=axis).astype(BF16)
    right = jnp.concatenate([wide[..., EDGE:, :], after], axis=axis).astype(BF16)
    return jnp.concatenate([left, middle, right], axis=axis + 1)


def fill_views(views, store, entry):
    views[0] = view_of(store, entry, -1, EDGE - 1)
    views[1 : EDGE + 1] = view_of(store, entry, 0, slice(0, EDGE))
    views[EDGE + 1] = view_of(store, entry, 1, 0)


def lookup(table, slot, first, last, zero_at):
    def entry(off_x, off_y):
        listed = table[slot, 9 * (off_x + 1) + 3 * (off_y + 1) + 1]
        return jnp.where((listed >= first) & (listed < last), listed - first, zero_at)

    return entry


def lhs_of(views):
    return jnp.concatenate(
        [views[dx : dx + EDGE].reshape(EDGE * PLANE, 384) for dx in range(3)], axis=1
    )


def shift_rows(wide, step):
    row = lax.broadcasted_iota(jnp.int32, wide.shape, 1)
    moved = pltpu.roll(wide, (-step) % EDGE, 1)
    return jnp.where(row == (EDGE - 1 if step > 0 else 0), 0.0, moved)


def join_taps(parts):
    shape = (parts.shape[0] // EDGE, EDGE, 128)
    blocks = [parts[:, 128 * dz : 128 * dz + 128].reshape(shape) for dz in range(3)]
    return blocks[1] + shift_rows(blocks[0], -1) + shift_rows(blocks[2], 1)


def tiles_here(counts):
    out = []
    for name, size in zip(("gx", "gy"), counts):
        at = lax.axis_index(name)
        steps = [step_of(at, phase) for phase in swap_phases(size)]
        out.append([(step, inside(at, size, step)) for step in steps])
    return out


def pack_all(bricks, lists, x_boxes, y_boxes, counts, send):
    tiles_x, tiles_y = tiles_here(counts)
    for (step_y, _), box in zip(tiles_y, y_boxes):
        pack_along_y(bricks, lists, box, step_y, send)
    for (step_x, _), box in zip(tiles_x, x_boxes):
        pack_along_x(bricks, lists, box, step_x, send)


def start_kernel(counts, send, lists_hbm, bricks_hbm, bricks, *rest):
    boxes, (lists, sems) = rest[:-2], rest[-2:]
    copies = [
        pltpu.make_async_copy(bricks_hbm, bricks, sems.at[0]),
        pltpu.make_async_copy(lists_hbm, lists, sems.at[1]),
    ]
    for copy in copies:
        copy.start()
    for copy in copies:
        copy.wait()
    number_x = len(swap_phases(counts[0]))
    pack_all(bricks, lists, boxes[:number_x], boxes[number_x:], counts, send)


def join_kernel(counts, send, *rest):
    tiles_x, tiles_y = tiles_here(counts)
    number_x, number_y = len(tiles_x), len(tiles_y)
    faces, y_boxes, x_boxes = rest[:number_x], rest[number_x : number_x + number_y], rest[number_x + number_y :]
    for (step_x, _), face, box in zip(tiles_x, faces, x_boxes):
        join_along_x(face, box, y_boxes, step_x, send)


def layout_kernel(table, bricks, weight, forward, views, preact, store):
    slots = bricks.shape[0]
    for tap in range(27):
        far, near = tap // 3 * 128, tap % 3 * 128
        forward[far : far + 128, near : near + 128] = weight[tap]
    store[0:slots] = bricks[...]
    store[slots] = jnp.zeros(store.shape[1:], BF16)
    for slot in range(slots):
        fill_views(views.at[slot], store, lookup(table, slot, 0, slots, slots))
    own_products(views, forward, preact, range(slots // 2))


def own_products(views, taps, preact, which):
    for slot in which:
        parts = jnp.dot(lhs_of(views.at[slot]), taps[...], preferred_element_type=F32)
        preact[slot] = join_taps(parts).reshape(EDGE, EDGE, EDGE, 128)


def own_kernel(views, taps, begun, preact):
    own_products(views, taps, preact, range(views.shape[0] // 2, views.shape[0]))


def add_remote(views, store, table, send, sides=None):
    slots = views.shape[0]
    nothing = jnp.zeros((EDGE, EDGE, 128), F32)
    for slot in range(slots):
        rows = slice(slot * PLANE, (slot + 1) * PLANE)
        entry = lookup(table, slot, slots, slots + 8 * send, store.shape[0] - 1)
        for side, off_x, source, target in ((0, -1, EDGE - 1, 0), (1, 1, 0, EDGE + 1)):
            plane = view_of(store, entry, off_x, source)
            if sides is not None:
                sides[side, rows] = plane
            views[slot, target] = views[slot, target] + plane
        for side, off_y, base, lanes in ((2, -1, 0, 0), (3, 1, PLANE - 16, 256)):
            group = slice(PLANE - 16, PLANE) if off_y < 0 else slice(0, 16)
            edge = low_or_high(store[entry(0, off_y), :, group, :], off_y < 0)
            padded = jnp.concatenate([nothing[:1], edge, nothing[:1]], axis=0)
            for dx in range(3 if sides is not None else 0):
                sides[side, rows, 128 * dx : 128 * dx + 128] = (
                    padded[dx : dx + EDGE].reshape(PLANE, 128).astype(BF16)
                )
            both = [edge, nothing] if off_y < 0 else [nothing, edge]
            wide = jnp.concatenate(both, axis=1).astype(BF16)
            at = (slot, slice(1, EDGE + 1), slice(base, base + 16), slice(lanes, lanes + 128))
            views[at] = views[at] + wide


def forward_kernel(counts, send, factor, table, lists, own_views, own_preact, cotangent, taps, *rest):
    tiles_x, tiles_y = tiles_here(counts)
    number_x, number_y = len(tiles_x), len(tiles_y)
    x_boxes, y_boxes, rest = rest[:number_x], rest[number_x : number_x + number_y], rest[number_x + number_y :]
    views, preacts, activated, grads, kept_term, sent_term = rest[:6]
    faces_out, boxes_out = rest[6 : 6 + number_x], rest[6 + number_x : 6 + number_x + number_y]
    store, sides = rest[6 + number_x + number_y :]
    core = lax.axis_index("dp") % CORES
    slots = cotangent.shape[0]
    fill_remote(store, 0, x_boxes, y_boxes, tiles_x, tiles_y, send)
    add_remote(views, store, table, send, sides)
    added = []
    for side in range(4):
        if side < 2:
            part = taps[768 * side : 768 * side + 384]
        else:
            dy = 0 if side == 2 else 2
            part = jnp.concatenate(
                [taps[(3 * dx + dy) * 128 : (3 * dx + dy) * 128 + 128] for dx in range(3)], axis=0
            )
        product = join_taps(jnp.dot(sides[side], part, preferred_element_type=F32))
        added.append(product.reshape(slots, EDGE, EDGE, 128))
    for slot in range(slots):
        preacts[slot, 0] = preacts[slot, 0] + added[0][slot]
        preacts[slot, EDGE - 1] = preacts[slot, EDGE - 1] + added[1][slot]
        preacts[slot, :, 0] = preacts[slot, :, 0] + added[2][slot]
        preacts[slot, :, EDGE - 1] = preacts[slot, :, EDGE - 1] + added[3][slot]
        preact = preacts[slot].reshape(PLANE, EDGE, 128)
        sigmoid = jax.nn.sigmoid(preact)
        activated[slot] = (preact * sigmoid).reshape(EDGE, PLANE, 128).astype(BF16)
        slope = sigmoid * (1.0 + preact * (1.0 - sigmoid))
        wide = cotangent[slot].astype(F32).reshape(PLANE, EDGE, 128) * slope
        wide = jnp.where(table[slot, 13] >= 0, wide, 0.0)
        grads[slot] = wide.reshape(EDGE, PLANE, 128).astype(BF16)
    pack_all(grads, lists, faces_out, boxes_out, counts, send)
    total = None
    for slot in range(slots):
        grad = grads[slot].astype(F32).reshape(PLANE, EDGE, 128)
        shifted = [shift_rows(grad, 1), grad, shift_rows(grad, -1)]
        rhs = jnp.concatenate([s.reshape(EDGE * PLANE, 128) for s in shifted], axis=1).astype(BF16)
        term = lax.dot_general(
            lhs_of(views.at[slot]), rhs, (((0,), (0,)), ((), ())), preferred_element_type=F32
        )
        total = term if total is None else total + term
    half = 128 // CORES

    def piece(at):
        far, near, low = at // CORES // 3 * 128, at // CORES % 3 * 128, at % CORES * half
        return total[far + low : far + low + half, near : near + 128] * factor

    for at in range(27):
        first, second = piece(at), piece(27 + at)
        rows = slice(at * half, (at + 1) * half)
        kept_term[rows] = jnp.where(core == 0, first, second)
        sent_term[rows] = jnp.where(core == 0, second, first).astype(BF16)
    for term in (kept_term, sent_term):
        if term.shape[0] > 27 * half:
            term[27 * half :] = jnp.zeros((term.shape[0] - 27 * half, 128), term.dtype)


def back_layout_kernel(table, bricks, weight, joined, backward, views, store):
    slots = bricks.shape[0]
    for tap in range(27):
        far, near = tap // 3 * 128, tap % 3 * 128
        backward[far : far + 128, near : near + 128] = weight[26 - tap].T
    store[0:slots] = bricks[...]
    store[slots] = jnp.zeros(store.shape[1:], BF16)
    for slot in range(slots):
        fill_views(views.at[slot], store, lookup(table, slot, 0, slots, slots))


def backward_kernel(counts, send, table, own_views, taps, *rest):
    tiles_x, tiles_y = tiles_here(counts)
    x_boxes, y_boxes = rest[: len(tiles_x)], rest[len(tiles_x) : len(tiles_x) + len(tiles_y)]
    views, result, ready, store = rest[-4:]
    fill_remote(store, 0, x_boxes, y_boxes, tiles_x, tiles_y, send)
    add_remote(views, store, table, send)
    for slot in range(views.shape[0]):
        parts = jnp.dot(lhs_of(views.at[slot]), taps[...], preferred_element_type=F32)
        result[slot] = join_taps(parts).reshape(EDGE, PLANE, 128).astype(BF16)
    ready[...] = jnp.zeros(ready.shape, F32)


VMEM = pl.BlockSpec(memory_space=pltpu.VMEM)
SMEM = pl.BlockSpec(memory_space=pltpu.SMEM)
ANY = pl.BlockSpec(memory_space=pl.ANY)
HBM = pl.BlockSpec(memory_space=pltpu.HBM)
PARAMS = pltpu.CompilerParams(vmem_limit_bytes=VMEM_BYTES)


def run(kernel, out_shape, ins, outs, scratch=(), aliases=None, micros=1.0):
    cost = pl.CostEstimate(flops=int(micros * 1e9), bytes_accessed=2**16, transcendentals=0)
    return pl.pallas_call(
        kernel,
        out_shape=out_shape,
        in_specs=ins,
        out_specs=outs,
        scratch_shapes=list(scratch),
        input_output_aliases=aliases or {},
        compiler_params=PARAMS,
        cost_estimate=cost,
    )


class Groups:
    def __init__(self):
        self.sizes = tuple(lax.axis_size(name) for name in ("dp", "gx", "gy"))
        dp, gx, gy = self.sizes
        self.plane, self.line = dp // CORES * gy, gx
        self.turned = self.plane == self.line
        at = lax.axis_index("dp")
        in_plane = at // CORES * gy + lax.axis_index("gy")
        self.core = at % CORES
        in_line = lax.axis_index("gx") if self.turned else in_plane
        self.mine = jnp.where(self.core == 0, in_plane, in_line).astype(jnp.int32)
        self.others = jnp.where(self.core == 0, in_line, in_plane).astype(jnp.int32)

    def places(self):
        masks = [0] + list(range(self.plane - 1, 0, -1))
        own = [(self.core, self.mine ^ mask) for mask in masks]
        return own + [(1 - self.core, self.others ^ mask) for mask in masks]

    def pairs(self, place):
        dp, gx, gy = self.sizes
        out = []
        for a in range(dp):
            for b in range(gx):
                for c in range(gy):
                    to = place(a, b, c)
                    out.append(((a * gx + b) * gy + c, (to[0] * gx + to[1]) * gy + to[2]))
        return out

    def swap(self, x, stage, mask):
        gy = self.sizes[2]

        def place(a, b, c):
            if self.turned and a % CORES == 1:
                plane = stage == 1
            else:
                plane = stage == 0
            if plane:
                return a ^ (mask // gy * CORES), b, c ^ (mask % gy)
            return a, b ^ mask, c

        return lax.ppermute(x, ("dp", "gx", "gy"), self.pairs(place))

    def swaps(self, boxes, stage):
        return [self.swap(box, stage, len(boxes) - at) for at, box in enumerate(boxes)]

    def swap_cores(self, x):
        return lax.ppermute(x, ("dp", "gx", "gy"), self.pairs(lambda a, b, c: (a ^ 1, b, c)))


def tree_sum(terms):
    while len(terms) > 1:
        terms = [a + b for a, b in zip(terms[::2], terms[1::2])]
    return terms[0]


def share_kernel(mine, kept, arrived, own, *boxes):
    own[...] = kept[mine[0]] + arrived[mine[0]].astype(F32)
    for mask, box in enumerate(reversed(boxes), 1):
        at = mine[0] ^ mask
        box[...] = (kept[at] + arrived[at].astype(F32)).astype(BF16)


def first_sum_kernel(boxes, own, *rest):
    total = own[...]
    for box in rest[:boxes]:
        total = total + box[...].astype(F32)
    rest[-1][...] = total.astype(BF16)


def second_sum_kernel(*rest):
    terms = [box[...].astype(F32) for box in rest[-3::-1]]
    rest[-1][...] = tree_sum(terms).astype(BF16)


def spread_kernel(count, first, *rest):
    out, wide, sems = rest[-3:]
    places = Groups().places()[first : first + count]
    copies = []
    for number, box in enumerate(rest[:count]):
        wide[number] = box[...].astype(F32)
        place = out.at[places[number]]
        copies.append(pltpu.make_async_copy(wide.at[number], place, sems.at[number]))
        copies[-1].start()
    for copy in copies:
        copy.wait()


def summed_everywhere(groups, kept, sent, early, late):
    group, line = groups.plane, groups.line
    rows = kept.shape[0] // group
    shares = (group, rows, 128)
    share_type = jax.ShapeDtypeStruct((rows, 128), BF16)
    mine = groups.mine.reshape(1)
    arrived = groups.swap_cores(sent)
    own, *boxes = run(
        share_kernel,
        [jax.ShapeDtypeStruct((rows, 128), F32)] + [share_type] * (group - 1),
        [SMEM, VMEM, VMEM],
        [VMEM] * group,
    )(mine, kept.reshape(shares), arrived.reshape(shares))
    boxes = groups.swaps(boxes, 0)
    first_sum = functools.partial(first_sum_kernel, group - 1)
    rounded = run(first_sum, share_type, [VMEM] * group + [ANY] * len(early), VMEM)(
        own, *boxes, *early
    )
    boxes = groups.swaps([rounded] * (line - 1), 1) + [rounded]
    rounded = run(second_sum_kernel, share_type, [VMEM] * line + [ANY], VMEM)(*boxes, late)
    boxes = [rounded] + groups.swaps([rounded] * (group - 1), 0)
    passed = [groups.swap_cores(box) for box in boxes]
    out_type = jax.ShapeDtypeStruct((CORES, group, rows, 128), F32)

    def spread(boxes, first, *out):
        count = len(boxes)
        return run(
            functools.partial(spread_kernel, count, first),
            out_type,
            [VMEM] * count + [ANY] * len(out),
            ANY,
            [pltpu.VMEM((count, rows, 128), F32), pltpu.SemaphoreType.DMA((count,))],
            aliases={count: 0} if out else None,
        )(*boxes, *out)

    out = spread(boxes + passed[:-2], 0)
    out = spread(passed[-2:], len(boxes + passed[:-2]), out)
    return out.reshape(CORES, group * rows, 128)[:, : 27 * 128 // CORES]


def body(features, weight, cotangent, neighbours, send_slots):
    slots, _, channels = features.shape[3:]
    send = send_slots.shape[-1]
    counts = (lax.axis_size("gx"), lax.axis_size("gy"))
    devices = lax.axis_size("dp") * counts[0] * counts[1]
    bricks = features.reshape(slots, EDGE, PLANE, channels)
    cot = cotangent.reshape(slots, EDGE, PLANE, channels)
    blocks = weight.reshape(27, channels, channels)
    table = neighbours.reshape(slots, 27)
    lists = send_slots.reshape(8, send).T
    factor = 1.0 / math.sqrt(float(devices * slots * EDGE * PLANE))
    phases_x, phases_y = swap_phases(counts[0]), swap_phases(counts[1])
    number_x, number_y = len(phases_x), len(phases_y)
    y_type = jax.ShapeDtypeStruct((send * (PLANE + 2 * EDGE), 128), BF16)
    x_type = jax.ShapeDtypeStruct((send * (PLANE + number_y * EDGE), 128), BF16)
    bricks_type = jax.ShapeDtypeStruct(bricks.shape, BF16)
    views_type = jax.ShapeDtypeStruct((slots, EDGE + 2, PLANE, 384), BF16)
    taps_type = jax.ShapeDtypeStruct((1152, 384), BF16)
    preact_type = jax.ShapeDtypeStruct((slots, EDGE, EDGE, EDGE, 128), F32)
    groups = Groups()
    block = 16 * groups.plane
    half_shape = (-(-27 * channels // CORES // block) * block, channels)

    def swapped(boxes, axis, phases):
        return [swap(box, axis, phase) for box, phase in zip(boxes, phases)]

    def store_of(entries):
        return pltpu.VMEM((entries, EDGE, PLANE, 128), BF16)

    face_type = jax.ShapeDtypeStruct((send * PLANE, 128), BF16)
    join = run(
        functools.partial(join_kernel, counts, send),
        [x_type] * number_x,
        [VMEM] * (number_x + number_y),
        [VMEM] * number_x,
    )

    bricks, *boxes = run(
        functools.partial(start_kernel, counts, send),
        [bricks_type] + [face_type] * number_x + [y_type] * number_y,
        [HBM, HBM],
        [VMEM] * (1 + number_x + number_y),
        [pltpu.SMEM((send, 8), jnp.int32), pltpu.SemaphoreType.DMA((2,))],
    )(*[pltpu.with_memory_space_constraint(x, pltpu.HBM) for x in (lists, bricks)])
    faces, y_boxes = boxes[:number_x], boxes[number_x:]
    y_boxes = swapped(y_boxes, "gy", phases_y)
    taps, views, preacts = run(
        layout_kernel,
        [
            taps_type,
            views_type,
            preact_type,
        ],
        [SMEM, VMEM, VMEM],
        [VMEM] * 3,
        [store_of(slots + 1)],
        micros=2.0,
    )(table, bricks, blocks)
    x_boxes = swapped(join(*faces, *y_boxes), "gx", phases_x)
    preacts = run(own_kernel, preact_type, [VMEM] * 3, VMEM, aliases={2: 0}, micros=4.0)(
        views, taps, preacts
    )
    _, _, activated, grads, kept, sent, *boxes = run(
        functools.partial(forward_kernel, counts, send, factor),
        [
            views_type,
            preact_type,
            bricks_type,
            bricks_type,
            jax.ShapeDtypeStruct(half_shape, F32),
            jax.ShapeDtypeStruct(half_shape, BF16),
        ]
        + [face_type] * number_x
        + [y_type] * number_y,
        [SMEM, SMEM] + [VMEM] * (4 + number_x + number_y),
        [VMEM] * (6 + number_x + number_y),
        [store_of(8 * send + 1), pltpu.VMEM((4, slots * PLANE, 384), BF16)],
        aliases={2: 0, 3: 1},
        micros=5.0,
    )(table, lists, views, preacts, cot, taps, *x_boxes, *y_boxes)
    faces, y_boxes = boxes[:number_x], swapped(boxes[number_x:], "gy", phases_y)
    packed = join(*faces, *y_boxes)
    x_boxes = swapped(packed, "gx", phases_x)
    back_taps, views = run(
        back_layout_kernel, [taps_type, views_type], [SMEM, VMEM, VMEM, ANY], [VMEM, VMEM], [store_of(slots + 1)]
    )(table, grads, blocks, packed[-1])
    _, input_grad, ready = run(
        functools.partial(backward_kernel, counts, send),
        [views_type, bricks_type, jax.ShapeDtypeStruct((8, 128), F32)],
        [SMEM, VMEM, VMEM] + [VMEM] * (number_x + number_y),
        [VMEM] * 3,
        [store_of(8 * send + 1)],
        aliases={1: 0},
        micros=5.0,
    )(table, views, back_taps, *x_boxes, *y_boxes)
    weight_grad = summed_everywhere(groups, kept, sent, [packed[-1], views], ready)
    return (
        activated.reshape(features.shape),
        input_grad.reshape(features.shape),
        weight_grad.reshape(weight.shape),
    )


def solution(mesh):
    split = P("dp", "gx", "gy", None, None, None)
    table = P("dp", "gx", "gy", None, None)
    return jax.shard_map(
        body,
        mesh=mesh,
        in_specs=(split, P(), split, table, table),
        out_specs=(split, split, P()),
        check_vma=False,
    )
```

```python
import functools
import math

import jax
import jax.numpy as jnp
from jax import lax
from jax.experimental import pallas as pl
from jax.experimental.pallas import tpu as pltpu
from jax.sharding import PartitionSpec as P

EDGE = 8
PLANE = EDGE * EDGE
VMEM_BYTES = 28 * 2**20
CORES = 2

F32 = jnp.float32
BF16 = jnp.bfloat16


def swap_phases(size):
    return ([0] if size > 1 else []) + ([1] if size > 2 else [])


def partner_of(at, size, phase):
    other = at + 1 if at % 2 == phase else at - 1
    return other if 0 <= other < size else at


def swap(x, axis, phase):
    sizes = [lax.axis_size(name) for name in ("dp", axis)]
    pairs = []
    for at in range(sizes[0]):
        for tile in range(sizes[1]):
            other = partner_of(tile, sizes[1], phase)
            to = (at ^ 1 if other == tile else at) * sizes[1] + other
            pairs.append((at * sizes[1] + tile, to))
    return lax.ppermute(x, ("dp", axis), pairs)


def inside(at, size, step):
    return (at + step >= 0) & (at + step < size)


def step_of(at, phase):
    return jnp.where(at % 2 == phase, 1, -1)


def direction(step_x, step_y):
    flat = 3 * (step_x + 1) + step_y + 1
    return flat - jnp.where(flat > 4, 1, 0)


def low_or_high(group, upper):
    wide = group.astype(F32)
    return wide[..., EDGE:, :] if upper else wide[..., :EDGE, :]


def y_edge(bricks, slot, plane, step_y):
    low = low_or_high(bricks[slot, plane, 0:16, :], False)
    high = low_or_high(bricks[slot, plane, PLANE - 16 : PLANE, :], True)
    return jnp.where(step_y > 0, high, low)


def pack_along_y(bricks, lists, box, step_y, send):
    number = direction(0, step_y)
    for entry in range(send):
        listed = lists[entry, number]
        face = y_edge(bricks, jnp.maximum(listed, 0), slice(0, EDGE), step_y)
        face = jnp.where(listed >= 0, face, 0.0).reshape(PLANE, 128)
        box[entry * PLANE : (entry + 1) * PLANE] = face.astype(BF16)
    at = send * PLANE
    for step_x in (-1, 1):
        number = direction(step_x, step_y)
        pieces = []
        for entry in range(send):
            listed = lists[entry, number]
            plane = EDGE - 1 if step_x > 0 else 0
            edge = y_edge(bricks, jnp.maximum(listed, 0), plane, step_y)
            pieces.append(jnp.where(listed >= 0, edge, 0.0))
        box[at : at + send * EDGE] = jnp.concatenate(pieces, axis=0).astype(BF16)
        at += send * EDGE


def pack_along_x(bricks, lists, box, step_x, send):
    number = direction(step_x, 0)
    for entry in range(send):
        listed = lists[entry, number]
        face = bricks[jnp.maximum(listed, 0), jnp.where(step_x > 0, EDGE - 1, 0)]
        box[entry * PLANE : (entry + 1) * PLANE] = jnp.where(listed >= 0, face, jnp.zeros_like(face))


def join_along_x(faces, box, y_boxes, step_x, send):
    at = send * PLANE
    box[:at] = faces[...]
    for y_box in y_boxes:
        first = y_box[send * PLANE : send * PLANE + send * EDGE]
        second = y_box[send * PLANE + send * EDGE : send * PLANE + 2 * send * EDGE]
        box[at : at + send * EDGE] = jnp.where(step_x > 0, second, first)
        at += send * EDGE


def fill_remote(store, base, x_boxes, y_boxes, tiles_x, tiles_y, send):
    store[store.shape[0] - 1] = jnp.zeros(store.shape[1:], BF16)
    for (step_y, in_y), box in zip(tiles_y, y_boxes):
        number = direction(0, step_y)
        for entry in range(send):
            rows = box[entry * PLANE : (entry + 1) * PLANE].astype(F32).reshape(EDGE, EDGE, 128)
            rows = jnp.where(in_y, rows, 0.0)
            twice = jnp.concatenate([rows, rows], axis=1).astype(BF16)
            store[base + number * send + entry, :, 0:16, :] = twice
            store[base + number * send + entry, :, PLANE - 16 : PLANE, :] = twice
    for (step_x, in_x), box in zip(tiles_x, x_boxes):
        number = direction(step_x, 0)
        for entry in range(send):
            face = box[entry * PLANE : (entry + 1) * PLANE]
            face = jnp.where(in_x, face, jnp.zeros_like(face))
            store[base + number * send + entry, 0] = face
            store[base + number * send + entry, EDGE - 1] = face
        at = send * PLANE
        for step_y, in_y in tiles_y:
            number = direction(step_x, step_y)
            edges = jnp.where(in_x & in_y, box[at : at + send * EDGE].astype(F32), 0.0)
            at += send * EDGE
            for entry in range(send):
                rows = edges[entry * EDGE : (entry + 1) * EDGE]
                twice = jnp.concatenate([rows, rows], axis=0).astype(BF16)
                for plane in (0, EDGE - 1):
                    store[base + number * send + entry, plane, 0:16, :] = twice
                    store[base + number * send + entry, plane, PLANE - 16 : PLANE, :] = twice


def view_of(store, entry, off_x, source):
    middle = store[entry(off_x, 0), source]
    before = low_or_high(store[entry(off_x, -1), source, PLANE - 16 : PLANE, :], True)
    after = low_or_high(store[entry(off_x, 1), source, 0:16, :], False)
    wide = middle.astype(F32)
    axis = wide.ndim - 2
    left = jnp.concatenate([before, wide[..., : PLANE - EDGE, :]], axis=axis).astype(BF16)
    right = jnp.concatenate([wide[..., EDGE:, :], after], axis=axis).astype(BF16)
    return jnp.concatenate([left, middle, right], axis=axis + 1)


def fill_views(views, store, entry):
    views[0] = view_of(store, entry, -1, EDGE - 1)
    views[1 : EDGE + 1] = view_of(store, entry, 0, slice(0, EDGE))
    views[EDGE + 1] = view_of(store, entry, 1, 0)


def lookup(table, slot, first, last, zero_at):
    def entry(off_x, off_y):
        listed = table[slot, 9 * (off_x + 1) + 3 * (off_y + 1) + 1]
        return jnp.where((listed >= first) & (listed < last), listed - first, zero_at)

    return entry


def lhs_of(views):
    return jnp.concatenate(
        [views[dx : dx + EDGE].reshape(EDGE * PLANE, 384) for dx in range(3)], axis=1
    )


def shift_rows(wide, step):
    row = lax.broadcasted_iota(jnp.int32, wide.shape, 1)
    moved = pltpu.roll(wide, (-step) % EDGE, 1)
    return jnp.where(row == (EDGE - 1 if step > 0 else 0), 0.0, moved)


def join_taps(parts):
    shape = (parts.shape[0] // EDGE, EDGE, 128)
    blocks = [parts[:, 128 * dz : 128 * dz + 128].reshape(shape) for dz in range(3)]
    return blocks[1] + shift_rows(blocks[0], -1) + shift_rows(blocks[2], 1)


def tiles_here(counts):
    out = []
    for name, size in zip(("gx", "gy"), counts):
        at = lax.axis_index(name)
        steps = [step_of(at, phase) for phase in swap_phases(size)]
        out.append([(step, inside(at, size, step)) for step in steps])
    return out


def pack_all(bricks, lists, x_boxes, y_boxes, counts, send):
    tiles_x, tiles_y = tiles_here(counts)
    for (step_y, _), box in zip(tiles_y, y_boxes):
        pack_along_y(bricks, lists, box, step_y, send)
    for (step_x, _), box in zip(tiles_x, x_boxes):
        pack_along_x(bricks, lists, box, step_x, send)


def start_kernel(counts, send, lists_hbm, bricks_hbm, bricks, *rest):
    boxes, (lists, sems) = rest[:-2], rest[-2:]
    copies = [
        pltpu.make_async_copy(bricks_hbm, bricks, sems.at[0]),
        pltpu.make_async_copy(lists_hbm, lists, sems.at[1]),
    ]
    for copy in copies:
        copy.start()
    for copy in copies:
        copy.wait()
    number_x = len(swap_phases(counts[0]))
    pack_all(bricks, lists, boxes[:number_x], boxes[number_x:], counts, send)


def join_kernel(counts, send, *rest):
    tiles_x, tiles_y = tiles_here(counts)
    number_x, number_y = len(tiles_x), len(tiles_y)
    faces, y_boxes, x_boxes = rest[:number_x], rest[number_x : number_x + number_y], rest[number_x + number_y :]
    for (step_x, _), face, box in zip(tiles_x, faces, x_boxes):
        join_along_x(face, box, y_boxes, step_x, send)


def layout_kernel(table, bricks, weight, forward, views, preact, store):
    slots = bricks.shape[0]
    for tap in range(27):
        far, near = tap // 3 * 128, tap % 3 * 128
        forward[far : far + 128, near : near + 128] = weight[tap]
    store[0:slots] = bricks[...]
    store[slots] = jnp.zeros(store.shape[1:], BF16)
    for slot in range(slots):
        fill_views(views.at[slot], store, lookup(table, slot, 0, slots, slots))
    own_products(views, forward, preact, range(slots // 2))


def own_products(views, taps, preact, which):
    for slot in which:
        parts = jnp.dot(lhs_of(views.at[slot]), taps[...], preferred_element_type=F32)
        preact[slot] = join_taps(parts).reshape(EDGE, EDGE, EDGE, 128)


def own_kernel(counts, send, table, own_views, taps, begun, *rest):
    tiles_y = tiles_here(counts)[1]
    y_boxes, (views, preacts, store, sides) = rest[: len(tiles_y)], rest[len(tiles_y) :]
    slots = views.shape[0]
    own_products(views, taps, preacts, range(slots // 2, slots))
    fill_remote(store, 0, [], y_boxes, [], tiles_y, send)
    add_remote(views, store, table, send, sides, "y")
    for side, at in ((0, 0), (1, EDGE - 1)):
        part = jnp.concatenate(
            [taps[(3 * dx + 2 * side) * 128 : (3 * dx + 2 * side) * 128 + 128] for dx in range(3)], axis=0
        )
        product = join_taps(jnp.dot(sides[side], part, preferred_element_type=F32))
        product = product.reshape(slots, EDGE, EDGE, 128)
        for slot in range(slots):
            preacts[slot, :, at] = preacts[slot, :, at] + product[slot]


PLANES = ((0, -1, EDGE - 1, 0), (1, 1, 0, EDGE + 1))
ROWS = ((0, -1, 0, 0), (1, 1, PLANE - 16, 256))


def add_remote(views, store, table, send, sides=None, along="xy"):
    slots = views.shape[0]
    nothing = jnp.zeros((EDGE, EDGE, 128), F32)
    for slot in range(slots):
        rows = slice(slot * PLANE, (slot + 1) * PLANE)
        entry = lookup(table, slot, slots, slots + 8 * send, store.shape[0] - 1)
        for side, off_x, source, target in PLANES if "x" in along else ():
            plane = view_of(store, entry, off_x, source)
            if sides is not None:
                sides[side, rows] = plane
            views[slot, target] = views[slot, target] + plane
        for side, off_y, base, lanes in ROWS if "y" in along else ():
            group = slice(PLANE - 16, PLANE) if off_y < 0 else slice(0, 16)
            edge = low_or_high(store[entry(0, off_y), :, group, :], off_y < 0)
            padded = jnp.concatenate([nothing[:1], edge, nothing[:1]], axis=0)
            for dx in range(3 if sides is not None else 0):
                sides[side, rows, 128 * dx : 128 * dx + 128] = (
                    padded[dx : dx + EDGE].reshape(PLANE, 128).astype(BF16)
                )
            both = [edge, nothing] if off_y < 0 else [nothing, edge]
            wide = jnp.concatenate(both, axis=1).astype(BF16)
            at = (slot, slice(1, EDGE + 1), slice(base, base + 16), slice(lanes, lanes + 128))
            views[at] = views[at] + wide


def forward_kernel(counts, send, factor, table, lists, own_views, own_preact, cotangent, taps, *rest):
    tiles_x, tiles_y = tiles_here(counts)
    number_x, number_y = len(tiles_x), len(tiles_y)
    x_boxes, y_boxes, rest = rest[:number_x], rest[number_x : number_x + number_y], rest[number_x + number_y :]
    views, preacts, activated, grads, kept_term, sent_term = rest[:6]
    faces_out, boxes_out = rest[6 : 6 + number_x], rest[6 + number_x : 6 + number_x + number_y]
    store, sides = rest[6 + number_x + number_y :]
    core = lax.axis_index("dp") % CORES
    slots = cotangent.shape[0]
    fill_remote(store, 0, x_boxes, y_boxes, tiles_x, tiles_y, send)
    add_remote(views, store, table, send, sides, "x")
    added = []
    for side in range(2):
        part = taps[768 * side : 768 * side + 384]
        product = join_taps(jnp.dot(sides[side], part, preferred_element_type=F32))
        added.append(product.reshape(slots, EDGE, EDGE, 128))
    for slot in range(slots):
        preacts[slot, 0] = preacts[slot, 0] + added[0][slot]
        preacts[slot, EDGE - 1] = preacts[slot, EDGE - 1] + added[1][slot]
        preact = preacts[slot].reshape(PLANE, EDGE, 128)
        sigmoid = jax.nn.sigmoid(preact)
        activated[slot] = (preact * sigmoid).reshape(EDGE, PLANE, 128).astype(BF16)
        slope = sigmoid * (1.0 + preact * (1.0 - sigmoid))
        wide = cotangent[slot].astype(F32).reshape(PLANE, EDGE, 128) * slope
        wide = jnp.where(table[slot, 13] >= 0, wide, 0.0)
        grads[slot] = wide.reshape(EDGE, PLANE, 128).astype(BF16)
    pack_all(grads, lists, faces_out, boxes_out, counts, send)
    total = None
    for slot in range(slots):
        grad = grads[slot].astype(F32).reshape(PLANE, EDGE, 128)
        shifted = [shift_rows(grad, 1), grad, shift_rows(grad, -1)]
        rhs = jnp.concatenate([s.reshape(EDGE * PLANE, 128) for s in shifted], axis=1).astype(BF16)
        term = lax.dot_general(
            lhs_of(views.at[slot]), rhs, (((0,), (0,)), ((), ())), preferred_element_type=F32
        )
        total = term if total is None else total + term
    half = 128 // CORES

    def piece(at):
        far, near, low = at // CORES // 3 * 128, at // CORES % 3 * 128, at % CORES * half
        return total[far + low : far + low + half, near : near + 128] * factor

    for at in range(27):
        first, second = piece(at), piece(27 + at)
        rows = slice(at * half, (at + 1) * half)
        kept_term[rows] = jnp.where(core == 0, first, second)
        sent_term[rows] = jnp.where(core == 0, second, first).astype(BF16)
    for term in (kept_term, sent_term):
        if term.shape[0] > 27 * half:
            term[27 * half :] = jnp.zeros((term.shape[0] - 27 * half, 128), term.dtype)


def back_layout_kernel(table, bricks, weight, joined, backward, views, store):
    slots = bricks.shape[0]
    for tap in range(27):
        far, near = tap // 3 * 128, tap % 3 * 128
        backward[far : far + 128, near : near + 128] = weight[26 - tap].T
    store[0:slots] = bricks[...]
    store[slots] = jnp.zeros(store.shape[1:], BF16)
    for slot in range(slots):
        fill_views(views.at[slot], store, lookup(table, slot, 0, slots, slots))


def backward_kernel(counts, send, table, own_views, taps, *rest):
    tiles_x, tiles_y = tiles_here(counts)
    x_boxes, y_boxes = rest[: len(tiles_x)], rest[len(tiles_x) : len(tiles_x) + len(tiles_y)]
    views, result, ready, store = rest[-4:]
    fill_remote(store, 0, x_boxes, y_boxes, tiles_x, tiles_y, send)
    add_remote(views, store, table, send)
    for slot in range(views.shape[0]):
        parts = jnp.dot(lhs_of(views.at[slot]), taps[...], preferred_element_type=F32)
        result[slot] = join_taps(parts).reshape(EDGE, PLANE, 128).astype(BF16)
    ready[...] = jnp.zeros(ready.shape, F32)


VMEM = pl.BlockSpec(memory_space=pltpu.VMEM)
SMEM = pl.BlockSpec(memory_space=pltpu.SMEM)
ANY = pl.BlockSpec(memory_space=pl.ANY)
HBM = pl.BlockSpec(memory_space=pltpu.HBM)
PARAMS = pltpu.CompilerParams(vmem_limit_bytes=VMEM_BYTES)


def run(kernel, out_shape, ins, outs, scratch=(), aliases=None, micros=1.0):
    cost = pl.CostEstimate(flops=int(micros * 1e9), bytes_accessed=2**16, transcendentals=0)
    return pl.pallas_call(
        kernel,
        out_shape=out_shape,
        in_specs=ins,
        out_specs=outs,
        scratch_shapes=list(scratch),
        input_output_aliases=aliases or {},
        compiler_params=PARAMS,
        cost_estimate=cost,
    )


class Groups:
    def __init__(self):
        self.sizes = tuple(lax.axis_size(name) for name in ("dp", "gx", "gy"))
        dp, gx, gy = self.sizes
        self.plane, self.line = dp // CORES * gy, gx
        self.turned = self.plane == self.line
        at = lax.axis_index("dp")
        in_plane = at // CORES * gy + lax.axis_index("gy")
        self.core = at % CORES
        in_line = lax.axis_index("gx") if self.turned else in_plane
        self.mine = jnp.where(self.core == 0, in_plane, in_line).astype(jnp.int32)
        self.others = jnp.where(self.core == 0, in_line, in_plane).astype(jnp.int32)

    def places(self):
        masks = [0] + list(range(self.plane - 1, 0, -1))
        own = [(self.core, self.mine ^ mask) for mask in masks]
        return own + [(1 - self.core, self.others ^ mask) for mask in masks]

    def pairs(self, place):
        dp, gx, gy = self.sizes
        out = []
        for a in range(dp):
            for b in range(gx):
                for c in range(gy):
                    to = place(a, b, c)
                    out.append(((a * gx + b) * gy + c, (to[0] * gx + to[1]) * gy + to[2]))
        return out

    def swap(self, x, stage, mask):
        gy = self.sizes[2]

        def place(a, b, c):
            if self.turned and a % CORES == 1:
                plane = stage == 1
            else:
                plane = stage == 0
            if plane:
                return a ^ (mask // gy * CORES), b, c ^ (mask % gy)
            return a, b ^ mask, c

        return lax.ppermute(x, ("dp", "gx", "gy"), self.pairs(place))

    def swaps(self, boxes, stage):
        return [self.swap(box, stage, len(boxes) - at) for at, box in enumerate(boxes)]

    def swap_cores(self, x):
        return lax.ppermute(x, ("dp", "gx", "gy"), self.pairs(lambda a, b, c: (a ^ 1, b, c)))


def tree_sum(terms):
    while len(terms) > 1:
        terms = [a + b for a, b in zip(terms[::2], terms[1::2])]
    return terms[0]


def share_kernel(mine, kept, arrived, own, *boxes):
    own[...] = kept[mine[0]] + arrived[mine[0]].astype(F32)
    for mask, box in enumerate(reversed(boxes), 1):
        at = mine[0] ^ mask
        box[...] = (kept[at] + arrived[at].astype(F32)).astype(BF16)


def first_sum_kernel(boxes, own, *rest):
    total = own[...]
    for box in rest[:boxes]:
        total = total + box[...].astype(F32)
    rest[-1][...] = total.astype(BF16)


def second_sum_kernel(*rest):
    terms = [box[...].astype(F32) for box in rest[-3::-1]]
    rest[-1][...] = tree_sum(terms).astype(BF16)


def spread_kernel(count, first, *rest):
    out, wide, sems = rest[-3:]
    places = Groups().places()[first : first + count]
    copies = []
    for number, box in enumerate(rest[:count]):
        wide[number] = box[...].astype(F32)
        place = out.at[places[number]]
        copies.append(pltpu.make_async_copy(wide.at[number], place, sems.at[number]))
        copies[-1].start()
    for copy in copies:
        copy.wait()


def summed_everywhere(groups, kept, sent, early, late):
    group, line = groups.plane, groups.line
    rows = kept.shape[0] // group
    shares = (group, rows, 128)
    share_type = jax.ShapeDtypeStruct((rows, 128), BF16)
    mine = groups.mine.reshape(1)
    arrived = groups.swap_cores(sent)
    own, *boxes = run(
        share_kernel,
        [jax.ShapeDtypeStruct((rows, 128), F32)] + [share_type] * (group - 1),
        [SMEM, VMEM, VMEM],
        [VMEM] * group,
    )(mine, kept.reshape(shares), arrived.reshape(shares))
    boxes = groups.swaps(boxes, 0)
    first_sum = functools.partial(first_sum_kernel, group - 1)
    rounded = run(first_sum, share_type, [VMEM] * group + [ANY] * len(early), VMEM)(
        own, *boxes, *early
    )
    boxes = groups.swaps([rounded] * (line - 1), 1) + [rounded]
    rounded = run(second_sum_kernel, share_type, [VMEM] * line + [ANY], VMEM)(*boxes, late)
    boxes = [rounded] + groups.swaps([rounded] * (group - 1), 0)
    passed = [groups.swap_cores(box) for box in boxes]
    out_type = jax.ShapeDtypeStruct((CORES, group, rows, 128), F32)

    def spread(boxes, first, *out):
        count = len(boxes)
        return run(
            functools.partial(spread_kernel, count, first),
            out_type,
            [VMEM] * count + [ANY] * len(out),
            ANY,
            [pltpu.VMEM((count, rows, 128), F32), pltpu.SemaphoreType.DMA((count,))],
            aliases={count: 0} if out else None,
        )(*boxes, *out)

    out = spread(boxes + passed[:-2], 0)
    out = spread(passed[-2:], len(boxes + passed[:-2]), out)
    return out.reshape(CORES, group * rows, 128)[:, : 27 * 128 // CORES]


def body(features, weight, cotangent, neighbours, send_slots):
    slots, _, channels = features.shape[3:]
    send = send_slots.shape[-1]
    counts = (lax.axis_size("gx"), lax.axis_size("gy"))
    devices = lax.axis_size("dp") * counts[0] * counts[1]
    bricks = features.reshape(slots, EDGE, PLANE, channels)
    cot = cotangent.reshape(slots, EDGE, PLANE, channels)
    blocks = weight.reshape(27, channels, channels)
    table = neighbours.reshape(slots, 27)
    lists = send_slots.reshape(8, send).T
    factor = 1.0 / math.sqrt(float(devices * slots * EDGE * PLANE))
    phases_x, phases_y = swap_phases(counts[0]), swap_phases(counts[1])
    number_x, number_y = len(phases_x), len(phases_y)
    y_type = jax.ShapeDtypeStruct((send * (PLANE + 2 * EDGE), 128), BF16)
    x_type = jax.ShapeDtypeStruct((send * (PLANE + number_y * EDGE), 128), BF16)
    bricks_type = jax.ShapeDtypeStruct(bricks.shape, BF16)
    views_type = jax.ShapeDtypeStruct((slots, EDGE + 2, PLANE, 384), BF16)
    taps_type = jax.ShapeDtypeStruct((1152, 384), BF16)
    preact_type = jax.ShapeDtypeStruct((slots, EDGE, EDGE, EDGE, 128), F32)
    groups = Groups()
    block = 16 * groups.plane
    half_shape = (-(-27 * channels // CORES // block) * block, channels)

    def swapped(boxes, axis, phases):
        return [swap(box, axis, phase) for box, phase in zip(boxes, phases)]

    sides_of = pltpu.VMEM((2, slots * PLANE, 384), BF16)

    def store_of(entries):
        return pltpu.VMEM((entries, EDGE, PLANE, 128), BF16)

    face_type = jax.ShapeDtypeStruct((send * PLANE, 128), BF16)
    join = run(
        functools.partial(join_kernel, counts, send),
        [x_type] * number_x,
        [VMEM] * (number_x + number_y),
        [VMEM] * number_x,
    )

    bricks, *boxes = run(
        functools.partial(start_kernel, counts, send),
        [bricks_type] + [face_type] * number_x + [y_type] * number_y,
        [HBM, HBM],
        [VMEM] * (1 + number_x + number_y),
        [pltpu.SMEM((send, 8), jnp.int32), pltpu.SemaphoreType.DMA((2,))],
    )(*[pltpu.with_memory_space_constraint(x, pltpu.HBM) for x in (lists, bricks)])
    faces, y_boxes = boxes[:number_x], boxes[number_x:]
    y_boxes = swapped(y_boxes, "gy", phases_y)
    taps, views, preacts = run(
        layout_kernel,
        [
            taps_type,
            views_type,
            preact_type,
        ],
        [SMEM, VMEM, VMEM],
        [VMEM] * 3,
        [store_of(slots + 1)],
        micros=2.0,
    )(table, bricks, blocks)
    x_boxes = swapped(join(*faces, *y_boxes), "gx", phases_x)
    views, preacts = run(
        functools.partial(own_kernel, counts, send),
        [views_type, preact_type],
        [SMEM] + [VMEM] * (3 + number_y),
        [VMEM, VMEM],
        [store_of(8 * send + 1), sides_of],
        aliases={1: 0, 3: 1},
        micros=4.0,
    )(table, views, taps, preacts, *y_boxes)
    _, _, activated, grads, kept, sent, *boxes = run(
        functools.partial(forward_kernel, counts, send, factor),
        [
            views_type,
            preact_type,
            bricks_type,
            bricks_type,
            jax.ShapeDtypeStruct(half_shape, F32),
            jax.ShapeDtypeStruct(half_shape, BF16),
        ]
        + [face_type] * number_x
        + [y_type] * number_y,
        [SMEM, SMEM] + [VMEM] * (4 + number_x + number_y),
        [VMEM] * (6 + number_x + number_y),
        [store_of(8 * send + 1), sides_of],
        aliases={2: 0, 3: 1},
        micros=5.0,
    )(table, lists, views, preacts, cot, taps, *x_boxes, *y_boxes)
    faces, y_boxes = boxes[:number_x], swapped(boxes[number_x:], "gy", phases_y)
    packed = join(*faces, *y_boxes)
    x_boxes = swapped(packed, "gx", phases_x)
    back_taps, views = run(
        back_layout_kernel, [taps_type, views_type], [SMEM, VMEM, VMEM, ANY], [VMEM, VMEM], [store_of(slots + 1)]
    )(table, grads, blocks, packed[-1])
    _, input_grad, ready = run(
        functools.partial(backward_kernel, counts, send),
        [views_type, bricks_type, jax.ShapeDtypeStruct((8, 128), F32)],
        [SMEM, VMEM, VMEM] + [VMEM] * (number_x + number_y),
        [VMEM] * 3,
        [store_of(8 * send + 1)],
        aliases={1: 0},
        micros=5.0,
    )(table, views, back_taps, *x_boxes, *y_boxes)
    weight_grad = summed_everywhere(groups, kept, sent, [packed[-1], views], ready)
    return (
        activated.reshape(features.shape),
        input_grad.reshape(features.shape),
        weight_grad.reshape(weight.shape),
    )


def solution(mesh):
    split = P("dp", "gx", "gy", None, None, None)
    table = P("dp", "gx", "gy", None, None)
    return jax.shard_map(
        body,
        mesh=mesh,
        in_specs=(split, P(), split, table, table),
        out_specs=(split, split, P()),
        check_vma=False,
    )
```
